32 devices in a mesh: dp: 8 (over z, x), tensor: 4 (over y, core).
Axes of the slice: x: 2, y: 2, z: 4, core: 2. Of those that a mesh axis runs over, the one named last changes fastest.
Arguments:
- inputs: bfloat16 [64, 512, 768], P('dp', 'tensor'), may hold values from -6 to 6
- lengths: int32 [64], P('dp'), may hold values from 51 to 512, as said below
- cotangent: bfloat16 [64, 512, 768], P('dp', 'tensor'), may hold values from -8 to 8
- ln1_gain: float32 [768], replicated, may hold values from 0.5 to 1.5
- ln1_bias: float32 [768], replicated, may hold values from -1.75 to 1.75
- w_qkv: bfloat16 [3, 768, 768], P(None, None, 'tensor'), may hold values from -0.21875 to 0.21875
- b_qv: float32 [2, 768], P(None, 'tensor'), may hold values from -3 to 3
- w_out: bfloat16 [768, 768], P('tensor'), may hold values from -0.875 to 0.875
- b_out: float32 [768], replicated, may hold values from -1.75 to 1.75
- ln2_gain: float32 [768], replicated, may hold values from 0.5 to 1.5
- ln2_bias: float32 [768], replicated, may hold values from -1.75 to 1.75
- w_up: bfloat16 [768, 3072], P(None, 'tensor'), may hold values from -0.21875 to 0.21875
- b_up: float32 [3072], P('tensor'), may hold values from -3 to 3
- w_down: bfloat16 [3072, 768], P('tensor'), may hold values from -0.109375 to 0.109375
- b_down: float32 [768], replicated, may hold values from -1.75 to 1.75
Outputs:
- layer_out: bfloat16 [64, 512, 768], P('dp', 'tensor')
- grad_input: bfloat16 [64, 512, 768], P('dp', 'tensor')
- grad_ln1_gain: float32 [768], replicated
- grad_ln1_bias: float32 [768], replicated
- grad_qkv: float32 [3, 768, 768], P(None, 'dp', 'tensor')
- grad_qv_bias: float32 [2, 768], P(None, 'tensor')
- grad_out_weight: float32 [768, 768], P('tensor', 'dp')
- grad_out_bias: float32 [768], replicated
- grad_ln2_gain: float32 [768], replicated
- grad_ln2_bias: float32 [768], replicated
- grad_up_weight: float32 [768, 3072], P('dp', 'tensor')
- grad_up_bias: float32 [3072], P('tensor')
- grad_down_weight: float32 [3072, 768], P('tensor', 'dp')
- grad_down_bias: float32 [768], replicated
The draws below stay inside these ranges and needn't reach their ends.
Inputs may be any that keep to these rules, and one draw needn't show every extreme that they name: `lengths`: in each aligned block of 8 texts one text, drawn from the seed, has all 512 molecules.
All inputs are finite; a program needn't handle non-finite values.
Results may differ from the reference program's by a relative error of at most 0.018.
Values may be sent and summed in bfloat16 or wider, within the bound.
No kernel may reach another device: no remote copies, remote signals or barrier semaphores. Data moves between devices by JAX's collectives and lax.ppermute only.
A program may use at most 192 MiB of HBM per device.

```python
import jax
import jax.numpy as jnp
from jax import lax

D = 768
HEADS = 12
HD = 64
FF = 3072
MOL = 512
TEXT_MB = 2
TEXT_DEV = 8
TEXTS = 64
MIN_MOL = 51


def draw_lengths(key, part):
    key = jax.random.fold_in(key, 7)
    key_len, key_pick, key_short = jax.random.split(key, 3)
    drawn = jax.random.randint(key_len, (TEXTS,), MIN_MOL, MOL + 1)
    picks = jax.random.randint(key_pick, (TEXTS // TEXT_DEV,), 0, TEXT_DEV)
    offset = jax.random.randint(key_short, (), 1, TEXT_DEV)
    index = jnp.arange(TEXTS)
    block_of = index // TEXT_DEV
    slot_of = index % TEXT_DEV
    longest = slot_of == picks[block_of]
    shortest = (block_of == 0) & (slot_of == (picks[0] + offset) % TEXT_DEV)
    result = jnp.where(longest, MOL, jnp.where(shortest, MIN_MOL, drawn))
    return result.astype(jnp.int32)


def with_spikes(values, key, source, target, shards_of, factor):
    owner, partner = [(jnp.arange(values.shape[axis_at]) // (values.shape[axis_at] // shards_of)).reshape([-1 if axis == axis_at else 1 for axis in range(values.ndim)]) for axis_at in (source, target)]
    chosen = jax.random.permutation(key, shards_of)[partner]
    strong = (owner == chosen) | (owner == (partner + shards_of // 2) % shards_of)
    return jnp.where(strong, factor * values, values)


def steps_of(rng, shape, cuts, low, top_value):
    level, own = 1.0, jax.random.fold_in(rng, 6)
    for axis_at, blocks in cuts:
        steps = jnp.exp(jax.random.uniform(jax.random.fold_in(own, axis_at), (blocks,), jnp.float32, low / len(cuts), top_value / len(cuts)))
        level = level * jnp.repeat(steps, shape[axis_at] // blocks).reshape([-1 if axis == axis_at else 1 for axis in range(len(shape))])
    return level


def bell_draw(own_key, dims, scale, limit, cuts=(), kind=jnp.bfloat16):
    entries = scale * jax.random.normal(own_key, dims, jnp.float32)
    if cuts:
        entries = entries * steps_of(own_key, dims, cuts, -0.22, 0.18)
    return jnp.clip(entries, -limit, limit).astype(kind)


def bell_draw_with(stream_key, dims, deviation, reach, pieces, heavy, held_as=jnp.bfloat16):
    values = deviation * jax.random.normal(stream_key, dims, jnp.float32)
    if pieces:
        values = values * steps_of(stream_key, dims, pieces, -0.22, 0.18)
    return jnp.clip(with_spikes(values, jax.random.fold_in(stream_key, 3), *heavy), -reach, reach).astype(held_as)


def setup_inputs(seed: int = 0) -> dict:
    key_list = jax.random.split(jax.random.key(seed), 16)
    return {
        "inputs": bell_draw(key_list[0], (TEXTS, MOL, D), 1.0, 6.0, ((0, 8), (1, 4))),
        "lengths": draw_lengths(jax.random.fold_in(key_list[15], 71), 0),
        "cotangent": bell_draw_with(key_list[2], (TEXTS, MOL, D), 1.0, 8.0, ((0, 8), (1, 4)), (0, 2, 8, 2.0)),
        "ln1_gain": jnp.clip(1.0 + 0.1 * jax.random.normal(key_list[3], (D,), jnp.float32), 0.5, 1.5),
        "ln1_bias": bell_draw(key_list[4], (D,), 0.3, 1.75, (), jnp.float32),
        "w_qkv": bell_draw(key_list[5], (3, D, D), D ** -0.5, 0.21875, ((2, 4),)),
        "b_qv": bell_draw(key_list[6], (2, D), 0.5, 3.0, ((1, 4),), jnp.float32),
        "w_out": bell_draw(key_list[7], (D, D), (D // 16) ** -0.5, 0.875, ((0, 4),)),
        "b_out": bell_draw(key_list[8], (D,), 0.3, 1.75, (), jnp.float32),
        "ln2_gain": jnp.clip(1.0 + 0.1 * jax.random.normal(key_list[9], (D,), jnp.float32), 0.5, 1.5),
        "ln2_bias": bell_draw(key_list[10], (D,), 0.3, 1.75, (), jnp.float32),
        "w_up": bell_draw(key_list[11], (D, FF), D ** -0.5, 0.21875, ((1, 4),)),
        "b_up": bell_draw(key_list[12], (FF,), 0.5, 3.0, ((0, 4),), jnp.float32),
        "w_down": bell_draw(key_list[13], (FF, D), FF ** -0.5, 0.109375, ((0, 4),)),
        "b_down": bell_draw(key_list[14], (D,), 0.3, 1.75, (), jnp.float32),
    }


@jax.custom_vjp
def low(v):
    return lax.optimization_barrier(v.astype(jnp.bfloat16)).astype(jnp.float32)

@jax.custom_vjp
def low_back(v):
    return v

def low_keep(v):
    return (low(v), None)

def low_pass(kept, grad):
    return (grad,)

def back_keep(v):
    return (v, None)

def back_low(kept, grad):
    return (low(grad),)
low.defvjp(low_keep, low_pass)
low_back.defvjp(back_keep, back_low)

def high(form, left, right):
    return jnp.einsum(form, left, right, precision=lax.Precision.HIGHEST)

def normalize(values, gain, shift):
    center = values - lax.optimization_barrier(jnp.mean(values, -1, keepdims=True))
    rstd = lax.rsqrt(lax.optimization_barrier(jnp.mean(center * center, -1, keepdims=True)) + 1e-05)
    return center * rstd * gain + shift

def forward(params, rows, text_lens):
    ln1_gain, ln1_bias, w_qkv, b_qv, w_out, b_out, ln2_gain, ln2_bias, w_up, b_up, w_down, b_down = params
    texts, length, model_width = rows.shape
    normed = low(normalize(rows, ln1_gain, ln1_bias))
    projected = high('tmd,cde->ctme', normed, w_qkv)
    head_shape = (texts, length, HEADS, HD)
    query = low(low_back(projected[0] + b_qv[0])).reshape(head_shape)
    keys = low(low_back(projected[1])).reshape(head_shape)
    values = low(low_back(projected[2] + b_qv[1])).reshape(head_shape)
    scores = low_back(high('tqhd,tkhd->thqk', query, keys) * HD ** (-0.5))
    key_live = jnp.arange(length)[None, :] < text_lens[:, None]
    scores = jnp.where(key_live[:, None, None, :], scores, -1e+30)
    attn_probs = jax.nn.softmax(scores, axis=-1)
    context = high('thqk,tkhd->tqhd', low(attn_probs), values).reshape(texts, length, model_width)
    context = low(low_back(context))
    resid = rows + low_back(high('tmf,fd->tmd', context, w_out)) + b_out
    normed_two = low(normalize(resid, ln2_gain, ln2_bias))
    upper = low_back(high('tmd,df->tmf', normed_two, w_up)) + b_up
    active = low(jax.nn.gelu(upper, approximate=False))
    return resid + high('tmf,fd->tmd', active, w_down) + b_down

def reference(inputs, lengths, cotangent, ln1_gain, ln1_bias, w_qkv, b_qv, w_out, b_out, ln2_gain, ln2_bias, w_up, b_up, w_down, b_down):
    params = tuple((item.astype(jnp.float32) for item in (ln1_gain, ln1_bias, w_qkv, b_qv, w_out, b_out, ln2_gain, ln2_bias, w_up, b_up, w_down, b_down)))
    blocks = TEXTS // TEXT_MB
    rows_all = inputs.reshape(blocks, TEXT_MB, MOL, D)
    lens_all = lengths.reshape(blocks, TEXT_MB)
    cot_all = cotangent.reshape(blocks, TEXT_MB, MOL, D)

    def block_step(summed, item):
        rows, text_lens, cot_rows = item
        rows = rows.astype(jnp.float32)
        output, pullback = jax.vjp(lambda weights, values: forward(weights, values, text_lens), params, rows)
        row_live = (jnp.arange(MOL)[None, :] < text_lens[:, None]).astype(jnp.float32)
        grad_params, grad_rows = pullback(cot_rows.astype(jnp.float32) * row_live[:, :, None])
        summed = jax.tree.map(lambda left, right: left + right, summed, grad_params)
        return (summed, (output.astype(jnp.bfloat16), grad_rows.astype(jnp.bfloat16)))
    zeros = jax.tree.map(jnp.zeros_like, params)
    totals, (outputs, grads) = lax.scan(block_step, zeros, (rows_all, lens_all, cot_all))
    return (outputs.reshape(TEXTS, MOL, D), grads.reshape(TEXTS, MOL, D), totals[0], totals[1], totals[2], totals[3], totals[4], totals[5], totals[6], totals[7], totals[8], totals[9], totals[10], totals[11])
```

```python
import functools

import jax
import jax.numpy as jnp
from jax import lax
from jax.experimental import pallas as pl
from jax.experimental.pallas import tpu as pltpu
from jax.sharding import PartitionSpec as P

D = 768
HD = 64
BF = jnp.bfloat16
F32 = jnp.float32
SCALE = HD**-0.5
LOG2E = 1.4426950408889634


def dot(left, right, left_dim, right_dim):
    return lax.dot_general(
        left, right, (((left_dim,), (right_dim,)), ((), ())), preferred_element_type=F32
    )


def attend_body(lens, q_ref, k_ref, v_ref, ctx_ref, p_ref, inv_ref, *, step):
    n = lens[pl.program_id(0)]
    length = q_ref.shape[0]

    def rows(live):
        edge = lax.broadcasted_iota(jnp.int32, (step, length), 0) < n - (live - step)
        for head in range(2):
            cols = slice(head * HD, head * HD + HD)
            keys = k_ref[:live, cols]
            values = v_ref[:live, cols]
            scores = dot(keys, q_ref[:, cols], 1, 1)
            last = jnp.where(edge, scores[live - step :], -1e30)
            if live > step:
                scores = jnp.concatenate([scores[: live - step], last], 0)
            else:
                scores = last
            top = jnp.max(scores, 0, keepdims=True)
            power = jnp.exp2((scores - top) * (SCALE * LOG2E))
            inverse = 1.0 / jnp.sum(power, 0, keepdims=True)
            low = power.astype(BF)
            p_ref[0, 0, head, :live, :] = low
            inv_ref[0, 0, head : head + 1, :] = inverse
            mixed = dot(low, values, 0, 0)
            ctx_ref[:, cols] = (mixed * inverse.reshape(length, 1)).astype(BF)

    for live in range(step, length + 1, step):
        pl.when((n > live - step) & (n <= live))(functools.partial(rows, live))


def attend_back_body(
    lens, q_ref, k_ref, v_ref, do_ref, p_ref, inv_ref, dq_ref, dk_ref, dv_ref, *, step
):
    n = lens[pl.program_id(0)]
    length = q_ref.shape[0]

    def rows(live):
        for head in range(2):
            cols = slice(head * HD, head * HD + HD)
            queries = q_ref[:live, cols]
            keys = k_ref[:live, cols]
            inverse = inv_ref[0, 0, head : head + 1, :live]
            grad = (do_ref[:live, cols].astype(F32) * inverse.reshape(live, 1)).astype(BF)
            low = p_ref[0, 0, head, :live, :live]
            grad_probs = dot(v_ref[:live, cols], grad, 1, 1)
            power = low.astype(F32)
            product = power * grad_probs
            inner = jnp.sum(product, 0, keepdims=True) * inverse
            grad_scores = (product - power * inner).astype(BF)
            dv_ref[:live, cols] = dot(low, grad, 1, 0).astype(BF)
            dk_ref[:live, cols] = (dot(grad_scores, queries, 1, 0) * SCALE).astype(BF)
            dq_ref[:live, cols] = (dot(grad_scores, keys, 0, 0) * SCALE).astype(BF)
        if live < length:
            for ref in (dq_ref, dk_ref, dv_ref):
                ref[live:, :] = jnp.zeros((length - live, 2 * HD), BF)

    for live in range(step, length + 1, step):
        pl.when((n > live - step) & (n <= live))(functools.partial(rows, live))


def attend_specs(texts, length, width):
    pairs = width // (2 * HD)
    cols = pl.BlockSpec((length, 2 * HD), lambda i, j, *_: (i, j))
    probs = pl.BlockSpec((1, 1, 2, length, length), lambda i, j, *_: (i, j, 0, 0, 0))
    inverse = pl.BlockSpec((1, 1, 2, length), lambda i, j, *_: (i, j, 0, 0))
    shapes = (
        jax.ShapeDtypeStruct((texts * length, width), BF),
        jax.ShapeDtypeStruct((texts, pairs, 2, length, length), BF),
        jax.ShapeDtypeStruct((texts, pairs, 2, length), F32),
    )
    return pairs, cols, probs, inverse, shapes


def attend(lens, q, k, v, length):
    texts = lens.shape[0]
    pairs, cols, probs, inverse, shapes = attend_specs(texts, length, q.shape[1])
    return pl.pallas_call(
        functools.partial(attend_body, step=length // 4),
        grid_spec=pltpu.PrefetchScalarGridSpec(
            num_scalar_prefetch=1,
            grid=(texts, pairs),
            in_specs=[cols] * 3,
            out_specs=[cols, probs, inverse],
        ),
        out_shape=shapes,
        compiler_params=pltpu.CompilerParams(vmem_limit_bytes=40 << 20),
        cost_estimate=pl.CostEstimate(
            flops=16 * texts * length * length * q.shape[1],
            bytes_accessed=2 * texts * length * length * q.shape[1] // HD,
            transcendentals=texts * length * length * q.shape[1] // HD,
        ),
        name="attend",
    )(lens, q, k, v)


def attend_back(lens, q, k, v, do, p, inv, length):
    texts = lens.shape[0]
    pairs, cols, probs, inverse, shapes = attend_specs(texts, length, q.shape[1])
    return pl.pallas_call(
        functools.partial(attend_back_body, step=length // 4),
        grid_spec=pltpu.PrefetchScalarGridSpec(
            num_scalar_prefetch=1,
            grid=(texts, pairs),
            in_specs=[cols] * 4 + [probs, inverse],
            out_specs=[cols] * 3,
        ),
        out_shape=[shapes[0]] * 3,
        compiler_params=pltpu.CompilerParams(vmem_limit_bytes=40 << 20),
        cost_estimate=pl.CostEstimate(
            flops=32 * texts * length * length * q.shape[1],
            bytes_accessed=2 * texts * length * length * q.shape[1] // HD,
            transcendentals=0,
        ),
        name="attend_back",
    )(lens, q, k, v, do, p, inv)


def norm_stats(values):
    center = values - jnp.mean(values, -1, keepdims=True)
    rstd = lax.rsqrt(jnp.mean(center * center, -1, keepdims=True) + 1e-05)
    return center * rstd, rstd


def norm_back(grad_norm, normal, rstd, gain):
    scaled = grad_norm * gain
    return rstd * (
        scaled
        - jnp.mean(scaled, -1, keepdims=True)
        - normal * jnp.mean(scaled * normal, -1, keepdims=True)
    )


def program(dp_size, tensor_size):
    bits = []
    while (1 << len(bits)) < dp_size:
        bits.append(1 << len(bits))

    def pp_tensor(values, flip):
        return lax.ppermute(values, "tensor", [(i, i ^ flip) for i in range(tensor_size)])

    def pp_dp(values, flip):
        return lax.ppermute(values, "dp", [(i, i ^ flip) for i in range(dp_size)])

    def on_device(
        inputs,
        lengths,
        cotangent,
        ln1_gain,
        ln1_bias,
        w_qkv,
        b_qv,
        w_out,
        b_out,
        ln2_gain,
        ln2_bias,
        w_up,
        b_up,
        w_down,
        b_down,
    ):
        t = lax.axis_index("tensor")
        d = lax.axis_index("dp")
        texts_all, part = inputs.shape[:2]
        texts = texts_all // tensor_size
        length = part * tensor_size
        rows = texts * length
        rels = range(tensor_size)

        def pick(values, index, axis):
            return lax.dynamic_index_in_dim(values, index, axis, keepdims=False)

        def to_texts(values):
            blocks = values.reshape(tensor_size, texts, part, D)
            out = jnp.zeros((texts, tensor_size, part, D), values.dtype)
            for r in rels:
                block = pick(blocks, t ^ r, 0)
                if r:
                    block = pp_tensor(block, r)
                out = lax.dynamic_update_slice(out, block[:, None], (0, t ^ r, 0, 0))
            return out.reshape(rows, D)

        def to_rows(values):
            blocks = values.reshape(texts, tensor_size, part, D)
            out = jnp.zeros((tensor_size, texts, part, D), values.dtype)
            for r in rels:
                block = pick(blocks, t ^ r, 1)
                if r:
                    block = pp_tensor(block, r)
                out = lax.dynamic_update_slice(out, block[None], (t ^ r, 0, 0, 0))
            return out.reshape(texts_all, part, D)

        def spread(shard):
            near = pp_tensor(shard, 1)
            far = pp_tensor(shard, 2)
            return [shard, near, far, pp_tensor(far, 1)]

        def after(values, *waits):
            return lax.optimization_barrier((values,) + waits)[0]

        x = to_texts(inputs).astype(F32)
        wq = spread(w_qkv)
        small = jnp.concatenate([b_qv.reshape(-1), b_up])
        small = [small] + [pp_tensor(small, r) for r in rels[1:]]
        local = w_qkv.shape[2]
        units = b_up.shape[0]
        bqv = [s[: 2 * local].reshape(2, local) for s in small]
        bup = [s[2 * local :] for s in small]
        wo = spread(after(w_out, wq[2]))
        wu = spread(after(w_up, wq[2]))
        wd = spread(after(w_down, wu[2]))
        cot = to_texts(after(cotangent, wd[2]))
        lens = lax.dynamic_slice_in_dim(lengths, t * texts, texts)

        normal_one, rstd_one = norm_stats(x)
        h1 = (normal_one * ln1_gain + ln1_bias).astype(BF)
        pairs = [(0, 1), (2, 3)]
        heads = []
        for a, b in pairs:
            w = jnp.concatenate([wq[a], wq[b]], 2)
            bias = jnp.concatenate([bqv[a], bqv[b]], 1)
            q = (dot(h1, w[0], 1, 0) + bias[0]).astype(BF)
            k = dot(h1, w[1], 1, 0).astype(BF)
            v = (dot(h1, w[2], 1, 0) + bias[1]).astype(BF)
            ctx, p, inv = attend(lens, q, k, v, length)
            heads.append((q, k, v, ctx, p, inv, w, jnp.concatenate([wo[a], wo[b]], 0)))
        resid = x + b_out
        for q, k, v, ctx, p, inv, w, w_o in heads:
            resid = resid + dot(ctx, w_o, 1, 0)
        normal_two, rstd_two = norm_stats(resid)
        h2 = (normal_two * ln2_gain + ln2_bias).astype(BF)
        acts, slopes = [], []
        out = resid + b_down
        for r in rels:
            upper = dot(h2, wu[r], 1, 0) + bup[r]
            below = 0.5 * (1.0 + lax.erf(upper * (0.5**0.5)))
            acts.append((upper * below).astype(BF))
            density = jnp.exp(-0.5 * upper * upper) * 0.3989422804014327
            slopes.append((below + upper * density).astype(BF))
            out = out + dot(acts[r], wd[r], 1, 0)
        layer_out = to_rows(out.astype(BF))

        def collect(parts):
            near = pp_tensor(jnp.concatenate([parts[1], parts[3]], 1).astype(BF), 1)
            width = parts[0].shape[1]
            far = pp_tensor((parts[2] + near[:, width:]).astype(BF), 2)
            total = parts[0] + near[:, :width] + far
            for bit in bits:
                block = total.shape[0] // 2
                inner = D // dp_size
                view = total.reshape(-1, 2, inner, width)
                mine = (d // bit) % 2
                send = pick(view, 1 - mine, 1).astype(BF)
                keep = pick(view, mine, 1)
                total = (keep + pp_dp(send, bit)).reshape(block, width)
            return total

        def all_sum(values):
            for flip in (1, 2):
                values = values + pp_tensor(values, flip)
            for bit in bits:
                values = values + pp_dp(values, bit)
            return values

        place = jnp.arange(length)
        live = (place[None, :] < lens[:, None]).reshape(rows, 1)
        g_low = jnp.where(live, cot, jnp.zeros_like(cot))
        g = g_low.astype(F32)
        bias_down = jnp.sum(g, 0)
        grad_down = collect([dot(g_low, acts[r], 0, 0) for r in rels])
        dups, bias_up = [], []
        dh2 = 0.0
        for r in rels:
            dup = dot(g_low, wd[r], 1, 1) * slopes[r].astype(F32)
            bias_up.append(jnp.sum(dup, 0))
            dups.append(dup.astype(BF))
            dh2 = dh2 + dot(dups[r], wu[r], 1, 1)
        grad_up = collect([dot(h2, dups[r], 0, 0) for r in rels])
        gain_two = jnp.sum(dh2 * normal_two, 0)
        shift_two = jnp.sum(dh2, 0)
        dres = g + norm_back(dh2, normal_two, rstd_two, ln2_gain)
        bias_attn = jnp.sum(dres, 0)
        dres_low = dres.astype(BF)
        grad_out_parts = []
        for q, k, v, ctx, p, inv, w, w_o in heads:
            both = dot(dres_low, ctx, 0, 0)
            grad_out_parts += [both[:, :local], both[:, local:]]
        grad_out = collect(grad_out_parts)
        up_full = jnp.zeros((tensor_size, units), F32)
        for r in rels:
            up_full = lax.dynamic_update_slice(up_full, bias_up[r][None], (t ^ r, 0))
        early = all_sum(
            jnp.concatenate([bias_down, gain_two, shift_two, bias_attn, up_full.reshape(-1)])
        )
        dh1 = 0.0
        qkv_parts = []
        qv_full = jnp.zeros((tensor_size, 2, local), F32)
        for (a, b), (q, k, v, ctx, p, inv, w, w_o) in list(zip(pairs, heads)):
            dctx = dot(dres_low, w_o, 1, 1).astype(BF)
            grads = attend_back(lens, q, k, v, dctx, p, inv, length)
            sums = [jnp.sum(grads[c].astype(F32), 0) for c in (0, 2)]
            mats = [dot(h1, grads[c], 0, 0) for c in range(3)]
            for index, r in enumerate((a, b)):
                cols = slice(index * local, index * local + local)
                qkv_parts.append(jnp.concatenate([m[:, cols] for m in mats], 1))
                qv = jnp.stack([s[cols] for s in sums])
                qv_full = lax.dynamic_update_slice(qv_full, qv[None], (t ^ r, 0, 0))
            for c in range(3):
                dh1 = dh1 + dot(grads[c], w[c], 1, 1)
        grad_qkv = collect(qkv_parts)
        gain_one = jnp.sum(dh1 * normal_one, 0)
        shift_one = jnp.sum(dh1, 0)
        grad_in = (dres + norm_back(dh1, normal_one, rstd_one, ln1_gain)).astype(BF)
        grad_input = to_rows(grad_in)
        late = all_sum(jnp.concatenate([gain_one, shift_one, qv_full.reshape(-1)]))
        grad_qv_bias = pick(late[2 * D :].reshape(tensor_size, 2, local), t, 0)
        grad_up_bias = pick(early[4 * D :].reshape(tensor_size, units), t, 0)
        return (
            layer_out,
            grad_input,
            late[:D],
            late[D : 2 * D],
            jnp.stack([grad_qkv[:, c * local : c * local + local] for c in range(3)]),
            grad_qv_bias,
            grad_out.T,
            early[3 * D : 4 * D],
            early[D : 2 * D],
            early[2 * D : 3 * D],
            grad_up,
            grad_up_bias,
            grad_down.T,
            early[:D],
        )

    return on_device


def solution(mesh):
    return jax.shard_map(
        program(mesh.shape["dp"], mesh.shape["tensor"]),
        mesh=mesh,
        in_specs=(
            P("dp", "tensor", None),
            P("dp"),
            P("dp", "tensor", None),
            P(),
            P(),
            P(None, None, "tensor"),
            P(None, "tensor"),
            P("tensor", None),
            P(),
            P(),
            P(),
            P(None, "tensor"),
            P("tensor"),
            P("tensor", None),
            P(),
        ),
        out_specs=(
            P("dp", "tensor", None),
            P("dp", "tensor", None),
            P(),
            P(),
            P(None, "dp", "tensor"),
            P(None, "tensor"),
            P("tensor", "dp"),
            P(),
            P(),
            P(),
            P("dp", "tensor"),
            P("tensor"),
            P("tensor", "dp"),
            P(),
        ),
        check_vma=False,
    )
```

```python
import functools

import jax
import jax.numpy as jnp
from jax import lax
from jax.experimental import pallas as pl
from jax.experimental.pallas import tpu as pltpu
from jax.sharding import PartitionSpec as P

D = 768
HD = 64
BF = jnp.bfloat16
F32 = jnp.float32
SCALE = HD**-0.5
LOG2E = 1.4426950408889634


def dot(left, right, left_dim, right_dim):
    return lax.dot_general(
        left, right, (((left_dim,), (right_dim,)), ((), ())), preferred_element_type=F32
    )


def norm_stats(values):
    center = values - jnp.mean(values, -1, keepdims=True)
    rstd = lax.rsqrt(jnp.mean(center * center, -1, keepdims=True) + 1e-05)
    return center * rstd, rstd


def norm_back(grad_norm, normal, rstd, gain):
    scaled = grad_norm * gain
    return rstd * (
        scaled
        - jnp.mean(scaled, -1, keepdims=True)
        - normal * jnp.mean(scaled * normal, -1, keepdims=True)
    )


class Clock:
    def __init__(self):
        self.last = None

    def after(self, values):
        return values if self.last is None else tie(values, self.last)

    def then(self, values):
        self.last = jax.tree.leaves(values)[0]
        return values


def tie(value, *waits):
    return lax.optimization_barrier((value,) + waits)[0]


def call(clock, body, out_shape, operands, *, grid=(), in_specs=None, out_specs=None, scalars=(), scratch=(),
         name=None):
    operands = (clock.after(operands[0]),) + tuple(operands[1:])
    out = pl.pallas_call(
        body,
        out_shape=out_shape,
        grid_spec=pltpu.PrefetchScalarGridSpec(
            num_scalar_prefetch=len(scalars),
            grid=grid,
            in_specs=in_specs,
            out_specs=out_specs,
            scratch_shapes=scratch,
        ),
        compiler_params=pltpu.CompilerParams(vmem_limit_bytes=48 << 20),
        cost_estimate=pl.CostEstimate(flops=0, bytes_accessed=0, transcendentals=0),
        name=name,
    )(*scalars, *operands)
    return clock.then(out)


def shape_of(dims, dtype=BF):
    return jax.ShapeDtypeStruct(tuple(dims), dtype)


def whole(values):
    return pl.BlockSpec(values.shape, lambda *_: (0,) * len(values.shape))


def side_by_side(clock, w):
    half, width = w.shape[1] // 2, w.shape[2]

    def body(w_ref, *refs):
        for i in range(2):
            for c in range(3):
                refs[i][:, c * width : (c + 1) * width] = w_ref[c, i * half : (i + 1) * half, :]

    out = [shape_of((half, 3 * width))] * 2
    return call(
        clock, body, out, (w,), grid=(1,), in_specs=[whole(w)], out_specs=[whole(v) for v in out],
        name="side_by_side",
    )


def order_halves(clock, mine, other, index):
    def body(at, mine_ref, other_ref, first_ref, second_ref):
        keep = at[0] == 0
        first_ref[...] = jnp.where(keep, mine_ref[...], other_ref[...])
        second_ref[...] = jnp.where(keep, other_ref[...], mine_ref[...])

    return call(
        clock, body, [shape_of(mine.shape)] * 2, (mine, other), grid=(1,), in_specs=[whole(mine), whole(other)],
        out_specs=[whole(mine), whole(mine)], scalars=(index.reshape(1),), name="order_halves",
    )


def times(left, pieces):
    total, start = None, 0
    for ref in pieces:
        part = dot(left[:, start : start + ref.shape[0]], ref[...], 1, 0)
        start += ref.shape[0]
        total = part if total is None else total + part
    return total


def times_turned(left, pieces):
    parts = [dot(left, ref[...], 1, 1) for ref in pieces]
    return parts[0] if len(parts) == 1 else jnp.concatenate(parts, 1)


def split_refs(refs, counts):
    out = []
    for count in counts:
        out.append(refs[:count])
        refs = refs[count:]
    return out


def row_block(values, steps):
    return pl.BlockSpec((values.shape[0] // steps, values.shape[1]), lambda i, *_: (i, 0))


def project(clock, h, w, bias):
    def body(h_ref, bias_ref, *refs):
        refs[-1][...] = (times(h_ref[...], refs[:-1]) + bias_ref[...]).astype(BF)

    bias = bias.reshape(1, -1)
    out = shape_of((h.shape[0], bias.shape[1]))
    return call(
        clock, body, out, (h, bias, *w), grid=(4,), in_specs=[row_block(h, 4), whole(bias)] + [whole(v) for v in w],
        out_specs=row_block(out, 4), name="project",
    )


def attention_out(clock, x, ctx, w, vectors):
    count = len(ctx)

    def body(x_ref, *refs):
        ctx_refs, w_refs, (bias_ref, gain_ref, shift_ref), (out_ref, h_ref) = split_refs(refs, (count, count, 3, 2))
        total = x_ref[...].astype(F32) + bias_ref[...]
        for r in range(count):
            total = total + dot(ctx_refs[r][...], w_refs[r][...], 1, 0)
        out_ref[...] = total
        normal, _ = norm_stats(total)
        h_ref[...] = (normal * gain_ref[...] + shift_ref[...]).astype(BF)

    vectors = [v.reshape(1, -1) for v in vectors]
    out = [shape_of(x.shape, F32), shape_of(x.shape)]
    return call(
        clock, body, out, (x, *ctx, *w, *vectors), grid=(4,),
        in_specs=[row_block(v, 4) for v in (x, *ctx)] + [whole(v) for v in (*w, *vectors)],
        out_specs=[row_block(v, 4) for v in out], name="attention_out",
    )


def up(clock, h, w, bias):
    def body(h_ref, bias_ref, *refs):
        upper = times(h_ref[...], refs[:-2]) + bias_ref[...]
        below = 0.5 * (1.0 + lax.erf(upper * (0.5**0.5)))
        density = jnp.exp(-0.5 * upper * upper) * 0.3989422804014327
        refs[-2][...] = (upper * below).astype(BF)
        refs[-1][...] = (below + upper * density).astype(BF)

    bias = bias.reshape(1, -1)
    out = [shape_of((h.shape[0], bias.shape[1]))] * 2
    return call(
        clock, body, out, (h, bias, *w), grid=(4,), in_specs=[row_block(h, 4), whole(bias)] + [whole(v) for v in w],
        out_specs=[row_block(v, 4) for v in out], name="up",
    )


def to_owner(refs, at, values, scratch, count):
    text, late = pl.program_id(0) // 2, pl.program_id(0) % 2
    part = values.shape[0] * 2 // count
    scratch[...] = values.astype(BF)
    for r in range(count):
        place = at[0] ^ r

        @pl.when(place // (count // 2) == late)
        def _():
            start = pl.multiple_of((place % (count // 2)) * part, part)
            refs[r][pl.ds(text, 1)] = scratch[pl.ds(start, part), :][None]


def down_out(clock, resid, acts, w, bias, me, texts):
    count = len(acts)
    steps = texts * 2

    def body(at, resid_ref, *refs):
        act_refs, w_refs, (bias_ref,), outs, (scratch,) = split_refs(refs, (count, count, 1, count, 1))
        total = resid_ref[...] + bias_ref[...]
        for r in range(count):
            total = total + dot(act_refs[r][...], w_refs[r][...], 1, 0)
        to_owner(outs, at, total, scratch, count)

    bias = bias.reshape(1, -1)
    out = [shape_of((texts, resid.shape[0] // texts // count, resid.shape[1]))] * count
    return call(
        clock, body, out, (resid, *acts, *w, bias), grid=(steps,),
        in_specs=[row_block(v, steps) for v in (resid, *acts)] + [whole(v) for v in (*w, bias)],
        out_specs=[whole(v) for v in out], scalars=(me.reshape(1),),
        scratch=[pltpu.VMEM((resid.shape[0] // steps, resid.shape[1]), BF)], name="down_out",
    )


def norm_one_back(clock, x, dres, dqkv, w, gain, me, texts):
    count = len(dqkv)
    steps = texts * 2
    sizes = [len(pieces) for pieces in w]
    flat = [v for pieces in w for v in pieces]

    def body(at, x_ref, dres_ref, *refs):
        grads, w_refs, (gain_ref,), outs, (gain_sum, shift_sum, scratch) = split_refs(
            refs, (count, len(flat), 1, count, 3)
        )
        w_refs = split_refs(w_refs, sizes)
        total = None
        for r in range(count):
            part = times_turned(grads[r][...], w_refs[r])
            total = part if total is None else total + part
        normal, rstd = norm_stats(x_ref[...].astype(F32))

        @pl.when(pl.program_id(0) == 0)
        def _():
            gain_sum[...] = jnp.zeros_like(gain_sum)
            shift_sum[...] = jnp.zeros_like(shift_sum)

        gain_sum[...] += jnp.sum(total * normal, 0, keepdims=True)
        shift_sum[...] += jnp.sum(total, 0, keepdims=True)
        to_owner(outs, at, dres_ref[...] + norm_back(total, normal, rstd, gain_ref[...]), scratch, count)

    gain = gain.reshape(1, -1)
    out = [shape_of((texts, x.shape[0] // texts // count, x.shape[1]))] * count + [shape_of(gain.shape, F32)] * 2
    out = call(
        clock, body, out, (x, dres, *dqkv, *flat, gain), grid=(steps,),
        in_specs=[row_block(v, steps) for v in (x, dres, *dqkv)] + [whole(v) for v in (*flat, gain)],
        out_specs=[whole(v) for v in out], scalars=(me.reshape(1),),
        scratch=[pltpu.VMEM((x.shape[0] // steps, x.shape[1]), BF)], name="norm_one_back",
    )
    return out[:count], out[count], out[count + 1]


def join_norm(clock, blocks, me, gain, shift):
    texts, part, width = blocks[0].shape
    count = len(blocks)

    def body(at, *refs):
        ins, (gain_ref, shift_ref, x_ref, h_ref) = refs[:count], refs[count:]
        for r in range(count):
            for i in range(texts):
                start = pl.multiple_of(i * count * part + (at[0] ^ r) * part, part)
                low = ins[r][i]
                normal, _ = norm_stats(low.astype(F32))
                x_ref[pl.ds(start, part), :] = low
                h_ref[pl.ds(start, part), :] = (normal * gain_ref[...] + shift_ref[...]).astype(BF)

    out = [shape_of((texts * count * part, width))] * 2
    operands = (*blocks, gain.reshape(1, -1), shift.reshape(1, -1))
    return call(
        clock, body, out, operands, grid=(1,), in_specs=[whole(v) for v in operands], out_specs=[whole(v) for v in out],
        scalars=(me.reshape(1),), name="join_norm",
    )


def join_mask(clock, blocks, me, lens):
    texts, part, width = blocks[0].shape
    count = len(blocks)

    def body(at, n, *refs):
        ins, (g_ref, sum_ref) = refs[:count], refs[count:]
        total = jnp.zeros((1, width), F32)
        for r in range(count):
            for i in range(texts):
                place = (at[0] ^ r) * part
                start = pl.multiple_of(i * count * part + place, part)
                live = lax.broadcasted_iota(jnp.int32, (part, width), 0) + place < n[i]
                values = jnp.where(live, ins[r][i].astype(F32), 0.0)
                total = total + jnp.sum(values, 0, keepdims=True)
                g_ref[pl.ds(start, part), :] = values.astype(BF)
        sum_ref[...] = total

    out = [shape_of((texts * count * part, width)), shape_of((1, width), F32)]
    return call(
        clock, body, out, blocks, grid=(1,), in_specs=[whole(v) for v in blocks], out_specs=[whole(v) for v in out],
        scalars=(me.reshape(1), lens), name="join_mask",
    )


def join_rows(clock, blocks, me):
    texts = blocks[0].shape[0]
    count = len(blocks)

    def body(at, *refs):
        for r in range(count):
            refs[count][pl.ds((at[0] ^ r) * texts, texts)] = refs[r][...]

    out = shape_of((texts * count,) + blocks[0].shape[1:])
    return call(
        clock, body, out, blocks, grid=(1,), in_specs=[whole(v) for v in blocks], out_specs=whole(out),
        scalars=(me.reshape(1),), name="join_rows",
    )


def up_back(clock, g, ups, downs, slopes, base, resid, gain):
    rows, width = g.shape
    count = len(ups)
    units = downs[0].shape[0]
    sizes = [len(pieces) for pieces in ups]
    flat = [v for pieces in ups for v in pieces]
    last = base is not None

    def body(g_ref, *refs):
        up_refs, down_refs, slope_refs, more, grad_refs, sum_refs, outs = split_refs(
            refs, (len(flat), count, count, 3 if last else 0, count, count, 5 if last else 1)
        )
        up_refs = split_refs(up_refs, sizes)
        grad = g_ref[...]
        total = more[0][...] if last else None

        @pl.when(pl.program_id(0) == 0)
        def _():
            for ref in list(sum_refs) + list(outs[2:]):
                ref[...] = jnp.zeros_like(ref)

        for s in range(count):
            upper = dot(grad, down_refs[s][...], 1, 1) * slope_refs[s][...].astype(F32)
            sum_refs[s][...] += jnp.sum(upper, 0, keepdims=True)
            low = upper.astype(BF)
            grad_refs[s][...] = low
            part = times_turned(low, up_refs[s])
            total = part if total is None else total + part
        if last:
            normal, rstd = norm_stats(more[1][...])
            outs[2][...] += jnp.sum(total * normal, 0, keepdims=True)
            outs[3][...] += jnp.sum(total, 0, keepdims=True)
            total = grad.astype(F32) + norm_back(total, normal, rstd, more[2][...])
            outs[4][...] += jnp.sum(total, 0, keepdims=True)
            outs[1][...] = total.astype(BF)
        outs[0][...] = total

    sums, vector = shape_of((1, units), F32), shape_of((1, width), F32)
    unit = pl.BlockSpec((rows // 4, units), lambda i: (i, 0))
    operands = (g, *flat, *downs, *slopes)
    in_specs = [row_block(g, 4)] + [whole(v) for v in (*flat, *downs)] + [unit] * count
    outs = [shape_of((rows, width), F32)]
    out_specs = [row_block(g, 4)]
    if last:
        gain = gain.reshape(1, -1)
        operands += (base, resid, gain)
        in_specs += [row_block(g, 4)] * 2 + [whole(gain)]
        outs += [shape_of((rows, width))] + [vector] * 3
        out_specs += [row_block(g, 4)] + [whole(vector)] * 3
    out = call(
        clock, body,
        [shape_of((rows, units))] * count + [sums] * count + outs,
        operands,
        grid=(4,),
        in_specs=in_specs,
        out_specs=[unit] * count + [whole(sums)] * count + out_specs,
        name="up_back",
    )
    return list(out[:count]), list(out[count : 2 * count]), out[2 * count :]


def weight_grads(clock, lefts, slots, near=None, split=None, apart=False, pieces=False):
    rows, width = lefts[0].shape
    columns = sum(right.shape[1] for _, right in slots[0])
    count = len(slots)
    half = width // 2
    rights = [right for slot in slots for _, right in slot]

    def body(*refs):
        if split is not None:
            at, refs = refs[0], refs[1:]
        left_refs, refs = refs[: len(lefts)], refs[len(lefts) :]
        right_refs, refs = list(refs[: len(rights)]), refs[len(rights) :]
        if near is not None:
            near_refs, refs = refs[: 2 * count], refs[2 * count :]
        for s, slot in enumerate(slots):
            start = 0
            for which, right in slot:
                product = dot(left_refs[which][...], right_refs.pop(0)[...], 0, 0)
                cols = slice(start, start + right.shape[1])
                start = cols.stop
                for i in range(2):
                    low, high = max(cols.start, i * columns // 2), min(cols.stop, (i + 1) * columns // 2)
                    if low < high:
                        here = slice(low - cols.start, high - cols.start)
                        there = slice(low - i * columns // 2, high - i * columns // 2)
                        value = product[:, here]
                        if near is not None:
                            value = value + near_refs[2 * s + i][:, there].astype(F32)
                        if pieces:
                            refs[2 * s + i][:, there] = value.astype(BF)
                        elif apart:
                            refs[s][0, :, low:high] = value.astype(BF)
                        elif split is None:
                            refs[0][s, :, low:high] = value.astype(BF)
                        else:
                            refs[2][:, low:high] = value
            if split is not None:
                outer, inner = split[0] // 2, width // split[0] // 2
                for a in range(outer):
                    for ref, bit in ((refs[0], 1 - at[0]), (refs[1], at[0])):
                        place = pl.multiple_of((2 * a + bit) * inner, inner)
                        ref[s, a * inner : (a + 1) * inner, :] = refs[2][pl.ds(place, inner), :].astype(BF)

    left = pl.BlockSpec((rows, half), lambda i, *_: (0, i))
    tall = pl.BlockSpec((count, half, columns), lambda i, *_: (0, i, 0))
    narrow = pl.BlockSpec((half, columns // 2), lambda i, *_: (i, 0))
    short = pl.BlockSpec((count, half // 2, columns), lambda i, *_: (0, i, 0))
    operands = (*lefts, *rights) + (() if near is None else tuple(near))
    if pieces:
        out_shape = [shape_of((width, columns // 2))] * (2 * count)
        out_specs = [narrow] * (2 * count)
    elif apart:
        out_shape = [shape_of((1, width, columns))] * count
        out_specs = [pl.BlockSpec((1, half, columns), lambda i, *_: (0, i, 0))] * count
    elif split is None:
        out_shape, out_specs = shape_of((count, width, columns)), tall
    else:
        out_shape, out_specs = [shape_of((count, half, columns))] * 2, [short] * 2
    return call(
        clock, body,
        out_shape,
        operands,
        grid=(2,),
        in_specs=[left] * len(lefts) + [whole(v) for v in rights] + ([] if near is None else [narrow] * len(near)),
        out_specs=out_specs,
        scalars=() if split is None else (split[1].reshape(1),),
        scratch=[] if split is None else [pltpu.VMEM((half, columns), F32)],
        name="weight_grads",
    )


def add_split(clock, keep, arrived, outer, index):
    columns = keep.shape[-1]
    inner = keep.size // columns // outer // 2

    def body(at, keep_ref, arrived_ref, send_ref, out_ref):
        for ref, bit in ((send_ref, 1 - at[0]), (out_ref, at[0])):
            ref[0] = (keep_ref[0, bit].astype(F32) + arrived_ref[0, bit].astype(F32)).astype(BF)

    tall = pl.BlockSpec((1, 2, inner, columns), lambda i, *_: (i, 0, 0, 0))
    short = pl.BlockSpec((1, inner, columns), lambda i, *_: (i, 0, 0))
    return call(
        clock, body,
        [shape_of((outer, inner, columns))] * 2,
        (keep.reshape(outer, 2, inner, columns), arrived.reshape(outer, 2, inner, columns)),
        grid=(outer,),
        in_specs=[tall] * 2,
        out_specs=[short] * 2,
        scalars=(jnp.asarray(index, jnp.int32).reshape(1),),
        name="add_split",
    )


def attend_body(lens, *refs, step, heads):
    ins, outs, (p_ref, inv_ref) = refs[:2], refs[2:4], refs[4:]
    n = lens[pl.program_id(0)]
    length = ins[0].shape[0]
    width = heads * HD

    def rows(live):
        edge = lax.broadcasted_iota(jnp.int32, (step, length), 0) < n - (live - step)
        for which in range(2):
            ref, ctx_ref = ins[which], outs[which]
            for head in range(heads):
                slot = which * heads + head
                cols = slice(head * HD, head * HD + HD)
                keys = ref[:live, width + head * HD : width + head * HD + HD]
                values = ref[:live, 2 * width + head * HD : 2 * width + head * HD + HD]
                scores = dot(keys, ref[:, cols], 1, 1)
                last = jnp.where(edge, scores[live - step :], -1e30)
                if live > step:
                    scores = jnp.concatenate([scores[: live - step], last], 0)
                else:
                    scores = last
                top = jnp.max(scores, 0, keepdims=True)
                power = jnp.exp2((scores - top) * (SCALE * LOG2E))
                inverse = 1.0 / jnp.sum(power, 0, keepdims=True)
                low = power.astype(BF)
                p_ref[0, slot, :live, :] = low
                inv_ref[0, slot : slot + 1, :] = inverse
                mixed = dot(low, values, 0, 0)
                ctx_ref[:, cols] = (mixed * inverse.reshape(length, 1)).astype(BF)

    for live in range(step, length + 1, step):
        pl.when((n > live - step) & (n <= live))(functools.partial(rows, live))


def attend_back_body(lens, *refs, step, heads):
    ins, (grad_ref,), w_refs, (p_ref, inv_ref) = refs[:2], refs[2:3], refs[3:5], refs[5:7]
    outs, sums, do_ref = refs[7:9], refs[9:11], refs[11]
    n = lens[pl.program_id(0)]
    length = ins[0].shape[0]
    width = heads * HD

    def rows(live):
        for which in range(2):
            ref, out_ref = ins[which], outs[which]
            do_ref[:live, :] = dot(grad_ref[:live, :], w_refs[which][...], 1, 1)
            for head in range(heads):
                slot = which * heads + head
                at = [slice(c * width + head * HD, c * width + head * HD + HD) for c in range(3)]
                inverse = inv_ref[0, slot : slot + 1, :live]
                grad = (do_ref[:live, at[0]] * inverse.reshape(live, 1)).astype(BF)
                low = p_ref[0, slot, :live, :live]
                grad_probs = dot(ref[:live, at[2]], grad, 1, 1)
                power = low.astype(F32)
                product = power * grad_probs
                inner = jnp.sum(product, 0, keepdims=True) * inverse
                grad_scores = (product - power * inner).astype(BF)
                out_ref[:live, at[2]] = dot(low, grad, 1, 0).astype(BF)
                out_ref[:live, at[1]] = (dot(grad_scores, ref[:live, at[0]], 1, 0) * SCALE).astype(BF)
                out_ref[:live, at[0]] = (dot(grad_scores, ref[:live, at[1]], 0, 0) * SCALE).astype(BF)
            if live < length:
                out_ref[live:, :] = jnp.zeros((length - live, 3 * width), BF)
            sums[which][...] += jnp.sum(out_ref[:live, :].astype(F32), 0, keepdims=True)

    @pl.when(pl.program_id(0) == 0)
    def _():
        for ref in sums:
            ref[...] = jnp.zeros_like(ref)

    for live in range(step, length + 1, step):
        pl.when((n > live - step) & (n <= live))(functools.partial(rows, live))


def attend_call(clock, lens, qkv, back, length):
    texts = lens.shape[0]
    width = qkv[0].shape[1] // 3
    heads = width // HD
    wide = pl.BlockSpec((length, 3 * width), lambda i, *_: (i, 0))
    slim = pl.BlockSpec((length, width), lambda i, *_: (i, 0))
    full = pl.BlockSpec((length, D), lambda i, *_: (i, 0))
    probs = pl.BlockSpec((1, 2 * heads, length, length), lambda i, *_: (i, 0, 0, 0))
    inverse = pl.BlockSpec((1, 2 * heads, length), lambda i, *_: (i, 0, 0))
    rows = texts * length
    if back is None:
        return call(
            clock,
            functools.partial(attend_body, step=length // 4, heads=heads),
            [shape_of((rows, width))] * 2
            + [shape_of((texts, 2 * heads, length, length)), shape_of((texts, 2 * heads, length), F32)],
            tuple(qkv),
            grid=(texts,),
            in_specs=[wide] * 2,
            out_specs=[slim] * 2 + [probs, inverse],
            scalars=(lens,),
            name="attend",
        )
    return call(
        clock,
        functools.partial(attend_back_body, step=length // 4, heads=heads),
        [shape_of((rows, 3 * width))] * 2 + [shape_of((1, 3 * width), F32)] * 2,
        tuple(qkv) + tuple(back),
        grid=(texts,),
        in_specs=[wide] * 2 + [full] + [whole(w) for w in back[1:3]] + [probs, inverse],
        out_specs=[wide] * 2 + [pl.BlockSpec((1, 3 * width), lambda i, *_: (0, 0))] * 2,
        scalars=(lens,),
        scratch=[pltpu.VMEM((length, width), F32)],
        name="attend_back",
    )


def program(dp_size, tensor_size):
    bits = dp_size.bit_length() - 1

    def pp_tensor(values, flip):
        return lax.ppermute(values, "tensor", [(i, i ^ flip) for i in range(tensor_size)])

    def pp_dp(values, bit):
        return lax.ppermute(values, "dp", [(i, i ^ (1 << bit)) for i in range(dp_size)])

    def on_device(
        inputs,
        lengths,
        cotangent,
        ln1_gain,
        ln1_bias,
        w_qkv,
        b_qv,
        w_out,
        b_out,
        ln2_gain,
        ln2_bias,
        w_up,
        b_up,
        w_down,
        b_down,
    ):
        t = lax.axis_index("tensor")
        d = lax.axis_index("dp")
        texts_all, part = inputs.shape[:2]
        texts = texts_all // tensor_size
        length = part * tensor_size
        rows = texts * length
        rels = range(tensor_size)
        local = w_qkv.shape[2]
        units = b_up.shape[0]
        inner = D // dp_size
        bit_of = [(d >> b) & 1 for b in range(bits)]
        clock = Clock()

        def pick(values, index, axis):
            return lax.dynamic_index_in_dim(values, index, axis, keepdims=False)

        def text_blocks(values):
            return [
                lax.dynamic_slice(values, ((t ^ r) * texts, 0, 0), (texts, part, D)) for r in rels
            ]

        def row_blocks(values):
            blocks = values.reshape(texts, tensor_size, part, D)
            return [pick(blocks, t ^ r, 1) for r in rels]

        def exchange(blocks):
            far = {r: pp_tensor(blocks[r], r) for r in (3, 2, 1)}
            return [blocks[0]] + [far[r] for r in (1, 2, 3)]

        def half(values):
            count = values.shape[0] // 2
            return lax.dynamic_slice_in_dim(values, bit_of[0] * count, count)

        class Chain:
            def __init__(self, lefts, slots, near, steps):
                self.steps = list(steps)
                self.dims = [len(slots)] + [2] * bits
                step = self.steps.pop(0)
                outer, index = self.place(step)
                if step == "y":
                    self.keep, self.sent = weight_grads(clock, lefts, slots, near, apart=True)
                elif inner % 16 == 0 and outer > len(slots):
                    split = (outer // len(slots), index)
                    self.sent, self.keep = weight_grads(clock, lefts, slots, near, split)
                else:
                    total = weight_grads(clock, lefts, slots, near)
                    self.sent, self.keep = self.halves(total, outer, index)
                self.fly(step)

            def place(self, step):
                axis = 0 if step == "y" else bits - step
                outer = 1
                for size in self.dims[:axis]:
                    outer *= size
                self.dims[axis] = 1
                return outer, 0 * t if step == "y" else bit_of[step]

            def halves(self, total, outer, index):
                view = total.reshape(outer, 2, -1, total.shape[-1])
                return pick(view, 1 - index, 1), pick(view, index, 1)

            def fly(self, step):
                self.flight = pp_tensor(self.sent, 2) if step == "y" else pp_dp(self.sent, step)

            def step(self):
                arrived = clock.after(self.flight)
                step = self.steps.pop(0)
                outer, index = self.place(step)
                if inner % 16 == 0:
                    self.sent, self.keep = add_split(clock, self.keep, arrived, outer, index)
                else:
                    total = (self.keep.astype(F32) + arrived.astype(F32)).astype(BF)
                    self.sent, self.keep = self.halves(total, outer, index)
                self.fly(step)

            def last(self):
                total = self.keep.astype(F32) + clock.after(self.flight).astype(F32)
                return total.reshape(-1, total.shape[-1])

        high = list(range(2, bits))

        def from_near(lefts, slots):
            return [pp_tensor(v, 1) for v in weight_grads(clock, lefts, slots, pieces=True)]

        x_own = text_blocks(inputs)
        x_blocks = exchange(x_own)
        wq_own = side_by_side(clock, tie(w_qkv, x_own[1]))
        wq_near = [pp_tensor(v, 1) for v in wq_own]
        small = jnp.concatenate([b_qv.reshape(-1), tie(b_up, wq_own[0])])
        small = [small] + [pp_tensor(small, r) for r in (1, 2, 3)]
        bqkv = [
            jnp.concatenate([s[:local], jnp.zeros((local,), F32), s[local : 2 * local]]) for s in small
        ]
        bup = [s[2 * local :] for s in small]
        lens = lax.dynamic_slice_in_dim(lengths, t * texts, texts)

        x, h1 = join_norm(clock, x_blocks, t, ln1_gain, ln1_bias)
        wq_far = [pp_tensor(clock.after(v), 2) for v in wq_own]
        wu_half = pp_tensor(half(clock.after(w_up)), 2)
        wo_near = pp_tensor(clock.after(w_out), 1)
        wq = [wq_own, wq_near]
        qkv = [project(clock, h1, wq[r], bqkv[r]) for r in (0, 1)]
        qkv[0] = tie(qkv[0], wo_near)
        attn_a = attend_call(clock, lens, qkv[:2], None, length)
        wo_far = pp_tensor(clock.after(w_out), 2)
        wu_near = pp_tensor(clock.after(w_up), 1)
        wd_near = pp_tensor(clock.after(w_down), 1)
        wq_far = [clock.after(v) for v in wq_far]
        wq += [wq_far, [pp_tensor(v, 1) for v in wq_far]]
        qkv += [project(clock, h1, wq[r], bqkv[r]) for r in (2, 3)]
        qkv[2] = tie(qkv[2], wu_near, wd_near)
        attn_b = attend_call(clock, lens, qkv[2:], None, length)
        wu_half = clock.after(wu_half)
        wu_other = pp_dp(wu_half, 0)
        cot_blocks = exchange(text_blocks(tie(cotangent, wu_half)))
        wo_far = clock.after(wo_far)
        wo = [w_out, wo_near, wo_far, pp_tensor(wo_far, 1)]
        ctx = [attn_a[0], attn_a[1], attn_b[0], attn_b[1]]
        resid, h2 = attention_out(clock, x, ctx, wo, (b_out, ln2_gain, ln2_bias))
        wu = [[w_up], [wu_near]]
        acts, slopes = [], []
        for r in rels:
            if r == 2:
                g_low, bias_down = join_mask(clock, [cot_blocks[0]] + [clock.after(b) for b in cot_blocks[1:]], t, lens)
                wd_far = pp_tensor(clock.after(w_down), 2)
                wu_far = order_halves(clock, wu_half, clock.after(wu_other), bit_of[0])
                wu += [wu_far, [pp_tensor(v, 1) for v in wu_far]]
            act, slope = up(clock, h2, wu[r], bup[r])
            acts.append(act)
            slopes.append(slope)

        near = from_near([g_low], [[(0, acts[1])], [(0, acts[3])]])
        down = Chain([g_low], [[(0, acts[0])], [(0, acts[2])]], near, [0, 1, "y"] + high)
        wd_far = clock.after(wd_far)
        wd = [w_down, wd_near, wd_far, pp_tensor(wd_far, 1)]
        dups_a, sums_a, dh2 = up_back(clock, g_low, wu[:2], wd[:2], slopes[:2], None, None, None)
        dups_b, sums_b, rest = up_back(clock, g_low, wu[2:], wd[2:], slopes[2:], dh2[0], resid, ln2_gain)
        dres, dres_low, gain_two, shift_two, bias_attn = rest
        dups, bias_up = dups_a + dups_b, sums_a + sums_b
        up_near = from_near([h2], [[(0, dups[1])], [(0, dups[3])]])
        down.step()
        grads_up = Chain([h2], [[(0, dups[0])], [(0, dups[2])]], up_near, ["y", 0, 1] + high)
        back = attend_call(clock, lens, qkv[2:], [dres_low] + wo[2:] + list(attn_b[2:]), length)
        dqkv_far, qkv_sums_far = back[:2], back[2:]
        near = from_near([h1, dres_low], [[(0, dqkv_far[1]), (1, ctx[3])]])
        down.step()
        q_far = Chain([h1, dres_low], [[(0, dqkv_far[0]), (1, ctx[2])]], near, [1, 0])
        back = attend_call(clock, lens, qkv[:2], [dres_low] + wo[:2] + list(attn_a[2:]), length)
        dqkv, qkv_sums = list(back[:2]) + list(dqkv_far), list(back[2:]) + list(qkv_sums_far)
        grads_up.step()
        if high:
            down.step()
        near = from_near([h1, dres_low], [[(0, dqkv[1]), (1, ctx[1])]])
        out_blocks = exchange(down_out(clock, resid, acts, wd, b_down, t, texts))
        q_own = Chain([h1, dres_low], [[(0, dqkv[0]), (1, ctx[0])]], near, [1, 0] + high)
        q_far.step()
        in_blocks, gain_one, shift_one = norm_one_back(clock, x, dres, dqkv, wq, ln1_gain, t, texts)
        in_blocks = exchange(in_blocks)
        layer_out = join_rows(clock, [out_blocks[0]] + [clock.after(b) for b in out_blocks[1:]], t)
        grads_up.step()
        up_full = jnp.zeros((tensor_size, units), F32)
        qv_full = jnp.zeros((tensor_size, 2, local), F32)
        for r in rels:
            up_full = lax.dynamic_update_slice(up_full, bias_up[r], (t ^ r, 0))
            sums = qkv_sums[r].reshape(3, local)
            sums = jnp.concatenate([sums[:1], sums[2:]], 0)
            qv_full = lax.dynamic_update_slice(qv_full, sums[None], (t ^ r, 0, 0))
        vectors = [gain_one, shift_one, gain_two, shift_two, bias_attn, bias_down]
        total = jnp.concatenate([v.reshape(-1) for v in vectors] + [qv_full.reshape(-1), up_full.reshape(-1)])

        def reduced(flip, tensor):
            moved = pp_tensor(total, flip) if tensor else pp_dp(total, flip)
            return clock.then(total + clock.after(moved))

        total = reduced(1, True)
        q_own.step()
        total = reduced(2, True)
        q_far_all = pp_tensor(q_far.last().astype(BF), 2)
        total = reduced(0, False)
        for bit in high:
            if bit != high[0]:
                down.step()
            grads_up.step()
            if bit == high[0]:
                arrived = clock.after(q_far_all).reshape(q_own.keep.shape)
                q_own.keep = (q_own.keep.astype(F32) + arrived.astype(F32)).astype(BF)
            q_own.step()
        total = reduced(1, False)
        grad_input = join_rows(clock, [in_blocks[0]] + [clock.after(b) for b in in_blocks[1:]], t)
        for bit in high:
            total = reduced(bit, False)
        grad_down, grad_up, both = down.last(), grads_up.last(), q_own.last()
        grad_qkv, grad_out = both[:, : 3 * local], both[:, 3 * local :]
        vector = [total[i * D : (i + 1) * D] for i in range(6)]
        rest = total[6 * D :]
        return (
            layer_out,
            grad_input,
            vector[0],
            vector[1],
            jnp.stack([grad_qkv[:, c * local : c * local + local] for c in range(3)]),
            pick(rest[: 2 * D].reshape(tensor_size, 2, local), t, 0),
            grad_out.T,
            vector[4],
            vector[2],
            vector[3],
            grad_up,
            pick(rest[2 * D :].reshape(tensor_size, units), t, 0),
            grad_down.T,
            vector[5],
        )

    return on_device


def solution(mesh):
    return jax.shard_map(
        program(mesh.shape["dp"], mesh.shape["tensor"]),
        mesh=mesh,
        in_specs=(
            P("dp", "tensor", None),
            P("dp"),
            P("dp", "tensor", None),
            P(),
            P(),
            P(None, None, "tensor"),
            P(None, "tensor"),
            P("tensor", None),
            P(),
            P(),
            P(),
            P(None, "tensor"),
            P("tensor"),
            P("tensor", None),
            P(),
        ),
        out_specs=(
            P("dp", "tensor", None),
            P("dp", "tensor", None),
            P(),
            P(),
            P(None, "dp", "tensor"),
            P(None, "tensor"),
            P("tensor", "dp"),
            P(),
            P(),
            P(),
            P("dp", "tensor"),
            P("tensor"),
            P("tensor", "dp"),
            P(),
        ),
        check_vma=False,
    )
```

```python
import functools

import jax
import jax.numpy as jnp
from jax import lax
from jax.experimental import pallas as pl
from jax.experimental.pallas import tpu as pltpu
from jax.sharding import PartitionSpec as P

D = 768
HD = 64
BF = jnp.bfloat16
F32 = jnp.float32
SCALE = HD**-0.5
LOG2E = 1.4426950408889634


def dot(left, right, left_dim, right_dim):
    return lax.dot_general(
        left, right, (((left_dim,), (right_dim,)), ((), ())), preferred_element_type=F32
    )


def norm_stats(values):
    center = values - jnp.mean(values, -1, keepdims=True)
    rstd = lax.rsqrt(jnp.mean(center * center, -1, keepdims=True) + 1e-05)
    return center * rstd, rstd


def norm_back(grad_norm, normal, rstd, gain):
    scaled = grad_norm * gain
    return rstd * (
        scaled
        - jnp.mean(scaled, -1, keepdims=True)
        - normal * jnp.mean(scaled * normal, -1, keepdims=True)
    )


class Clock:
    def __init__(self):
        self.last = None

    def after(self, values):
        return values if self.last is None else tie(values, self.last)

    def then(self, values):
        self.last = jax.tree.leaves(values)[0]
        return values


def tie(value, *waits):
    return lax.optimization_barrier((value,) + waits)[0]


def call(clock, body, out_shape, operands, *, grid=(), in_specs=None, out_specs=None, scalars=(), scratch=(),
         name=None, flops=0, plain=False):
    operands = (clock.after(operands[0]),) + tuple(operands[1:])
    if plain:
        operands = [pltpu.with_memory_space_constraint(v, pltpu.HBM) for v in operands]
    out = pl.pallas_call(
        body,
        out_shape=jax.tree.map(lambda v: pltpu.HBM(v.shape, v.dtype), out_shape),
        grid_spec=pltpu.PrefetchScalarGridSpec(
            num_scalar_prefetch=len(scalars),
            grid=grid,
            in_specs=in_specs,
            out_specs=out_specs,
            scratch_shapes=scratch,
        ),
        compiler_params=pltpu.CompilerParams(vmem_limit_bytes=48 << 20),
        cost_estimate=pl.CostEstimate(flops=flops, bytes_accessed=0, transcendentals=0),
        name=name,
    )(*scalars, *operands)
    return clock.then(out)


def shape_of(dims, dtype=BF):
    return jax.ShapeDtypeStruct(tuple(dims), dtype)


def whole(values):
    return pl.BlockSpec(values.shape, lambda *_: (0,) * len(values.shape))


def side_by_side(clock, w):
    half, width = w.shape[1] // 2, w.shape[2]

    def body(w_ref, *refs):
        for i in range(2):
            for c in range(3):
                refs[i][:, c * width : (c + 1) * width] = w_ref[c, i * half : (i + 1) * half, :]

    out = [shape_of((half, 3 * width))] * 2
    return call(
        clock, body, out, (w,), grid=(1,), in_specs=[whole(w)], out_specs=[whole(v) for v in out],
        name="side_by_side",
    )


def times(left, pieces):
    total, start = None, 0
    for ref in pieces:
        part = dot(left[:, start : start + ref.shape[0]], ref[...], 1, 0)
        start += ref.shape[0]
        total = part if total is None else total + part
    return total


def times_turned(left, pieces):
    parts = [dot(left, ref[...], 1, 1) for ref in pieces]
    return parts[0] if len(parts) == 1 else jnp.concatenate(parts, 1)


def split_refs(refs, counts):
    out = []
    for count in counts:
        out.append(refs[:count])
        refs = refs[count:]
    return out


def row_block(values, steps):
    return pl.BlockSpec((values.shape[0] // steps, values.shape[1]), lambda i, *_: (i, 0))


def project(clock, h, w, bias):
    def body(h_ref, bias_ref, *refs):
        refs[-1][...] = (times(h_ref[...], refs[:-1]) + bias_ref[...]).astype(BF)

    bias = bias.reshape(1, -1)
    out = shape_of((h.shape[0], bias.shape[1]))
    return call(
        clock, body, out, (h, bias, *w), grid=(4,), in_specs=[row_block(h, 4), whole(bias)] + [whole(v) for v in w],
        out_specs=row_block(out, 4), name="project",
    )


def attention_out(clock, x, ctx, w, vectors, cost=0):
    count = len(ctx)

    def body(x_ref, *refs):
        ctx_refs, w_refs, (bias_ref, gain_ref, shift_ref), (out_ref, h_ref) = split_refs(refs, (count, count, 3, 2))
        total = x_ref[...].astype(F32) + bias_ref[...]
        for r in range(count):
            total = total + dot(ctx_refs[r][...], w_refs[r][...], 1, 0)
        out_ref[...] = total
        normal, _ = norm_stats(total)
        h_ref[...] = (normal * gain_ref[...] + shift_ref[...]).astype(BF)

    vectors = [v.reshape(1, -1) for v in vectors]
    out = [shape_of(x.shape, F32), shape_of(x.shape)]
    return call(
        clock, body, out, (x, *ctx, *w, *vectors), grid=(4,),
        in_specs=[row_block(v, 4) for v in (x, *ctx)] + [whole(v) for v in (*w, *vectors)],
        out_specs=[row_block(v, 4) for v in out], name="attention_out", flops=cost, plain=True,
    )


def up(clock, h, w, bias, cost=0):
    def body(h_ref, bias_ref, *refs):
        upper = times(h_ref[...], refs[:-2]) + bias_ref[...]
        below = 0.5 * (1.0 + lax.erf(upper * (0.5**0.5)))
        density = jnp.exp(-0.5 * upper * upper) * 0.3989422804014327
        refs[-2][...] = (upper * below).astype(BF)
        refs[-1][...] = (below + upper * density).astype(BF)

    bias = bias.reshape(1, -1)
    out = [shape_of((h.shape[0], bias.shape[1]))] * 2
    return call(
        clock, body, out, (h, bias, *w), grid=(4,), in_specs=[row_block(h, 4), whole(bias)] + [whole(v) for v in w],
        out_specs=[row_block(v, 4) for v in out], name="up", flops=cost,
    )


def to_owner(refs, at, values, scratch, count):
    text, late = pl.program_id(0) // 2, pl.program_id(0) % 2
    part = values.shape[0] * 2 // count
    scratch[...] = values.astype(BF)
    for r in range(count):
        place = at[0] ^ r

        @pl.when(place // (count // 2) == late)
        def _():
            start = pl.multiple_of((place % (count // 2)) * part, part)
            rows = scratch[pl.ds(start, part), :]
            if r < 2:
                refs[r][pl.ds(text, 1)] = rows[None]
            else:
                refs[2][pl.ds(place % 2, 1), pl.ds(text, 1)] = rows[None, None]


def owner_shapes(texts, count, rows, width):
    block = (texts, rows // texts // count, width)
    return [shape_of(block), shape_of(block), shape_of((2, *block))]


def down_out(clock, resid, acts, w, bias, me, texts):
    count = len(acts)
    sizes = [len(pieces) for pieces in w]
    w = [v for pieces in w for v in pieces]
    steps = texts * 2

    def body(at, resid_ref, *refs):
        act_refs, w_refs, (bias_ref,), outs, (scratch,) = split_refs(refs, (count, len(w), 1, 3, 1))
        w_refs = split_refs(w_refs, sizes)
        total = resid_ref[...] + bias_ref[...]
        for r in range(count):
            total = total + times(act_refs[r], w_refs[r])
        to_owner(outs, at, total, scratch, count)

    bias = bias.reshape(1, -1)
    out = owner_shapes(texts, count, *resid.shape)
    return call(
        clock, body, out, (resid, *acts, *w, bias), grid=(steps,),
        in_specs=[row_block(v, steps) for v in (resid, *acts)] + [whole(v) for v in (*w, bias)],
        out_specs=[whole(v) for v in out], scalars=(me.reshape(1),),
        scratch=[pltpu.VMEM((resid.shape[0] // steps, resid.shape[1]), BF)], name="down_out",
    )


def norm_one_back(clock, x, dres, dqkv, w, gain, me, texts):
    count = len(dqkv)
    steps = texts * 2
    sizes = [len(pieces) for pieces in w]
    flat = [v for pieces in w for v in pieces]

    def body(at, x_ref, dres_ref, *refs):
        grads, w_refs, (gain_ref,), outs, (gain_sum, shift_sum, scratch) = split_refs(
            refs, (count, len(flat), 1, 3, 3)
        )
        w_refs = split_refs(w_refs, sizes)
        total = None
        for r in range(count):
            part = times_turned(grads[r][...], w_refs[r])
            total = part if total is None else total + part
        normal, rstd = norm_stats(x_ref[...].astype(F32))

        @pl.when(pl.program_id(0) == 0)
        def _():
            gain_sum[...] = jnp.zeros_like(gain_sum)
            shift_sum[...] = jnp.zeros_like(shift_sum)

        gain_sum[...] += jnp.sum(total * normal, 0, keepdims=True)
        shift_sum[...] += jnp.sum(total, 0, keepdims=True)
        to_owner(outs, at, dres_ref[...] + norm_back(total, normal, rstd, gain_ref[...]), scratch, count)

    gain = gain.reshape(1, -1)
    out = owner_shapes(texts, count, *x.shape) + [shape_of(gain.shape, F32)] * 2
    out = call(
        clock, body, out, (x, dres, *dqkv, *flat, gain), grid=(steps,),
        in_specs=[row_block(v, steps) for v in (x, dres, *dqkv)] + [whole(v) for v in (*flat, gain)],
        out_specs=[whole(v) for v in out], scalars=(me.reshape(1),),
        scratch=[pltpu.VMEM((x.shape[0] // steps, x.shape[1]), BF)], name="norm_one_back",
    )
    return out[:3], out[3], out[4]


def block_of(refs, at, r, i):
    return refs[r][i] if refs[r].ndim == 3 else refs[r][at[0] % 2, i]


def join_norm(clock, blocks, me, gain, shift):
    texts, part, width = blocks[0].shape
    count = len(blocks)

    def body(at, *refs):
        ins, (gain_ref, shift_ref, x_ref, h_ref) = refs[:count], refs[count:]
        for r in range(count):
            for i in range(texts):
                start = pl.multiple_of(i * count * part + (at[0] ^ r) * part, part)
                low = ins[r][i]
                normal, _ = norm_stats(low.astype(F32))
                x_ref[pl.ds(start, part), :] = low
                h_ref[pl.ds(start, part), :] = (normal * gain_ref[...] + shift_ref[...]).astype(BF)

    out = [shape_of((texts * count * part, width))] * 2
    operands = (*blocks, gain.reshape(1, -1), shift.reshape(1, -1))
    return call(
        clock, body, out, operands, grid=(1,), in_specs=[whole(v) for v in operands], out_specs=[whole(v) for v in out],
        scalars=(me.reshape(1),), name="join_norm",
    )


def join_mask(clock, blocks, me, lens):
    texts, part, width = blocks[0].shape
    count = len(blocks)

    def body(at, n, *refs):
        ins, (g_ref, sum_ref) = refs[:count], refs[count:]
        total = jnp.zeros((1, width), F32)
        for r in range(count):
            for i in range(texts):
                place = (at[0] ^ r) * part
                start = pl.multiple_of(i * count * part + place, part)
                live = lax.broadcasted_iota(jnp.int32, (part, width), 0) + place < n[i]
                values = jnp.where(live, block_of(ins, at, r, i).astype(F32), 0.0)
                total = total + jnp.sum(values, 0, keepdims=True)
                g_ref[pl.ds(start, part), :] = values.astype(BF)
        sum_ref[...] = total

    out = [shape_of((texts * count * part, width)), shape_of((1, width), F32)]
    return call(
        clock, body, out, blocks, grid=(1,), in_specs=[whole(v) for v in blocks], out_specs=[whole(v) for v in out],
        scalars=(me.reshape(1), lens), name="join_mask",
    )


def join_rows(clock, blocks, me, cost=0):
    texts = blocks[0].shape[0]
    count = len(blocks)

    def body(at, *refs):
        for r in range(count):
            for i in range(texts):
                refs[count][pl.ds((at[0] ^ r) * texts + i, 1)] = block_of(refs, at, r, i)[None]

    out = shape_of((texts * count,) + blocks[0].shape[1:])
    return call(
        clock, body, out, blocks, grid=(1,), in_specs=[whole(v) for v in blocks], out_specs=whole(out),
        scalars=(me.reshape(1),), name="join_rows", flops=cost,
    )


def up_back(clock, g, ups, downs, slopes, base, resid, gain):
    rows, width = g.shape
    count = len(ups)
    units = slopes[0].shape[1]
    down_sizes = [len(pieces) for pieces in downs]
    downs = [v for pieces in downs for v in pieces]
    sizes = [len(pieces) for pieces in ups]
    flat = [v for pieces in ups for v in pieces]
    last = base is not None

    def body(g_ref, *refs):
        up_refs, down_refs, slope_refs, more, grad_refs, sum_refs, outs = split_refs(
            refs, (len(flat), len(downs), count, 3 if last else 0, count, count, 5 if last else 1)
        )
        up_refs = split_refs(up_refs, sizes)
        down_refs = split_refs(down_refs, down_sizes)
        grad = g_ref[...]
        total = more[0][...] if last else None

        @pl.when(pl.program_id(0) == 0)
        def _():
            for ref in list(sum_refs) + list(outs[2:]):
                ref[...] = jnp.zeros_like(ref)

        for s in range(count):
            upper = times_turned(grad, down_refs[s]) * slope_refs[s][...].astype(F32)
            sum_refs[s][...] += jnp.sum(upper, 0, keepdims=True)
            low = upper.astype(BF)
            grad_refs[s][...] = low
            part = times_turned(low, up_refs[s])
            total = part if total is None else total + part
        if last:
            normal, rstd = norm_stats(more[1][...])
            outs[2][...] += jnp.sum(total * normal, 0, keepdims=True)
            outs[3][...] += jnp.sum(total, 0, keepdims=True)
            total = grad.astype(F32) + norm_back(total, normal, rstd, more[2][...])
            outs[4][...] += jnp.sum(total, 0, keepdims=True)
            outs[1][...] = total.astype(BF)
        outs[0][...] = total

    sums, vector = shape_of((1, units), F32), shape_of((1, width), F32)
    unit = pl.BlockSpec((rows // 4, units), lambda i: (i, 0))
    operands = (g, *flat, *downs, *slopes)
    in_specs = [row_block(g, 4)] + [whole(v) for v in (*flat, *downs)] + [unit] * count
    outs = [shape_of((rows, width), F32)]
    out_specs = [row_block(g, 4)]
    if last:
        gain = gain.reshape(1, -1)
        operands += (base, resid, gain)
        in_specs += [row_block(g, 4)] * 2 + [whole(gain)]
        outs += [shape_of((rows, width))] + [vector] * 3
        out_specs += [row_block(g, 4)] + [whole(vector)] * 3
    out = call(
        clock, body,
        [shape_of((rows, units))] * count + [sums] * count + outs,
        operands,
        grid=(4,),
        in_specs=in_specs,
        out_specs=[unit] * count + [whole(sums)] * count + out_specs,
        name="up_back",
    )
    return list(out[:count]), list(out[count : 2 * count]), out[2 * count :]


def weight_grads(clock, lefts, slots, near=None, split=None, apart=False, pieces=False, extra=None):
    rows, width = lefts[0].shape
    columns = sum(right.shape[1] for _, right in slots[0])
    count = len(slots)
    half = width // 2
    rights = [right for slot in slots for _, right in slot]

    def body(*refs):
        if split is not None:
            at, refs = refs[0], refs[1:]
        left_refs, refs = refs[: len(lefts)], refs[len(lefts) :]
        right_refs, refs = list(refs[: len(rights)]), refs[len(rights) :]
        if near is not None:
            near_refs, refs = refs[: len(near)], refs[len(near) :]
        if extra is not None:
            extra_ref, refs = refs[0], refs[1:]
        for s, slot in enumerate(slots):
            start = 0
            for which, right in slot:
                product = dot(left_refs[which][...], right_refs.pop(0)[...], 0, 0)
                cols = slice(start, start + right.shape[1])
                start = cols.stop
                for i in range(2):
                    low, high = max(cols.start, i * columns // 2), min(cols.stop, (i + 1) * columns // 2)
                    if low < high:
                        here = slice(low - cols.start, high - cols.start)
                        there = slice(low - i * columns // 2, high - i * columns // 2)
                        value = product[:, here]
                        if near is not None:
                            value = value + near_refs[2 * s + i][:, there].astype(F32)
                        if extra is not None:
                            value = value + extra_ref[s, :, low:high].astype(F32)
                        if pieces:
                            refs[2 * s + i][:, there] = value.astype(BF)
                        elif apart:
                            refs[s][0, :, low:high] = value.astype(BF)
                        elif split is None:
                            refs[0][s, :, low:high] = value.astype(BF)
                        else:
                            refs[2][:, low:high] = value
            if split is not None:
                outer, inner = split[0] // 2, width // split[0] // 2
                for a in range(outer):
                    for ref, bit in ((refs[0], 1 - at[0]), (refs[1], at[0])):
                        place = pl.multiple_of((2 * a + bit) * inner, inner)
                        ref[s, a * inner : (a + 1) * inner, :] = refs[2][pl.ds(place, inner), :].astype(BF)

    left = pl.BlockSpec((rows, half), lambda i, *_: (0, i))
    tall = pl.BlockSpec((count, half, columns), lambda i, *_: (0, i, 0))
    narrow = pl.BlockSpec((half, columns // 2), lambda i, *_: (i, 0))
    short = pl.BlockSpec((count, half // 2, columns), lambda i, *_: (0, i, 0))
    operands = (*lefts, *rights) + (() if near is None else tuple(near)) + (() if extra is None else (extra,))
    if pieces:
        out_shape = [shape_of((width, columns // 2))] * (2 * count)
        out_specs = [narrow] * (2 * count)
    elif apart:
        out_shape = [shape_of((1, width, columns))] * count
        out_specs = [pl.BlockSpec((1, half, columns), lambda i, *_: (0, i, 0))] * count
    elif split is None:
        out_shape, out_specs = shape_of((count, width, columns)), tall
    else:
        out_shape, out_specs = [shape_of((count, half, columns))] * 2, [short] * 2
    return call(
        clock, body,
        out_shape,
        operands,
        grid=(2,),
        in_specs=[left] * len(lefts) + [whole(v) for v in rights] + ([] if near is None else [narrow] * len(near)) + ([] if extra is None else [tall]),
        out_specs=out_specs,
        scalars=() if split is None else (split[1].reshape(1),),
        scratch=[] if split is None else [pltpu.VMEM((half, columns), F32)],
        name="weight_grads",
    )


def add_split(clock, keep, arrived, outer, index):
    columns = keep.shape[-1]
    inner = keep.size // columns // outer // 2

    def body(at, keep_ref, arrived_ref, send_ref, out_ref):
        for ref, bit in ((send_ref, 1 - at[0]), (out_ref, at[0])):
            ref[0] = (keep_ref[0, bit].astype(F32) + arrived_ref[0, bit].astype(F32)).astype(BF)

    tall = pl.BlockSpec((1, 2, inner, columns), lambda i, *_: (i, 0, 0, 0))
    short = pl.BlockSpec((1, inner, columns), lambda i, *_: (i, 0, 0))
    return call(
        clock, body,
        [shape_of((outer, inner, columns))] * 2,
        (keep.reshape(outer, 2, inner, columns), arrived.reshape(outer, 2, inner, columns)),
        grid=(outer,),
        in_specs=[tall] * 2,
        out_specs=[short] * 2,
        scalars=(jnp.asarray(index, jnp.int32).reshape(1),),
        name="add_split",
    )


def pack(clock, shared, units, projected, me):
    count = len(units)
    first = len(shared)

    def body(at, *refs):
        shared_refs, unit_refs, q_refs, (out_ref,) = split_refs(refs, (first, count, count, 1))
        out_ref[...] = jnp.zeros_like(out_ref)
        for i in range(first):
            out_ref[i : i + 1, :] = shared_refs[i][...]
        for r in range(count):
            width = q_refs[r].shape[1] // 3
            row = pl.ds(first + (at[0] ^ r), 1)
            out_ref[row, : unit_refs[r].shape[1]] = unit_refs[r][...]
            row = pl.ds(first + count + (at[0] ^ r), 1)
            out_ref[row, :width] = q_refs[r][:, :width]
            out_ref[row, width : 2 * width] = q_refs[r][:, 2 * width :]

    out = shape_of((first + 2 * count, max(D, units[0].shape[1])), F32)
    operands = (*shared, *units, *projected)
    return call(
        clock, body, out, operands, grid=(1,), in_specs=[whole(v) for v in operands], out_specs=whole(out),
        scalars=(me.reshape(1),), name="pack",
    )


def attend_body(lens, *refs, step, heads):
    ins, outs, (p_ref, inv_ref) = refs[:2], refs[2:4], refs[4:]
    n = lens[pl.program_id(0)]
    length = ins[0].shape[0]
    width = heads * HD

    def rows(live):
        edge = lax.broadcasted_iota(jnp.int32, (step, length), 0) < n - (live - step)
        for which in range(2):
            ref, ctx_ref = ins[which], outs[which]
            for head in range(heads):
                slot = which * heads + head
                cols = slice(head * HD, head * HD + HD)
                keys = ref[:live, width + head * HD : width + head * HD + HD]
                values = ref[:live, 2 * width + head * HD : 2 * width + head * HD + HD]
                scores = dot(keys, ref[:, cols], 1, 1)
                last = jnp.where(edge, scores[live - step :], -1e30)
                if live > step:
                    scores = jnp.concatenate([scores[: live - step], last], 0)
                else:
                    scores = last
                top = jnp.max(scores, 0, keepdims=True)
                power = jnp.exp2((scores - top) * (SCALE * LOG2E))
                inverse = 1.0 / jnp.sum(power, 0, keepdims=True)
                low = power.astype(BF)
                p_ref[0, slot, :live, :] = low
                inv_ref[0, slot : slot + 1, :] = inverse
                mixed = dot(low, values, 0, 0)
                ctx_ref[:, cols] = (mixed * inverse.reshape(length, 1)).astype(BF)

    for live in range(step, length + 1, step):
        pl.when((n > live - step) & (n <= live))(functools.partial(rows, live))


def attend_back_body(lens, *refs, step, heads):
    ins, (grad_ref,), w_refs, (p_ref, inv_ref) = refs[:2], refs[2:3], refs[3:5], refs[5:7]
    outs, sums, do_ref = refs[7:9], refs[9:11], refs[11]
    n = lens[pl.program_id(0)]
    length = ins[0].shape[0]
    width = heads * HD

    def rows(live):
        for which in range(2):
            ref, out_ref = ins[which], outs[which]
            do_ref[:live, :] = dot(grad_ref[:live, :], w_refs[which][...], 1, 1)
            for head in range(heads):
                slot = which * heads + head
                at = [slice(c * width + head * HD, c * width + head * HD + HD) for c in range(3)]
                inverse = inv_ref[0, slot : slot + 1, :live]
                grad = (do_ref[:live, at[0]] * inverse.reshape(live, 1)).astype(BF)
                low = p_ref[0, slot, :live, :live]
                grad_probs = dot(ref[:live, at[2]], grad, 1, 1)
                power = low.astype(F32)
                product = power * grad_probs
                inner = jnp.sum(product, 0, keepdims=True) * inverse
                grad_scores = (product - power * inner).astype(BF)
                out_ref[:live, at[2]] = dot(low, grad, 1, 0).astype(BF)
                out_ref[:live, at[1]] = (dot(grad_scores, ref[:live, at[0]], 1, 0) * SCALE).astype(BF)
                out_ref[:live, at[0]] = (dot(grad_scores, ref[:live, at[1]], 0, 0) * SCALE).astype(BF)
            if live < length:
                out_ref[live:, :] = jnp.zeros((length - live, 3 * width), BF)
            sums[which][...] += jnp.sum(out_ref[:live, :].astype(F32), 0, keepdims=True)

    @pl.when(pl.program_id(0) == 0)
    def _():
        for ref in sums:
            ref[...] = jnp.zeros_like(ref)

    for live in range(step, length + 1, step):
        pl.when((n > live - step) & (n <= live))(functools.partial(rows, live))


def attend_call(clock, lens, qkv, back, length, cost=0):
    texts = lens.shape[0]
    width = qkv[0].shape[1] // 3
    heads = width // HD
    wide = pl.BlockSpec((length, 3 * width), lambda i, *_: (i, 0))
    slim = pl.BlockSpec((length, width), lambda i, *_: (i, 0))
    full = pl.BlockSpec((length, D), lambda i, *_: (i, 0))
    probs = pl.BlockSpec((1, 2 * heads, length, length), lambda i, *_: (i, 0, 0, 0))
    inverse = pl.BlockSpec((1, 2 * heads, length), lambda i, *_: (i, 0, 0))
    rows = texts * length
    if back is None:
        return call(
            clock,
            functools.partial(attend_body, step=length // 4, heads=heads),
            [shape_of((rows, width))] * 2
            + [shape_of((texts, 2 * heads, length, length)), shape_of((texts, 2 * heads, length), F32)],
            tuple(qkv),
            grid=(texts,),
            in_specs=[wide] * 2,
            out_specs=[slim] * 2 + [probs, inverse],
            scalars=(lens,),
            name="attend",
            flops=cost,
        )
    return call(
        clock,
        functools.partial(attend_back_body, step=length // 4, heads=heads),
        [shape_of((rows, 3 * width))] * 2 + [shape_of((1, 3 * width), F32)] * 2,
        tuple(qkv) + tuple(back),
        grid=(texts,),
        in_specs=[wide] * 2 + [full] + [whole(w) for w in back[1:3]] + [probs, inverse],
        out_specs=[wide] * 2 + [pl.BlockSpec((1, 3 * width), lambda i, *_: (0, 0))] * 2,
        scalars=(lens,),
        scratch=[pltpu.VMEM((length, width), F32)],
        name="attend_back",
    )


COST_FAR, COST_OUT, COST_END = 14 * 10**9, 6 * 10**9, 2 * 10**9


def program(dp_size, tensor_size):
    bits = dp_size.bit_length() - 1

    def pp_tensor(values, flip):
        return lax.ppermute(values, "tensor", [(i, i ^ flip) for i in range(tensor_size)])

    def pp_dp(values, bit):
        return lax.ppermute(values, "dp", [(i, i ^ (1 << bit)) for i in range(dp_size)])

    def on_device(
        inputs,
        lengths,
        cotangent,
        ln1_gain,
        ln1_bias,
        w_qkv,
        b_qv,
        w_out,
        b_out,
        ln2_gain,
        ln2_bias,
        w_up,
        b_up,
        w_down,
        b_down,
    ):
        t = lax.axis_index("tensor")
        d = lax.axis_index("dp")
        texts_all, part = inputs.shape[:2]
        texts = texts_all // tensor_size
        length = part * tensor_size
        rows = texts * length
        rels = range(tensor_size)
        local = w_qkv.shape[2]
        units = b_up.shape[0]
        inner = D // dp_size
        bit_of = [(d >> b) & 1 for b in range(bits)]
        clock = Clock()
        chains = []

        def pick(values, index, axis):
            return lax.dynamic_index_in_dim(values, index, axis, keepdims=False)

        def text_blocks(values):
            return [
                lax.dynamic_slice(values, ((t ^ r) * texts, 0, 0), (texts, part, D)) for r in rels
            ]

        def exchange(blocks):
            far = {r: pp_tensor(blocks[r], r) for r in (3, 2, 1)}
            return [blocks[0]] + [far[r] for r in (1, 2, 3)]

        class Exchange:
            def __init__(self, own, near, far):
                self.own, self.near, self.far = own, near, pp_tensor(far, 2)

            def forward(self):
                self.far = clock.after(self.far)
                self.near = pp_tensor(clock.after(self.near), 1)
                self.last = pp_tensor(pick(self.far, 1 - t % 2, 0), 1)

            def blocks(self):
                return [self.own, clock.after(self.near), self.far, clock.after(self.last)]

        class Chain:
            def __init__(self, lefts, slots, near, steps, extra=None):
                self.steps = list(steps)
                self.dims = [len(slots)] + [2] * bits
                step = self.steps.pop(0)
                outer, index = self.place(step)
                if step == "y":
                    self.keep, self.sent = weight_grads(clock, lefts, slots, near, apart=True)
                elif inner % 16 == 0 and outer > len(slots):
                    split = (outer // len(slots), index)
                    self.sent, self.keep = weight_grads(clock, lefts, slots, near, split, extra=extra)
                else:
                    total = weight_grads(clock, lefts, slots, near, extra=extra)
                    self.sent, self.keep = self.halves(total, outer, index)
                self.fly(step)

            def place(self, step):
                axis = 0 if step == "y" else bits - step
                outer = 1
                for size in self.dims[:axis]:
                    outer *= size
                self.dims[axis] = 1
                return outer, 0 * t if step == "y" else bit_of[step]

            def halves(self, total, outer, index):
                view = total.reshape(outer, 2, -1, total.shape[-1])
                return pick(view, 1 - index, 1), pick(view, index, 1)

            def fly(self, step):
                self.flight = pp_tensor(self.sent, 2) if step == "y" else pp_dp(self.sent, step)

            def step(self):
                arrived = clock.after(self.flight)
                step = self.steps.pop(0)
                outer, index = self.place(step)
                if inner % 16 == 0:
                    self.sent, self.keep = add_split(clock, self.keep, arrived, outer, index)
                else:
                    total = (self.keep.astype(F32) + arrived.astype(F32)).astype(BF)
                    self.sent, self.keep = self.halves(total, outer, index)
                self.fly(step)

            def last(self):
                total = self.keep.astype(F32) + clock.after(self.flight).astype(F32)
                return total.reshape(-1, total.shape[-1])

        high = list(range(2, bits))

        always = (lengths[0] | 1) != 0

        def block(steps, *operands):
            operands = (clock.after(operands[0]),) + operands[1:]

            def run(*values):
                clock.last = None
                return steps(*values)

            saved = [(list(chain.steps), list(chain.dims)) for chain in chains]
            shapes = jax.eval_shape(lambda *v: run(*v), *operands)
            for chain, (left, dims) in zip(chains, saved):
                chain.steps, chain.dims = left, dims
            out = lax.cond(
                always, run, lambda *_: jax.tree.map(lambda v: jnp.zeros(v.shape, v.dtype), shapes), *operands
            )
            clock.last = None
            return clock.then(out)

        def from_near(lefts, slots):
            return [pp_tensor(v, 1) for v in weight_grads(clock, lefts, slots, pieces=True)]

        x_own = text_blocks(inputs)
        x_blocks = exchange(x_own)
        wq_own = side_by_side(clock, tie(w_qkv, *x_own[1:]))
        wq_near = [pp_tensor(v, 1) for v in wq_own]
        wo_near = pp_tensor(tie(w_out, x_blocks[1]), 1)
        small = jnp.concatenate([b_qv.reshape(-1), tie(b_up, x_blocks[1])])
        small = jnp.stack([small, pp_tensor(small, 1)])
        small = list(small) + list(pp_tensor(small, 2))
        bqkv = [
            jnp.concatenate([s[:local], jnp.zeros((local,), F32), s[local : 2 * local]]) for s in small
        ]
        bup = [s[2 * local :] for s in small]
        lens = lax.dynamic_slice_in_dim(lengths, t * texts, texts)


        x_blocks[0] = tie(x_blocks[0], wo_near, *wq_near)
        wq_far = [pp_tensor(tie(v, x_blocks[3]), 2) for v in wq_own]
        cut = w_up.shape[0] // 2
        up_first, up_second = jnp.concatenate([w_up[:cut], w_out], 0), w_up[cut:]
        first_far, second_far = [pp_tensor(tie(v, x_blocks[3]), 2) for v in (up_first, up_second)]
        cot_far = lax.dynamic_slice_in_dim(cotangent, (t // 2 ^ 1) * 2 * texts, 2 * texts)
        cot_own = text_blocks(cotangent)
        cot = Exchange(cot_own[0], cot_own[1], tie(cot_far, x_blocks[3]).reshape(2, texts, part, D))
        wd_far = pp_tensor(tie(w_down, x_blocks[3]), 2)
        x, h1 = join_norm(clock, x_blocks, t, ln1_gain, ln1_bias)
        wq = [wq_own, wq_near]
        qkv = [project(clock, h1, wq[r], bqkv[r]) for r in (0, 1)]
        attn_a = attend_call(clock, lens, qkv[:2], None, length)
        wq_far = [clock.after(v) for v in wq_far]

        def project_far(values):
            passed = [pp_tensor(v, 1) for v in wq_far]
            return passed, project(clock, values, wq_far, bqkv[2])

        passed, q_first = block(project_far, h1)
        wq += [wq_far, passed]
        qkv += [q_first, project(clock, h1, wq[3], bqkv[3])]
        attn_b = attend_call(clock, lens, qkv[2:], None, length, COST_FAR)
        wu_near = [pp_tensor(clock.after(v), 1) for v in (w_up[:cut], up_second)]
        first_far = clock.after(first_far)
        wo_far = first_far[cut:]
        wo = [w_out, wo_near, wo_far, pp_tensor(wo_far, 1)]
        ctx = [attn_a[0], attn_a[1], attn_b[0], attn_b[1]]
        resid, h2 = attention_out(clock, x, ctx, wo, (b_out, ln2_gain, ln2_bias), COST_OUT)
        ups = [up(clock, h2, [w_up], bup[0])]
        wu_far = [first_far[:cut], clock.after(second_far)]
        wu = [[w_up], wu_near, wu_far, [pp_tensor(v, 1) for v in wu_far]]
        ups.append(up(clock, h2, wu[1], bup[1], COST_OUT))
        cot.forward()
        ups.append(up(clock, h2, wu[3], bup[3]))
        g_low, bias_down = join_mask(clock, cot.blocks(), t, lens)
        wd_near = [pp_tensor(clock.after(v), 1) for v in (w_down[:cut], w_down[cut:])]

        near = from_near([tie(g_low, *wd_near)], [[(0, ups[1][0])], [(0, ups[2][0])]])
        ups.insert(2, up(clock, h2, wu[2], bup[2]))
        acts, slopes = [u[0] for u in ups], [u[1] for u in ups]
        down = Chain([g_low], [[(0, acts[0])], [(0, acts[2])]], near, ["y", 0, 1] + high)
        wd_far = clock.after(wd_far)
        wd = [[w_down], wd_near, [wd_far], [pp_tensor(wd_far, 1)]]
        dups_a, sums_a, dh2 = up_back(clock, g_low, wu[:2], wd[:2], slopes[:2], None, None, None)
        dups_b, sums_b, rest = up_back(clock, g_low, wu[2:], wd[2:], slopes[2:], dh2[0], resid, ln2_gain)
        dres, dres_low, gain_two, shift_two, bias_attn = rest
        dups, bias_up = dups_a + dups_b, sums_a + sums_b
        up_near = from_near([h2], [[(0, dups[1])], [(0, dups[3])]])
        down.step()
        grads_up = Chain([h2], [[(0, dups[0])], [(0, dups[2])]], up_near, ["y", 0, 1] + high)
        back = attend_call(clock, lens, qkv[2:], [dres_low] + wo[2:] + list(attn_b[2:]), length)
        dqkv_far, qkv_sums_far = back[:2], back[2:]
        near = from_near([h1, dres_low], [[(0, dqkv_far[1]), (1, ctx[3])]])
        down.step()
        q_far = weight_grads(clock, [h1, dres_low], [[(0, dqkv_far[0]), (1, ctx[2])]], near)
        q_far = pp_tensor(q_far, 2)
        back = attend_call(clock, lens, qkv[:2], [dres_low] + wo[:2] + list(attn_a[2:]), length)
        dqkv, qkv_sums = list(back[:2]) + list(dqkv_far), list(back[2:]) + list(qkv_sums_far)
        grads_up.step()
        for bit in high:
            down.step()
        near = from_near([h1, dres_low], [[(0, dqkv[1]), (1, ctx[1])]])
        out = Exchange(*down_out(clock, resid, acts, wd, b_down, t, texts))
        grad_down = clock.then(down.last())
        grads_up.step()
        q_own = Chain([h1, dres_low], [[(0, dqkv[0]), (1, ctx[0])]], near, [1, 0] + high, clock.after(q_far))
        in_blocks, gain_one, shift_one = norm_one_back(clock, x, dres, dqkv, wq, ln1_gain, t, texts)
        gin = Exchange(*in_blocks)
        shared = [gain_one, shift_one, gain_two, shift_two, bias_attn, bias_down]
        out.forward()
        total = pack(clock, shared, bias_up, qkv_sums, t)
        chains += [grads_up, q_own]
        for chain in chains:
            chain.flight = clock.after(chain.flight)

        def finish(total, state):
            for chain, (keep, flight) in zip(chains, state):
                chain.keep, chain.flight = keep, flight

            def reduced(flip, tensor):
                moved = pp_tensor(total, flip) if tensor else pp_dp(total, flip)
                return clock.then(total + clock.after(moved))

            q_own.step()
            total = reduced(1, True)
            total = reduced(0, False)
            for bit in high:
                q_own.step()
                grads_up.step()
            for bit in range(1, bits):
                total = reduced(bit, False)
            total = reduced(2, True)
            both = q_own.last()
            weights = jnp.stack([both[:, c * local : c * local + local] for c in range(3)])
            return total, grads_up.last(), weights, both[:, 3 * local :].T

        state = [(chain.keep, chain.flight) for chain in chains]
        total, grad_up, grad_qkv, grad_out = block(finish, total, state)
        layer_out = join_rows(clock, out.blocks(), t, COST_END)
        gin.forward()
        grad_input = join_rows(clock, gin.blocks(), t)
        first = len(shared)
        units_sum = lax.dynamic_slice_in_dim(total, first + t, 1)[0, :units]
        qv_sum = lax.dynamic_slice_in_dim(total, first + tensor_size + t, 1)[0, : 2 * local]
        return (
            layer_out,
            grad_input,
            total[0],
            total[1],
            grad_qkv,
            qv_sum.reshape(2, local),
            grad_out,
            total[4],
            total[2],
            total[3],
            grad_up,
            units_sum,
            grad_down.T,
            total[5],
        )

    return on_device


def solution(mesh):
    return jax.shard_map(
        program(mesh.shape["dp"], mesh.shape["tensor"]),
        mesh=mesh,
        in_specs=(
            P("dp", "tensor", None),
            P("dp"),
            P("dp", "tensor", None),
            P(),
            P(),
            P(None, None, "tensor"),
            P(None, "tensor"),
            P("tensor", None),
            P(),
            P(),
            P(),
            P(None, "tensor"),
            P("tensor"),
            P("tensor", None),
            P(),
        ),
        out_specs=(
            P("dp", "tensor", None),
            P("dp", "tensor", None),
            P(),
            P(),
            P(None, "dp", "tensor"),
            P(None, "tensor"),
            P("tensor", "dp"),
            P(),
            P(),
            P(),
            P("dp", "tensor"),
            P("tensor"),
            P("tensor", "dp"),
            P(),
        ),
        check_vma=False,
    )
```

```python
import functools

import jax
import jax.numpy as jnp
from jax import lax
from jax.experimental import pallas as pl
from jax.experimental.pallas import tpu as pltpu
from jax.sharding import PartitionSpec as P

D = 768
HD = 64
BF = jnp.bfloat16
F32 = jnp.float32
SCALE = HD**-0.5
LOG2E = 1.4426950408889634


def dot(left, right, left_dim, right_dim):
    return lax.dot_general(
        left, right, (((left_dim,), (right_dim,)), ((), ())), preferred_element_type=F32
    )


def norm_stats(values):
    center = values - jnp.mean(values, -1, keepdims=True)
    rstd = lax.rsqrt(jnp.mean(center * center, -1, keepdims=True) + 1e-05)
    return center * rstd, rstd


def norm_back(grad_norm, normal, rstd, gain):
    scaled = grad_norm * gain
    return rstd * (
        scaled
        - jnp.mean(scaled, -1, keepdims=True)
        - normal * jnp.mean(scaled * normal, -1, keepdims=True)
    )


class Clock:
    def __init__(self):
        self.last = None

    def after(self, values):
        return values if self.last is None else tie(values, self.last)

    def then(self, values):
        self.last = jax.tree.leaves(values)[0]
        return values


def tie(value, *waits):
    return lax.optimization_barrier((value,) + waits)[0]


def call(clock, body, out_shape, operands, *, grid=(), in_specs=None, out_specs=None, scalars=(), scratch=(),
         name=None, flops=0, plain=False):
    operands = (clock.after(operands[0]),) + tuple(operands[1:])
    if plain:
        operands = [pltpu.with_memory_space_constraint(v, pltpu.HBM) for v in operands]
    out = pl.pallas_call(
        body,
        out_shape=jax.tree.map(lambda v: pltpu.HBM(v.shape, v.dtype), out_shape) if name in ("up", "attend", "up_back") else out_shape,
        grid_spec=pltpu.PrefetchScalarGridSpec(
            num_scalar_prefetch=len(scalars),
            grid=grid,
            in_specs=in_specs,
            out_specs=out_specs,
            scratch_shapes=scratch,
        ),
        compiler_params=pltpu.CompilerParams(vmem_limit_bytes=48 << 20),
        cost_estimate=pl.CostEstimate(flops=flops, bytes_accessed=0, transcendentals=0),
        name=name,
    )(*scalars, *operands)
    return clock.then(out)


def shape_of(dims, dtype=BF):
    return jax.ShapeDtypeStruct(tuple(dims), dtype)


def whole(values):
    return pl.BlockSpec(values.shape, lambda *_: (0,) * len(values.shape))


def side_by_side(clock, w):
    half, width = w.shape[1] // 2, w.shape[2]

    def body(w_ref, *refs):
        for i in range(2):
            for c in range(3):
                refs[i][:, c * width : (c + 1) * width] = w_ref[c, i * half : (i + 1) * half, :]

    out = [shape_of((half, 3 * width))] * 2
    return call(
        clock, body, out, (w,), grid=(1,), in_specs=[whole(w)], out_specs=[whole(v) for v in out],
        name="side_by_side",
    )


def times(left, pieces):
    total, start = None, 0
    for ref in pieces:
        part = dot(left[:, start : start + ref.shape[0]], ref[...], 1, 0)
        start += ref.shape[0]
        total = part if total is None else total + part
    return total


def times_turned(left, pieces):
    parts = [dot(left, ref[...], 1, 1) for ref in pieces]
    return parts[0] if len(parts) == 1 else jnp.concatenate(parts, 1)


def split_refs(refs, counts):
    out = []
    for count in counts:
        out.append(refs[:count])
        refs = refs[count:]
    return out


def row_block(values, steps):
    return pl.BlockSpec((values.shape[0] // steps, values.shape[1]), lambda i, *_: (i, 0))


def project(clock, h, w, bias):
    def body(h_ref, bias_ref, *refs):
        refs[-1][...] = (times(h_ref[...], refs[:-1]) + bias_ref[...]).astype(BF)

    bias = bias.reshape(1, -1)
    out = shape_of((h.shape[0], bias.shape[1]))
    return call(
        clock, body, out, (h, bias, *w), grid=(4,), in_specs=[row_block(h, 4), whole(bias)] + [whole(v) for v in w],
        out_specs=row_block(out, 4), name="project",
    )


def attention_out(clock, x, ctx, w, vectors, cost=0):
    count = len(ctx)

    def body(x_ref, *refs):
        ctx_refs, w_refs, (bias_ref, gain_ref, shift_ref), (out_ref, h_ref) = split_refs(refs, (count, count, 3, 2))
        total = x_ref[...].astype(F32) + bias_ref[...]
        for r in range(count):
            total = total + dot(ctx_refs[r][...], w_refs[r][...], 1, 0)
        out_ref[...] = total
        normal, _ = norm_stats(total)
        h_ref[...] = (normal * gain_ref[...] + shift_ref[...]).astype(BF)

    vectors = [v.reshape(1, -1) for v in vectors]
    out = [shape_of(x.shape, F32), shape_of(x.shape)]
    return call(
        clock, body, out, (x, *ctx, *w, *vectors), grid=(4,),
        in_specs=[row_block(v, 4) for v in (x, *ctx)] + [whole(v) for v in (*w, *vectors)],
        out_specs=[row_block(v, 4) for v in out], name="attention_out", flops=cost, plain=True,
    )


def up(clock, h, w, bias, cost=0):
    def body(h_ref, bias_ref, *refs):
        upper = times(h_ref[...], refs[:-2]) + bias_ref[...]
        below = 0.5 * (1.0 + lax.erf(upper * (0.5**0.5)))
        density = jnp.exp(-0.5 * upper * upper) * 0.3989422804014327
        refs[-2][...] = (upper * below).astype(BF)
        refs[-1][...] = (below + upper * density).astype(BF)

    bias = bias.reshape(1, -1)
    out = [shape_of((h.shape[0], bias.shape[1]))] * 2
    return call(
        clock, body, out, (h, bias, *w), grid=(4,), in_specs=[row_block(h, 4), whole(bias)] + [whole(v) for v in w],
        out_specs=[row_block(v, 4) for v in out], name="up", flops=cost,
    )


def to_owner(refs, at, values, scratch, count):
    text, late = pl.program_id(0) // 2, pl.program_id(0) % 2
    part = values.shape[0] * 2 // count
    scratch[...] = values.astype(BF)
    for r in range(count):
        place = at[0] ^ r

        @pl.when(place // (count // 2) == late)
        def _():
            start = pl.multiple_of((place % (count // 2)) * part, part)
            rows = scratch[pl.ds(start, part), :]
            if r < 2:
                refs[r][pl.ds(text, 1)] = rows[None]
            else:
                refs[2][pl.ds(place % 2, 1), pl.ds(text, 1)] = rows[None, None]


def owner_shapes(texts, count, rows, width):
    block = (texts, rows // texts // count, width)
    return [shape_of(block), shape_of(block), shape_of((2, *block))]


def down_out(clock, resid, acts, w, bias, me, texts):
    count = len(acts)
    sizes = [len(pieces) for pieces in w]
    w = [v for pieces in w for v in pieces]
    steps = texts * 2

    def body(at, resid_ref, *refs):
        act_refs, w_refs, (bias_ref,), outs, (scratch,) = split_refs(refs, (count, len(w), 1, 3, 1))
        w_refs = split_refs(w_refs, sizes)
        total = resid_ref[...] + bias_ref[...]
        for r in range(count):
            total = total + times(act_refs[r], w_refs[r])
        to_owner(outs, at, total, scratch, count)

    bias = bias.reshape(1, -1)
    out = owner_shapes(texts, count, *resid.shape)
    return call(
        clock, body, out, (resid, *acts, *w, bias), grid=(steps,),
        in_specs=[row_block(v, steps) for v in (resid, *acts)] + [whole(v) for v in (*w, bias)],
        out_specs=[whole(v) for v in out], scalars=(me.reshape(1),),
        scratch=[pltpu.VMEM((resid.shape[0] // steps, resid.shape[1]), BF)], name="down_out",
    )


def norm_one_back(clock, x, dres, dqkv, w, gain, me, texts):
    count = len(dqkv)
    steps = texts * 2
    sizes = [len(pieces) for pieces in w]
    flat = [v for pieces in w for v in pieces]

    def body(at, x_ref, dres_ref, *refs):
        grads, w_refs, (gain_ref,), outs, (gain_sum, shift_sum, scratch) = split_refs(
            refs, (count, len(flat), 1, 3, 3)
        )
        w_refs = split_refs(w_refs, sizes)
        total = None
        for r in range(count):
            part = times_turned(grads[r][...], w_refs[r])
            total = part if total is None else total + part
        normal, rstd = norm_stats(x_ref[...].astype(F32))

        @pl.when(pl.program_id(0) == 0)
        def _():
            gain_sum[...] = jnp.zeros_like(gain_sum)
            shift_sum[...] = jnp.zeros_like(shift_sum)

        gain_sum[...] += jnp.sum(total * normal, 0, keepdims=True)
        shift_sum[...] += jnp.sum(total, 0, keepdims=True)
        to_owner(outs, at, dres_ref[...] + norm_back(total, normal, rstd, gain_ref[...]), scratch, count)

    gain = gain.reshape(1, -1)
    out = owner_shapes(texts, count, *x.shape) + [shape_of(gain.shape, F32)] * 2
    out = call(
        clock, body, out, (x, dres, *dqkv, *flat, gain), grid=(steps,),
        in_specs=[row_block(v, steps) for v in (x, dres, *dqkv)] + [whole(v) for v in (*flat, gain)],
        out_specs=[whole(v) for v in out], scalars=(me.reshape(1),),
        scratch=[pltpu.VMEM((x.shape[0] // steps, x.shape[1]), BF)], name="norm_one_back",
    )
    return out[:3], out[3], out[4]


def block_of(refs, at, r, i):
    return refs[r][i] if refs[r].ndim == 3 else refs[r][at[0] % 2, i]


def join_norm(clock, blocks, me, gain, shift):
    texts, part, width = blocks[0].shape
    count = len(blocks)

    def body(at, *refs):
        ins, (gain_ref, shift_ref, x_ref, h_ref) = refs[:count], refs[count:]
        for r in range(count):
            for i in range(texts):
                start = pl.multiple_of(i * count * part + (at[0] ^ r) * part, part)
                low = ins[r][i]
                normal, _ = norm_stats(low.astype(F32))
                x_ref[pl.ds(start, part), :] = low
                h_ref[pl.ds(start, part), :] = (normal * gain_ref[...] + shift_ref[...]).astype(BF)

    out = [shape_of((texts * count * part, width))] * 2
    operands = (*blocks, gain.reshape(1, -1), shift.reshape(1, -1))
    return call(
        clock, body, out, operands, grid=(1,), in_specs=[whole(v) for v in operands], out_specs=[whole(v) for v in out],
        scalars=(me.reshape(1),), name="join_norm",
    )


def join_mask(clock, blocks, me, lens):
    texts, part, width = blocks[0].shape
    count = len(blocks)

    def body(at, n, *refs):
        ins, (g_ref, sum_ref) = refs[:count], refs[count:]
        total = jnp.zeros((1, width), F32)
        for r in range(count):
            for i in range(texts):
                place = (at[0] ^ r) * part
                start = pl.multiple_of(i * count * part + place, part)
                live = lax.broadcasted_iota(jnp.int32, (part, width), 0) + place < n[i]
                values = jnp.where(live, block_of(ins, at, r, i).astype(F32), 0.0)
                total = total + jnp.sum(values, 0, keepdims=True)
                g_ref[pl.ds(start, part), :] = values.astype(BF)
        sum_ref[...] = total

    out = [shape_of((texts * count * part, width)), shape_of((1, width), F32)]
    return call(
        clock, body, out, blocks, grid=(1,), in_specs=[whole(v) for v in blocks], out_specs=[whole(v) for v in out],
        scalars=(me.reshape(1), lens), name="join_mask",
    )


def join_rows(clock, blocks, me, cost=0):
    texts = blocks[0].shape[0]
    count = len(blocks)

    def body(at, *refs):
        for r in range(count):
            for i in range(texts):
                refs[count][pl.ds((at[0] ^ r) * texts + i, 1)] = block_of(refs, at, r, i)[None]

    out = shape_of((texts * count,) + blocks[0].shape[1:])
    return call(
        clock, body, out, blocks, grid=(1,), in_specs=[whole(v) for v in blocks], out_specs=whole(out),
        scalars=(me.reshape(1),), name="join_rows", flops=cost,
    )


def up_back(clock, g, ups, downs, slopes, base, resid, gain):
    rows, width = g.shape
    count = len(ups)
    units = slopes[0].shape[1]
    down_sizes = [len(pieces) for pieces in downs]
    downs = [v for pieces in downs for v in pieces]
    sizes = [len(pieces) for pieces in ups]
    flat = [v for pieces in ups for v in pieces]
    last = base is not None

    def body(g_ref, *refs):
        up_refs, down_refs, slope_refs, more, grad_refs, sum_refs, outs = split_refs(
            refs, (len(flat), len(downs), count, 3 if last else 0, count, count, 5 if last else 1)
        )
        up_refs = split_refs(up_refs, sizes)
        down_refs = split_refs(down_refs, down_sizes)
        grad = g_ref[...]
        total = more[0][...] if last else None

        @pl.when(pl.program_id(0) == 0)
        def _():
            for ref in list(sum_refs) + list(outs[2:]):
                ref[...] = jnp.zeros_like(ref)

        for s in range(count):
            upper = times_turned(grad, down_refs[s]) * slope_refs[s][...].astype(F32)
            sum_refs[s][...] += jnp.sum(upper, 0, keepdims=True)
            low = upper.astype(BF)
            grad_refs[s][...] = low
            part = times_turned(low, up_refs[s])
            total = part if total is None else total + part
        if last:
            normal, rstd = norm_stats(more[1][...])
            outs[2][...] += jnp.sum(total * normal, 0, keepdims=True)
            outs[3][...] += jnp.sum(total, 0, keepdims=True)
            total = grad.astype(F32) + norm_back(total, normal, rstd, more[2][...])
            outs[4][...] += jnp.sum(total, 0, keepdims=True)
            outs[1][...] = total.astype(BF)
        outs[0][...] = total

    sums, vector = shape_of((1, units), F32), shape_of((1, width), F32)
    unit = pl.BlockSpec((rows // 4, units), lambda i: (i, 0))
    operands = (g, *flat, *downs, *slopes)
    in_specs = [row_block(g, 4)] + [whole(v) for v in (*flat, *downs)] + [unit] * count
    outs = [shape_of((rows, width), F32)]
    out_specs = [row_block(g, 4)]
    if last:
        gain = gain.reshape(1, -1)
        operands += (base, resid, gain)
        in_specs += [row_block(g, 4)] * 2 + [whole(gain)]
        outs += [shape_of((rows, width))] + [vector] * 3
        out_specs += [row_block(g, 4)] + [whole(vector)] * 3
    out = call(
        clock, body,
        [shape_of((rows, units))] * count + [sums] * count + outs,
        operands,
        grid=(4,),
        in_specs=in_specs,
        out_specs=[unit] * count + [whole(sums)] * count + out_specs,
        name="up_back",
    )
    return list(out[:count]), list(out[count : 2 * count]), out[2 * count :]


def weight_grads(clock, lefts, slots, near=None, split=None, apart=False, pieces=False, extra=None):
    rows, width = lefts[0].shape
    columns = sum(right.shape[1] for _, right in slots[0])
    count = len(slots)
    half = width // 2
    rights = [right for slot in slots for _, right in slot]

    def body(*refs):
        if split is not None:
            at, refs = refs[0], refs[1:]
        left_refs, refs = refs[: len(lefts)], refs[len(lefts) :]
        right_refs, refs = list(refs[: len(rights)]), refs[len(rights) :]
        if near is not None:
            near_refs, refs = refs[: len(near)], refs[len(near) :]
        if extra is not None:
            extra_ref, refs = refs[0], refs[1:]
        for s, slot in enumerate(slots):
            start = 0
            for which, right in slot:
                product = dot(left_refs[which][...], right_refs.pop(0)[...], 0, 0)
                cols = slice(start, start + right.shape[1])
                start = cols.stop
                for i in range(2):
                    low, high = max(cols.start, i * columns // 2), min(cols.stop, (i + 1) * columns // 2)
                    if low < high:
                        here = slice(low - cols.start, high - cols.start)
                        there = slice(low - i * columns // 2, high - i * columns // 2)
                        value = product[:, here]
                        if near is not None:
                            value = value + near_refs[2 * s + i][:, there].astype(F32)
                        if extra is not None:
                            value = value + extra_ref[s, :, low:high].astype(F32)
                        if pieces:
                            refs[2 * s + i][:, there] = value.astype(BF)
                        elif apart:
                            refs[s][0, :, low:high] = value.astype(BF)
                        elif split is None:
                            refs[0][s, :, low:high] = value.astype(BF)
                        else:
                            refs[2][:, low:high] = value
            if split is not None:
                outer, inner = split[0] // 2, width // split[0] // 2
                for a in range(outer):
                    for ref, bit in ((refs[0], 1 - at[0]), (refs[1], at[0])):
                        place = pl.multiple_of((2 * a + bit) * inner, inner)
                        ref[s, a * inner : (a + 1) * inner, :] = refs[2][pl.ds(place, inner), :].astype(BF)

    left = pl.BlockSpec((rows, half), lambda i, *_: (0, i))
    tall = pl.BlockSpec((count, half, columns), lambda i, *_: (0, i, 0))
    narrow = pl.BlockSpec((half, columns // 2), lambda i, *_: (i, 0))
    short = pl.BlockSpec((count, half // 2, columns), lambda i, *_: (0, i, 0))
    operands = (*lefts, *rights) + (() if near is None else tuple(near)) + (() if extra is None else (extra,))
    if pieces:
        out_shape = [shape_of((width, columns // 2))] * (2 * count)
        out_specs = [narrow] * (2 * count)
    elif apart:
        out_shape = [shape_of((1, width, columns))] * count
        out_specs = [pl.BlockSpec((1, half, columns), lambda i, *_: (0, i, 0))] * count
    elif split is None:
        out_shape, out_specs = shape_of((count, width, columns)), tall
    else:
        out_shape, out_specs = [shape_of((count, half, columns))] * 2, [short] * 2
    return call(
        clock, body,
        out_shape,
        operands,
        grid=(2,),
        in_specs=[left] * len(lefts) + [whole(v) for v in rights] + ([] if near is None else [narrow] * len(near)) + ([] if extra is None else [tall]),
        out_specs=out_specs,
        scalars=() if split is None else (split[1].reshape(1),),
        scratch=[] if split is None else [pltpu.VMEM((half, columns), F32)],
        name="weight_grads",
    )


def add_split(clock, keep, arrived, outer, index):
    columns = keep.shape[-1]
    inner = keep.size // columns // outer // 2

    def body(at, keep_ref, arrived_ref, send_ref, out_ref):
        for ref, bit in ((send_ref, 1 - at[0]), (out_ref, at[0])):
            ref[0] = (keep_ref[0, bit].astype(F32) + arrived_ref[0, bit].astype(F32)).astype(BF)

    tall = pl.BlockSpec((1, 2, inner, columns), lambda i, *_: (i, 0, 0, 0))
    short = pl.BlockSpec((1, inner, columns), lambda i, *_: (i, 0, 0))
    return call(
        clock, body,
        [shape_of((outer, inner, columns))] * 2,
        (keep.reshape(outer, 2, inner, columns), arrived.reshape(outer, 2, inner, columns)),
        grid=(outer,),
        in_specs=[tall] * 2,
        out_specs=[short] * 2,
        scalars=(jnp.asarray(index, jnp.int32).reshape(1),),
        name="add_split",
    )


def pack(clock, shared, units, projected, me):
    count = len(units)
    first = len(shared)

    def body(at, *refs):
        shared_refs, unit_refs, q_refs, (out_ref,) = split_refs(refs, (first, count, count, 1))
        out_ref[...] = jnp.zeros_like(out_ref)
        for i in range(first):
            out_ref[i : i + 1, :] = shared_refs[i][...]
        for r in range(count):
            width = q_refs[r].shape[1] // 3
            row = pl.ds(first + (at[0] ^ r), 1)
            out_ref[row, : unit_refs[r].shape[1]] = unit_refs[r][...]
            row = pl.ds(first + count + (at[0] ^ r), 1)
            out_ref[row, :width] = q_refs[r][:, :width]
            out_ref[row, width : 2 * width] = q_refs[r][:, 2 * width :]

    out = shape_of((first + 2 * count, max(D, units[0].shape[1])), F32)
    operands = (*shared, *units, *projected)
    return call(
        clock, body, out, operands, grid=(1,), in_specs=[whole(v) for v in operands], out_specs=whole(out),
        scalars=(me.reshape(1),), name="pack",
    )


def attend_body(lens, *refs, step, heads):
    ins, outs, (p_ref, inv_ref) = refs[:2], refs[2:4], refs[4:]
    n = lens[pl.program_id(0)]
    length = ins[0].shape[0]
    width = heads * HD

    def rows(live):
        edge = lax.broadcasted_iota(jnp.int32, (step, length), 0) < n - (live - step)
        for which in range(2):
            ref, ctx_ref = ins[which], outs[which]
            for head in range(heads):
                slot = which * heads + head
                cols = slice(head * HD, head * HD + HD)
                keys = ref[:live, width + head * HD : width + head * HD + HD]
                values = ref[:live, 2 * width + head * HD : 2 * width + head * HD + HD]
                scores = dot(keys, ref[:, cols], 1, 1)
                last = jnp.where(edge, scores[live - step :], -1e30)
                if live > step:
                    scores = jnp.concatenate([scores[: live - step], last], 0)
                else:
                    scores = last
                top = jnp.max(scores, 0, keepdims=True)
                power = jnp.exp2((scores - top) * (SCALE * LOG2E))
                inverse = 1.0 / jnp.sum(power, 0, keepdims=True)
                low = power.astype(BF)
                p_ref[0, slot, :live, :] = low
                inv_ref[0, slot : slot + 1, :] = inverse
                mixed = dot(low, values, 0, 0)
                ctx_ref[:, cols] = (mixed * inverse.reshape(length, 1)).astype(BF)

    for live in range(step, length + 1, step):
        pl.when((n > live - step) & (n <= live))(functools.partial(rows, live))


def attend_back_body(lens, *refs, step, heads):
    ins, (grad_ref,), w_refs, (p_ref, inv_ref) = refs[:2], refs[2:3], refs[3:5], refs[5:7]
    outs, sums, do_ref = refs[7:9], refs[9:11], refs[11]
    n = lens[pl.program_id(0)]
    length = ins[0].shape[0]
    width = heads * HD

    def rows(live):
        for which in range(2):
            ref, out_ref = ins[which], outs[which]
            do_ref[:live, :] = dot(grad_ref[:live, :], w_refs[which][...], 1, 1)
            for head in range(heads):
                slot = which * heads + head
                at = [slice(c * width + head * HD, c * width + head * HD + HD) for c in range(3)]
                inverse = inv_ref[0, slot : slot + 1, :live]
                grad = (do_ref[:live, at[0]] * inverse.reshape(live, 1)).astype(BF)
                low = p_ref[0, slot, :live, :live]
                grad_probs = dot(ref[:live, at[2]], grad, 1, 1)
                power = low.astype(F32)
                product = power * grad_probs
                inner = jnp.sum(product, 0, keepdims=True) * inverse
                grad_scores = (product - power * inner).astype(BF)
                out_ref[:live, at[2]] = dot(low, grad, 1, 0).astype(BF)
                out_ref[:live, at[1]] = (dot(grad_scores, ref[:live, at[0]], 1, 0) * SCALE).astype(BF)
                out_ref[:live, at[0]] = (dot(grad_scores, ref[:live, at[1]], 0, 0) * SCALE).astype(BF)
            if live < length:
                out_ref[live:, :] = jnp.zeros((length - live, 3 * width), BF)
            sums[which][...] += jnp.sum(out_ref[:live, :].astype(F32), 0, keepdims=True)

    @pl.when(pl.program_id(0) == 0)
    def _():
        for ref in sums:
            ref[...] = jnp.zeros_like(ref)

    for live in range(step, length + 1, step):
        pl.when((n > live - step) & (n <= live))(functools.partial(rows, live))


def attend_call(clock, lens, qkv, back, length, cost=0):
    texts = lens.shape[0]
    width = qkv[0].shape[1] // 3
    heads = width // HD
    wide = pl.BlockSpec((length, 3 * width), lambda i, *_: (i, 0))
    slim = pl.BlockSpec((length, width), lambda i, *_: (i, 0))
    full = pl.BlockSpec((length, D), lambda i, *_: (i, 0))
    probs = pl.BlockSpec((1, 2 * heads, length, length), lambda i, *_: (i, 0, 0, 0))
    inverse = pl.BlockSpec((1, 2 * heads, length), lambda i, *_: (i, 0, 0))
    rows = texts * length
    if back is None:
        return call(
            clock,
            functools.partial(attend_body, step=length // 4, heads=heads),
            [shape_of((rows, width))] * 2
            + [shape_of((texts, 2 * heads, length, length)), shape_of((texts, 2 * heads, length), F32)],
            tuple(qkv),
            grid=(texts,),
            in_specs=[wide] * 2,
            out_specs=[slim] * 2 + [probs, inverse],
            scalars=(lens,),
            name="attend",
            flops=cost,
        )
    return call(
        clock,
        functools.partial(attend_back_body, step=length // 4, heads=heads),
        [shape_of((rows, 3 * width))] * 2 + [shape_of((1, 3 * width), F32)] * 2,
        tuple(qkv) + tuple(back),
        grid=(texts,),
        in_specs=[wide] * 2 + [full] + [whole(w) for w in back[1:3]] + [probs, inverse],
        out_specs=[wide] * 2 + [pl.BlockSpec((1, 3 * width), lambda i, *_: (0, 0))] * 2,
        scalars=(lens,),
        scratch=[pltpu.VMEM((length, width), F32)],
        name="attend_back",
    )


COST_FAR, COST_OUT, COST_END = 14 * 10**9, 4 * 10**9, 2 * 10**9


def program(dp_size, tensor_size):
    bits = dp_size.bit_length() - 1

    def pp_tensor(values, flip):
        return lax.ppermute(values, "tensor", [(i, i ^ flip) for i in range(tensor_size)])

    def pp_dp(values, bit):
        return lax.ppermute(values, "dp", [(i, i ^ (1 << bit)) for i in range(dp_size)])

    def on_device(
        inputs,
        lengths,
        cotangent,
        ln1_gain,
        ln1_bias,
        w_qkv,
        b_qv,
        w_out,
        b_out,
        ln2_gain,
        ln2_bias,
        w_up,
        b_up,
        w_down,
        b_down,
    ):
        t = lax.axis_index("tensor")
        d = lax.axis_index("dp")
        texts_all, part = inputs.shape[:2]
        texts = texts_all // tensor_size
        length = part * tensor_size
        rows = texts * length
        rels = range(tensor_size)
        local = w_qkv.shape[2]
        units = b_up.shape[0]
        inner = D // dp_size
        bit_of = [(d >> b) & 1 for b in range(bits)]
        clock = Clock()
        chains = []

        def pick(values, index, axis):
            return lax.dynamic_index_in_dim(values, index, axis, keepdims=False)

        def text_blocks(values):
            return [
                lax.dynamic_slice(values, ((t ^ r) * texts, 0, 0), (texts, part, D)) for r in rels
            ]

        def exchange(blocks):
            far = {r: pp_tensor(blocks[r], r) for r in (3, 2, 1)}
            return [blocks[0]] + [far[r] for r in (1, 2, 3)]

        class Exchange:
            def __init__(self, own, near, far):
                self.own, self.near, self.far = own, near, pp_tensor(far, 2)

            def forward(self):
                self.far = clock.after(self.far)
                self.near = pp_tensor(clock.after(self.near), 1)
                self.last = pp_tensor(pick(self.far, 1 - t % 2, 0), 1)

            def blocks(self):
                return [self.own, clock.after(self.near), self.far, clock.after(self.last)]

        class Chain:
            def __init__(self, lefts, slots, near, steps, extra=None):
                self.steps = list(steps)
                self.dims = [len(slots)] + [2] * bits
                step = self.steps.pop(0)
                outer, index = self.place(step)
                if step == "y":
                    self.keep, self.sent = weight_grads(clock, lefts, slots, near, apart=True)
                elif inner % 16 == 0 and outer > len(slots):
                    split = (outer // len(slots), index)
                    self.sent, self.keep = weight_grads(clock, lefts, slots, near, split, extra=extra)
                else:
                    total = weight_grads(clock, lefts, slots, near, extra=extra)
                    self.sent, self.keep = self.halves(total, outer, index)
                self.fly(step)

            def place(self, step):
                axis = 0 if step == "y" else bits - step
                outer = 1
                for size in self.dims[:axis]:
                    outer *= size
                self.dims[axis] = 1
                return outer, 0 * t if step == "y" else bit_of[step]

            def halves(self, total, outer, index):
                view = total.reshape(outer, 2, -1, total.shape[-1])
                return pick(view, 1 - index, 1), pick(view, index, 1)

            def fly(self, step):
                self.flight = pp_tensor(self.sent, 2) if step == "y" else pp_dp(self.sent, step)

            def step(self):
                arrived = clock.after(self.flight)
                step = self.steps.pop(0)
                outer, index = self.place(step)
                if inner % 16 == 0:
                    self.sent, self.keep = add_split(clock, self.keep, arrived, outer, index)
                else:
                    total = (self.keep.astype(F32) + arrived.astype(F32)).astype(BF)
                    self.sent, self.keep = self.halves(total, outer, index)
                self.fly(step)

            def last(self):
                total = self.keep.astype(F32) + clock.after(self.flight).astype(F32)
                return total.reshape(-1, total.shape[-1])

        high = list(range(2, bits))

        always = (lengths[0] | 1) != 0

        def block(steps, *operands):
            operands = (clock.after(operands[0]),) + operands[1:]

            def run(*values):
                clock.last = None
                return steps(*values)

            saved = [(list(chain.steps), list(chain.dims)) for chain in chains]
            shapes = jax.eval_shape(lambda *v: run(*v), *operands)
            for chain, (left, dims) in zip(chains, saved):
                chain.steps, chain.dims = left, dims
            out = lax.cond(
                always, run, lambda *_: jax.tree.map(lambda v: jnp.zeros(v.shape, v.dtype), shapes), *operands
            )
            clock.last = None
            return clock.then(out)

        def from_near(lefts, slots):
            return [pp_tensor(v, 1) for v in weight_grads(clock, lefts, slots, pieces=True)]

        x_own = text_blocks(inputs)
        x_blocks = exchange(x_own)
        wq_own = side_by_side(clock, tie(w_qkv, *x_own[1:]))
        wq_near = [pp_tensor(v, 1) for v in wq_own]
        wo_near = pp_tensor(tie(w_out, x_blocks[1]), 1)
        small = jnp.concatenate([b_qv.reshape(-1), tie(b_up, x_blocks[1])])
        small = jnp.stack([small, pp_tensor(small, 1)])
        small = list(small) + list(pp_tensor(small, 2))
        bqkv = [
            jnp.concatenate([s[:local], jnp.zeros((local,), F32), s[local : 2 * local]]) for s in small
        ]
        bup = [s[2 * local :] for s in small]
        lens = lax.dynamic_slice_in_dim(lengths, t * texts, texts)


        x_blocks[0] = tie(x_blocks[0], wo_near, *wq_near)
        wq_far = [pp_tensor(tie(v, x_blocks[3]), 2) for v in wq_own]
        cut = w_up.shape[0] // 2
        up_first, up_second = jnp.concatenate([w_up[:cut], w_out], 0), w_up[cut:]
        first_far, second_far = [pp_tensor(tie(v, x_blocks[3]), 2) for v in (up_first, up_second)]
        cot_far = lax.dynamic_slice_in_dim(cotangent, (t // 2 ^ 1) * 2 * texts, 2 * texts)
        cot_own = text_blocks(cotangent)
        cot = Exchange(cot_own[0], cot_own[1], tie(cot_far, x_blocks[3]).reshape(2, texts, part, D))
        wd_far = pp_tensor(tie(w_down, x_blocks[3]), 2)
        x, h1 = join_norm(clock, x_blocks, t, ln1_gain, ln1_bias)
        wq = [wq_own, wq_near]
        qkv = [project(clock, h1, wq[r], bqkv[r]) for r in (0, 1)]
        attn_a = attend_call(clock, lens, qkv[:2], None, length)
        wq_far = [clock.after(v) for v in wq_far]

        def project_far(values):
            passed = [pp_tensor(v, 1) for v in wq_far]
            ups, downs = pp_tensor(w_up, 1), pp_tensor(w_down, 1)
            return passed, project(clock, values, wq_far, bqkv[2]), ups, downs

        passed, q_first, wu_near, wd_near = block(project_far, h1)
        wq += [wq_far, passed]
        qkv += [q_first, project(clock, h1, wq[3], bqkv[3])]
        attn_b = attend_call(clock, lens, qkv[2:], None, length, COST_FAR)
        first_far = clock.after(first_far)
        wo_far = first_far[cut:]
        wo = [w_out, wo_near, wo_far, pp_tensor(wo_far, 1)]
        ctx = [attn_a[0], attn_a[1], attn_b[0], attn_b[1]]
        resid, h2 = attention_out(clock, x, ctx, wo, (b_out, ln2_gain, ln2_bias))
        ups = [up(clock, h2, [w_up], bup[0])]
        wu_far = [first_far[:cut], clock.after(second_far)]
        wu = [[w_up], [wu_near], wu_far, [pp_tensor(v, 1) for v in wu_far]]
        ups.append(up(clock, h2, wu[1], bup[1], COST_OUT))
        cot.forward()
        ups.append(up(clock, h2, wu[3], bup[3]))
        g_low, bias_down = join_mask(clock, cot.blocks(), t, lens)

        near = from_near([g_low], [[(0, ups[1][0])], [(0, ups[2][0])]])
        ups.insert(2, up(clock, h2, wu[2], bup[2]))
        acts, slopes = [u[0] for u in ups], [u[1] for u in ups]
        down = Chain([g_low], [[(0, acts[0])], [(0, acts[2])]], near, ["y", 0, 1] + high)
        wd_far = clock.after(wd_far)
        wd = [[w_down], [wd_near], [wd_far], [pp_tensor(wd_far, 1)]]
        dups_a, sums_a, dh2 = up_back(clock, g_low, wu[:2], wd[:2], slopes[:2], None, None, None)
        dups_b, sums_b, rest = up_back(clock, g_low, wu[2:], wd[2:], slopes[2:], dh2[0], resid, ln2_gain)
        dres, dres_low, gain_two, shift_two, bias_attn = rest
        dups, bias_up = dups_a + dups_b, sums_a + sums_b
        up_near = from_near([h2], [[(0, dups[1])], [(0, dups[3])]])
        down.step()
        grads_up = Chain([h2], [[(0, dups[0])], [(0, dups[2])]], up_near, ["y", 0, 1] + high)
        back = attend_call(clock, lens, qkv[2:], [dres_low] + wo[2:] + list(attn_b[2:]), length)
        dqkv_far, qkv_sums_far = back[:2], back[2:]
        near = from_near([h1, dres_low], [[(0, dqkv_far[1]), (1, ctx[3])]])
        down.step()
        q_far = weight_grads(clock, [h1, dres_low], [[(0, dqkv_far[0]), (1, ctx[2])]], near)
        q_far = pp_tensor(q_far, 2)
        back = attend_call(clock, lens, qkv[:2], [dres_low] + wo[:2] + list(attn_a[2:]), length)
        dqkv, qkv_sums = list(back[:2]) + list(dqkv_far), list(back[2:]) + list(qkv_sums_far)
        grads_up.step()
        for bit in high:
            down.step()
        near = from_near([h1, dres_low], [[(0, dqkv[1]), (1, ctx[1])]])
        out = Exchange(*down_out(clock, resid, acts, wd, b_down, t, texts))
        grad_down = clock.then(down.last())
        grads_up.step()
        q_own = Chain([h1, dres_low], [[(0, dqkv[0]), (1, ctx[0])]], near, [1, 0] + high, clock.after(q_far))
        in_blocks, gain_one, shift_one = norm_one_back(clock, x, dres, dqkv, wq, ln1_gain, t, texts)
        gin = Exchange(*in_blocks)
        shared = [gain_one, shift_one, gain_two, shift_two, bias_attn, bias_down]
        out.forward()
        total = pack(clock, shared, bias_up, qkv_sums, t)
        chains += [grads_up, q_own]
        for chain in chains:
            chain.flight = clock.after(chain.flight)

        def finish(total, state):
            for chain, (keep, flight) in zip(chains, state):
                chain.keep, chain.flight = keep, flight

            def reduced(flip, tensor):
                moved = pp_tensor(total, flip) if tensor else pp_dp(total, flip)
                return clock.then(total + clock.after(moved))

            q_own.step()
            total = reduced(1, True)
            total = reduced(0, False)
            for bit in high:
                q_own.step()
                grads_up.step()
            for bit in range(1, bits):
                total = reduced(bit, False)
            total = reduced(2, True)
            both = q_own.last()
            weights = jnp.stack([both[:, c * local : c * local + local] for c in range(3)])
            return total, grads_up.last(), weights, both[:, 3 * local :].T

        state = [(chain.keep, chain.flight) for chain in chains]
        total, grad_up, grad_qkv, grad_out = block(finish, total, state)
        layer_out = join_rows(clock, out.blocks(), t, COST_END)
        gin.forward()
        grad_input = join_rows(clock, gin.blocks(), t)
        first = len(shared)
        units_sum = lax.dynamic_slice_in_dim(total, first + t, 1)[0, :units]
        qv_sum = lax.dynamic_slice_in_dim(total, first + tensor_size + t, 1)[0, : 2 * local]
        return (
            layer_out,
            grad_input,
            total[0],
            total[1],
            grad_qkv,
            qv_sum.reshape(2, local),
            grad_out,
            total[4],
            total[2],
            total[3],
            grad_up,
            units_sum,
            grad_down.T,
            total[5],
        )

    return on_device


def solution(mesh):
    return jax.shard_map(
        program(mesh.shape["dp"], mesh.shape["tensor"]),
        mesh=mesh,
        in_specs=(
            P("dp", "tensor", None),
            P("dp"),
            P("dp", "tensor", None),
            P(),
            P(),
            P(None, None, "tensor"),
            P(None, "tensor"),
            P("tensor", None),
            P(),
            P(),
            P(),
            P(None, "tensor"),
            P("tensor"),
            P("tensor", None),
            P(),
        ),
        out_specs=(
            P("dp", "tensor", None),
            P("dp", "tensor", None),
            P(),
            P(),
            P(None, "dp", "tensor"),
            P(None, "tensor"),
            P("tensor", "dp"),
            P(),
            P(),
            P(),
            P("dp", "tensor"),
            P("tensor"),
            P("tensor", "dp"),
            P(),
        ),
        check_vma=False,
    )
```

```python
import functools

import jax
import jax.numpy as jnp
from jax import lax
from jax.experimental import pallas as pl
from jax.experimental.pallas import tpu as pltpu
from jax.sharding import PartitionSpec as P

D = 768
HD = 64
BF = jnp.bfloat16
F32 = jnp.float32
SCALE = HD**-0.5
LOG2E = 1.4426950408889634


def dot(left, right, left_dim, right_dim):
    return lax.dot_general(
        left, right, (((left_dim,), (right_dim,)), ((), ())), preferred_element_type=F32
    )


def norm_stats(values):
    center = values - jnp.mean(values, -1, keepdims=True)
    rstd = lax.rsqrt(jnp.mean(center * center, -1, keepdims=True) + 1e-05)
    return center * rstd, rstd


def norm_back(grad_norm, normal, rstd, gain):
    scaled = grad_norm * gain
    return rstd * (
        scaled
        - jnp.mean(scaled, -1, keepdims=True)
        - normal * jnp.mean(scaled * normal, -1, keepdims=True)
    )


class Clock:
    def __init__(self):
        self.last = None

    def after(self, values):
        return values if self.last is None else tie(values, self.last)

    def then(self, values):
        self.last = jax.tree.leaves(values)[0]
        return values


def tie(value, *waits):
    return lax.optimization_barrier((value,) + waits)[0]


def call(clock, body, out_shape, operands, *, grid=(), in_specs=None, out_specs=None, scalars=(), scratch=(),
         name=None, flops=0, plain=False):
    operands = (clock.after(operands[0]),) + tuple(operands[1:])
    if plain:
        operands = [pltpu.with_memory_space_constraint(v, pltpu.HBM) for v in operands]
    out = pl.pallas_call(
        body,
        out_shape=jax.tree.map(lambda v: pltpu.HBM(v.shape, v.dtype), out_shape) if name in ("up", "attend", "up_back") else out_shape,
        grid_spec=pltpu.PrefetchScalarGridSpec(
            num_scalar_prefetch=len(scalars),
            grid=grid,
            in_specs=in_specs,
            out_specs=out_specs,
            scratch_shapes=scratch,
        ),
        compiler_params=pltpu.CompilerParams(vmem_limit_bytes=48 << 20),
        cost_estimate=pl.CostEstimate(flops=flops, bytes_accessed=0, transcendentals=0),
        name=name,
    )(*scalars, *operands)
    return clock.then(out)


def shape_of(dims, dtype=BF):
    return jax.ShapeDtypeStruct(tuple(dims), dtype)


def whole(values):
    return pl.BlockSpec(values.shape, lambda *_: (0,) * len(values.shape))


def side_by_side(clock, w):
    half, width = w.shape[1] // 2, w.shape[2]

    def body(w_ref, *refs):
        for i in range(2):
            for c in range(3):
                refs[i][:, c * width : (c + 1) * width] = w_ref[c, i * half : (i + 1) * half, :]

    out = [shape_of((half, 3 * width))] * 2
    return call(
        clock, body, out, (w,), grid=(1,), in_specs=[whole(w)], out_specs=[whole(v) for v in out],
        name="side_by_side",
    )


def times(left, pieces):
    total, start = None, 0
    for ref in pieces:
        part = dot(left[:, start : start + ref.shape[0]], ref[...], 1, 0)
        start += ref.shape[0]
        total = part if total is None else total + part
    return total


def times_turned(left, pieces):
    parts = [dot(left, ref[...], 1, 1) for ref in pieces]
    return parts[0] if len(parts) == 1 else jnp.concatenate(parts, 1)


def split_refs(refs, counts):
    out = []
    for count in counts:
        out.append(refs[:count])
        refs = refs[count:]
    return out


def row_block(values, steps):
    return pl.BlockSpec((values.shape[0] // steps, values.shape[1]), lambda i, *_: (i, 0))


def project(clock, h, w, bias):
    def body(h_ref, bias_ref, *refs):
        refs[-1][...] = (times(h_ref[...], refs[:-1]) + bias_ref[...]).astype(BF)

    bias = bias.reshape(1, -1)
    out = shape_of((h.shape[0], bias.shape[1]))
    return call(
        clock, body, out, (h, bias, *w), grid=(4,), in_specs=[row_block(h, 4), whole(bias)] + [whole(v) for v in w],
        out_specs=row_block(out, 4), name="project",
    )


def attention_out(clock, x, ctx, w, vectors, cost=0):
    count = len(ctx)

    def body(x_ref, *refs):
        ctx_refs, w_refs, (bias_ref, gain_ref, shift_ref), (out_ref, h_ref) = split_refs(refs, (count, count, 3, 2))
        total = x_ref[...].astype(F32) + bias_ref[...]
        for r in range(count):
            total = total + dot(ctx_refs[r][...], w_refs[r][...], 1, 0)
        out_ref[...] = total
        normal, _ = norm_stats(total)
        h_ref[...] = (normal * gain_ref[...] + shift_ref[...]).astype(BF)

    vectors = [v.reshape(1, -1) for v in vectors]
    out = [shape_of(x.shape, F32), shape_of(x.shape)]
    return call(
        clock, body, out, (x, *ctx, *w, *vectors), grid=(4,),
        in_specs=[row_block(v, 4) for v in (x, *ctx)] + [whole(v) for v in (*w, *vectors)],
        out_specs=[row_block(v, 4) for v in out], name="attention_out", flops=cost, plain=True,
    )


def up(clock, h, w, bias, cost=0):
    def body(h_ref, bias_ref, *refs):
        upper = times(h_ref[...], refs[:-2]) + bias_ref[...]
        below = 0.5 * (1.0 + lax.erf(upper * (0.5**0.5)))
        density = jnp.exp(-0.5 * upper * upper) * 0.3989422804014327
        refs[-2][...] = (upper * below).astype(BF)
        refs[-1][...] = (below + upper * density).astype(BF)

    bias = bias.reshape(1, -1)
    out = [shape_of((h.shape[0], bias.shape[1]))] * 2
    return call(
        clock, body, out, (h, bias, *w), grid=(4,), in_specs=[row_block(h, 4), whole(bias)] + [whole(v) for v in w],
        out_specs=[row_block(v, 4) for v in out], name="up", flops=cost,
    )


def to_owner(refs, at, values, scratch, count):
    text, late = pl.program_id(0) // 2, pl.program_id(0) % 2
    part = values.shape[0] * 2 // count
    scratch[...] = values.astype(BF)
    for r in range(count):
        place = at[0] ^ r

        @pl.when(place // (count // 2) == late)
        def _():
            start = pl.multiple_of((place % (count // 2)) * part, part)
            rows = scratch[pl.ds(start, part), :]
            if r < 2:
                refs[r][pl.ds(text, 1)] = rows[None]
            else:
                refs[2][pl.ds(place % 2, 1), pl.ds(text, 1)] = rows[None, None]


def owner_shapes(texts, count, rows, width):
    block = (texts, rows // texts // count, width)
    return [shape_of(block), shape_of(block), shape_of((2, *block))]


def down_out(clock, resid, acts, w, bias, me, texts):
    count = len(acts)
    sizes = [len(pieces) for pieces in w]
    w = [v for pieces in w for v in pieces]
    steps = texts * 2

    def body(at, resid_ref, *refs):
        act_refs, w_refs, (bias_ref,), outs, (scratch,) = split_refs(refs, (count, len(w), 1, 3, 1))
        w_refs = split_refs(w_refs, sizes)
        total = resid_ref[...] + bias_ref[...]
        for r in range(count):
            total = total + times(act_refs[r], w_refs[r])
        to_owner(outs, at, total, scratch, count)

    bias = bias.reshape(1, -1)
    out = owner_shapes(texts, count, *resid.shape)
    return call(
        clock, body, out, (resid, *acts, *w, bias), grid=(steps,),
        in_specs=[row_block(v, steps) for v in (resid, *acts)] + [whole(v) for v in (*w, bias)],
        out_specs=[whole(v) for v in out], scalars=(me.reshape(1),),
        scratch=[pltpu.VMEM((resid.shape[0] // steps, resid.shape[1]), BF)], name="down_out",
    )


def norm_one_back(clock, x, dres, dqkv, w, gain, me, texts):
    count = len(dqkv)
    steps = texts * 2
    sizes = [len(pieces) for pieces in w]
    flat = [v for pieces in w for v in pieces]

    def body(at, x_ref, dres_ref, *refs):
        grads, w_refs, (gain_ref,), outs, (gain_sum, shift_sum, scratch) = split_refs(
            refs, (count, len(flat), 1, 3, 3)
        )
        w_refs = split_refs(w_refs, sizes)
        total = None
        for r in range(count):
            part = times_turned(grads[r][...], w_refs[r])
            total = part if total is None else total + part
        normal, rstd = norm_stats(x_ref[...].astype(F32))

        @pl.when(pl.program_id(0) == 0)
        def _():
            gain_sum[...] = jnp.zeros_like(gain_sum)
            shift_sum[...] = jnp.zeros_like(shift_sum)

        gain_sum[...] += jnp.sum(total * normal, 0, keepdims=True)
        shift_sum[...] += jnp.sum(total, 0, keepdims=True)
        to_owner(outs, at, dres_ref[...] + norm_back(total, normal, rstd, gain_ref[...]), scratch, count)

    gain = gain.reshape(1, -1)
    out = owner_shapes(texts, count, *x.shape) + [shape_of(gain.shape, F32)] * 2
    out = call(
        clock, body, out, (x, dres, *dqkv, *flat, gain), grid=(steps,),
        in_specs=[row_block(v, steps) for v in (x, dres, *dqkv)] + [whole(v) for v in (*flat, gain)],
        out_specs=[whole(v) for v in out], scalars=(me.reshape(1),),
        scratch=[pltpu.VMEM((x.shape[0] // steps, x.shape[1]), BF)], name="norm_one_back",
    )
    return out[:3], out[3], out[4]


def block_of(refs, at, r, i):
    return refs[r][i] if refs[r].ndim == 3 else refs[r][at[0] % 2, i]


def join_norm(clock, blocks, me, gain, shift):
    texts, part, width = blocks[0].shape
    count = len(blocks)

    def body(at, *refs):
        ins, (gain_ref, shift_ref, x_ref, h_ref) = refs[:count], refs[count:]
        for r in range(count):
            for i in range(texts):
                start = pl.multiple_of(i * count * part + (at[0] ^ r) * part, part)
                low = ins[r][i]
                normal, _ = norm_stats(low.astype(F32))
                x_ref[pl.ds(start, part), :] = low
                h_ref[pl.ds(start, part), :] = (normal * gain_ref[...] + shift_ref[...]).astype(BF)

    out = [shape_of((texts * count * part, width))] * 2
    operands = (*blocks, gain.reshape(1, -1), shift.reshape(1, -1))
    return call(
        clock, body, out, operands, grid=(1,), in_specs=[whole(v) for v in operands], out_specs=[whole(v) for v in out],
        scalars=(me.reshape(1),), name="join_norm",
    )


def join_mask(clock, blocks, me, lens):
    texts, part, width = blocks[0].shape
    count = len(blocks)

    def body(at, n, *refs):
        ins, (g_ref, sum_ref) = refs[:count], refs[count:]
        total = jnp.zeros((1, width), F32)
        for r in range(count):
            for i in range(texts):
                place = (at[0] ^ r) * part
                start = pl.multiple_of(i * count * part + place, part)
                live = lax.broadcasted_iota(jnp.int32, (part, width), 0) + place < n[i]
                values = jnp.where(live, block_of(ins, at, r, i).astype(F32), 0.0)
                total = total + jnp.sum(values, 0, keepdims=True)
                g_ref[pl.ds(start, part), :] = values.astype(BF)
        sum_ref[...] = total

    out = [shape_of((texts * count * part, width)), shape_of((1, width), F32)]
    return call(
        clock, body, out, blocks, grid=(1,), in_specs=[whole(v) for v in blocks], out_specs=[whole(v) for v in out],
        scalars=(me.reshape(1), lens), name="join_mask",
    )


def join_rows(clock, blocks, me, cost=0):
    texts = blocks[0].shape[0]
    count = len(blocks)

    def body(at, *refs):
        for r in range(count):
            for i in range(texts):
                refs[count][pl.ds((at[0] ^ r) * texts + i, 1)] = block_of(refs, at, r, i)[None]

    out = shape_of((texts * count,) + blocks[0].shape[1:])
    return call(
        clock, body, out, blocks, grid=(1,), in_specs=[whole(v) for v in blocks], out_specs=whole(out),
        scalars=(me.reshape(1),), name="join_rows", flops=cost,
    )


def up_back(clock, g, ups, downs, slopes, base, resid, gain):
    rows, width = g.shape
    count = len(ups)
    units = slopes[0].shape[1]
    down_sizes = [len(pieces) for pieces in downs]
    downs = [v for pieces in downs for v in pieces]
    sizes = [len(pieces) for pieces in ups]
    flat = [v for pieces in ups for v in pieces]
    last = base is not None

    def body(g_ref, *refs):
        up_refs, down_refs, slope_refs, more, grad_refs, sum_refs, outs = split_refs(
            refs, (len(flat), len(downs), count, 3 if last else 0, count, count, 5 if last else 1)
        )
        up_refs = split_refs(up_refs, sizes)
        down_refs = split_refs(down_refs, down_sizes)
        grad = g_ref[...]
        total = more[0][...] if last else None

        @pl.when(pl.program_id(0) == 0)
        def _():
            for ref in list(sum_refs) + list(outs[2:]):
                ref[...] = jnp.zeros_like(ref)

        for s in range(count):
            upper = times_turned(grad, down_refs[s]) * slope_refs[s][...].astype(F32)
            sum_refs[s][...] += jnp.sum(upper, 0, keepdims=True)
            low = upper.astype(BF)
            grad_refs[s][...] = low
            part = times_turned(low, up_refs[s])
            total = part if total is None else total + part
        if last:
            normal, rstd = norm_stats(more[1][...])
            outs[2][...] += jnp.sum(total * normal, 0, keepdims=True)
            outs[3][...] += jnp.sum(total, 0, keepdims=True)
            total = grad.astype(F32) + norm_back(total, normal, rstd, more[2][...])
            outs[4][...] += jnp.sum(total, 0, keepdims=True)
            outs[1][...] = total.astype(BF)
        outs[0][...] = total

    sums, vector = shape_of((1, units), F32), shape_of((1, width), F32)
    unit = pl.BlockSpec((rows // 4, units), lambda i: (i, 0))
    operands = (g, *flat, *downs, *slopes)
    in_specs = [row_block(g, 4)] + [whole(v) for v in (*flat, *downs)] + [unit] * count
    outs = [shape_of((rows, width), F32)]
    out_specs = [row_block(g, 4)]
    if last:
        gain = gain.reshape(1, -1)
        operands += (base, resid, gain)
        in_specs += [row_block(g, 4)] * 2 + [whole(gain)]
        outs += [shape_of((rows, width))] + [vector] * 3
        out_specs += [row_block(g, 4)] + [whole(vector)] * 3
    out = call(
        clock, body,
        [shape_of((rows, units))] * count + [sums] * count + outs,
        operands,
        grid=(4,),
        in_specs=in_specs,
        out_specs=[unit] * count + [whole(sums)] * count + out_specs,
        name="up_back",
    )
    return list(out[:count]), list(out[count : 2 * count]), out[2 * count :]


def weight_grads(clock, lefts, slots, near=None, split=None, apart=False, pieces=False, extra=None):
    rows, width = lefts[0].shape
    columns = sum(right.shape[1] for _, right in slots[0])
    count = len(slots)
    half = width // 2
    rights = [right for slot in slots for _, right in slot]

    def body(*refs):
        if split is not None:
            at, refs = refs[0], refs[1:]
        left_refs, refs = refs[: len(lefts)], refs[len(lefts) :]
        right_refs, refs = list(refs[: len(rights)]), refs[len(rights) :]
        if near is not None:
            near_refs, refs = refs[: len(near)], refs[len(near) :]
        if extra is not None:
            extra_ref, refs = refs[0], refs[1:]
        for s, slot in enumerate(slots):
            start = 0
            for which, right in slot:
                product = dot(left_refs[which][...], right_refs.pop(0)[...], 0, 0)
                cols = slice(start, start + right.shape[1])
                start = cols.stop
                for i in range(2):
                    low, high = max(cols.start, i * columns // 2), min(cols.stop, (i + 1) * columns // 2)
                    if low < high:
                        here = slice(low - cols.start, high - cols.start)
                        there = slice(low - i * columns // 2, high - i * columns // 2)
                        value = product[:, here]
                        if near is not None:
                            value = value + near_refs[2 * s + i][:, there].astype(F32)
                        if extra is not None:
                            value = value + extra_ref[s, :, low:high].astype(F32)
                        if pieces:
                            refs[2 * s + i][:, there] = value.astype(BF)
                        elif apart:
                            refs[s][0, :, low:high] = value.astype(BF)
                        elif split is None:
                            refs[0][s, :, low:high] = value.astype(BF)
                        else:
                            refs[2][:, low:high] = value
            if split is not None:
                outer, inner = split[0] // 2, width // split[0] // 2
                for a in range(outer):
                    for ref, bit in ((refs[0], 1 - at[0]), (refs[1], at[0])):
                        place = pl.multiple_of((2 * a + bit) * inner, inner)
                        ref[s, a * inner : (a + 1) * inner, :] = refs[2][pl.ds(place, inner), :].astype(BF)

    left = pl.BlockSpec((rows, half), lambda i, *_: (0, i))
    tall = pl.BlockSpec((count, half, columns), lambda i, *_: (0, i, 0))
    narrow = pl.BlockSpec((half, columns // 2), lambda i, *_: (i, 0))
    short = pl.BlockSpec((count, half // 2, columns), lambda i, *_: (0, i, 0))
    operands = (*lefts, *rights) + (() if near is None else tuple(near)) + (() if extra is None else (extra,))
    if pieces:
        out_shape = [shape_of((width, columns // 2))] * (2 * count)
        out_specs = [narrow] * (2 * count)
    elif apart:
        out_shape = [shape_of((1, width, columns))] * count
        out_specs = [pl.BlockSpec((1, half, columns), lambda i, *_: (0, i, 0))] * count
    elif split is None:
        out_shape, out_specs = shape_of((count, width, columns)), tall
    else:
        out_shape, out_specs = [shape_of((count, half, columns))] * 2, [short] * 2
    return call(
        clock, body,
        out_shape,
        operands,
        grid=(2,),
        in_specs=[left] * len(lefts) + [whole(v) for v in rights] + ([] if near is None else [narrow] * len(near)) + ([] if extra is None else [tall]),
        out_specs=out_specs,
        scalars=() if split is None else (split[1].reshape(1),),
        scratch=[] if split is None else [pltpu.VMEM((half, columns), F32)],
        name="weight_grads",
    )


def add_split(clock, keep, arrived, outer, index):
    columns = keep.shape[-1]
    inner = keep.size // columns // outer // 2

    def body(at, keep_ref, arrived_ref, send_ref, out_ref):
        for ref, bit in ((send_ref, 1 - at[0]), (out_ref, at[0])):
            ref[0] = (keep_ref[0, bit].astype(F32) + arrived_ref[0, bit].astype(F32)).astype(BF)

    tall = pl.BlockSpec((1, 2, inner, columns), lambda i, *_: (i, 0, 0, 0))
    short = pl.BlockSpec((1, inner, columns), lambda i, *_: (i, 0, 0))
    return call(
        clock, body,
        [shape_of((outer, inner, columns))] * 2,
        (keep.reshape(outer, 2, inner, columns), arrived.reshape(outer, 2, inner, columns)),
        grid=(outer,),
        in_specs=[tall] * 2,
        out_specs=[short] * 2,
        scalars=(jnp.asarray(index, jnp.int32).reshape(1),),
        name="add_split",
    )


def pack(clock, shared, units, projected, me, cost=0):
    count = len(units)
    first = len(shared)

    def body(at, *refs):
        shared_refs, unit_refs, q_refs, (out_ref,) = split_refs(refs, (first, count, count, 1))
        out_ref[...] = jnp.zeros_like(out_ref)
        for i in range(first):
            out_ref[i : i + 1, :] = shared_refs[i][...]
        for r in range(count):
            width = q_refs[r].shape[1] // 3
            row = pl.ds(first + (at[0] ^ r), 1)
            out_ref[row, : unit_refs[r].shape[1]] = unit_refs[r][...]
            row = pl.ds(first + count + (at[0] ^ r), 1)
            out_ref[row, :width] = q_refs[r][:, :width]
            out_ref[row, width : 2 * width] = q_refs[r][:, 2 * width :]

    out = shape_of((first + 2 * count, max(D, units[0].shape[1])), F32)
    operands = (*shared, *units, *projected)
    return call(
        clock, body, out, operands, grid=(1,), in_specs=[whole(v) for v in operands], out_specs=whole(out),
        scalars=(me.reshape(1),), name="pack", flops=cost,
    )


def attend_body(lens, *refs, step, heads):
    ins, outs, (p_ref, inv_ref) = refs[:2], refs[2:4], refs[4:]
    n = lens[pl.program_id(0)]
    length = ins[0].shape[0]
    width = heads * HD

    def rows(live):
        edge = lax.broadcasted_iota(jnp.int32, (step, length), 0) < n - (live - step)
        for which in range(2):
            ref, ctx_ref = ins[which], outs[which]
            for head in range(heads):
                slot = which * heads + head
                cols = slice(head * HD, head * HD + HD)
                keys = ref[:live, width + head * HD : width + head * HD + HD]
                values = ref[:live, 2 * width + head * HD : 2 * width + head * HD + HD]
                scores = dot(keys, ref[:, cols], 1, 1)
                last = jnp.where(edge, scores[live - step :], -1e30)
                if live > step:
                    scores = jnp.concatenate([scores[: live - step], last], 0)
                else:
                    scores = last
                top = jnp.max(scores, 0, keepdims=True)
                power = jnp.exp2((scores - top) * (SCALE * LOG2E))
                inverse = 1.0 / jnp.sum(power, 0, keepdims=True)
                low = power.astype(BF)
                p_ref[0, slot, :live, :] = low
                inv_ref[0, slot : slot + 1, :] = inverse
                mixed = dot(low, values, 0, 0)
                ctx_ref[:, cols] = (mixed * inverse.reshape(length, 1)).astype(BF)

    for live in range(step, length + 1, step):
        pl.when((n > live - step) & (n <= live))(functools.partial(rows, live))


def attend_back_body(lens, *refs, step, heads):
    ins, (grad_ref,), w_refs, (p_ref, inv_ref) = refs[:2], refs[2:3], refs[3:5], refs[5:7]
    outs, sums, do_ref = refs[7:9], refs[9:11], refs[11]
    n = lens[pl.program_id(0)]
    length = ins[0].shape[0]
    width = heads * HD

    def rows(live):
        for which in range(2):
            ref, out_ref = ins[which], outs[which]
            do_ref[:live, :] = dot(grad_ref[:live, :], w_refs[which][...], 1, 1)
            for head in range(heads):
                slot = which * heads + head
                at = [slice(c * width + head * HD, c * width + head * HD + HD) for c in range(3)]
                inverse = inv_ref[0, slot : slot + 1, :live]
                grad = (do_ref[:live, at[0]] * inverse.reshape(live, 1)).astype(BF)
                low = p_ref[0, slot, :live, :live]
                grad_probs = dot(ref[:live, at[2]], grad, 1, 1)
                power = low.astype(F32)
                product = power * grad_probs
                inner = jnp.sum(product, 0, keepdims=True) * inverse
                grad_scores = (product - power * inner).astype(BF)
                out_ref[:live, at[2]] = dot(low, grad, 1, 0).astype(BF)
                out_ref[:live, at[1]] = (dot(grad_scores, ref[:live, at[0]], 1, 0) * SCALE).astype(BF)
                out_ref[:live, at[0]] = (dot(grad_scores, ref[:live, at[1]], 0, 0) * SCALE).astype(BF)
            if live < length:
                out_ref[live:, :] = jnp.zeros((length - live, 3 * width), BF)
            sums[which][...] += jnp.sum(out_ref[:live, :].astype(F32), 0, keepdims=True)

    @pl.when(pl.program_id(0) == 0)
    def _():
        for ref in sums:
            ref[...] = jnp.zeros_like(ref)

    for live in range(step, length + 1, step):
        pl.when((n > live - step) & (n <= live))(functools.partial(rows, live))


def attend_call(clock, lens, qkv, back, length, cost=0):
    texts = lens.shape[0]
    width = qkv[0].shape[1] // 3
    heads = width // HD
    wide = pl.BlockSpec((length, 3 * width), lambda i, *_: (i, 0))
    slim = pl.BlockSpec((length, width), lambda i, *_: (i, 0))
    full = pl.BlockSpec((length, D), lambda i, *_: (i, 0))
    probs = pl.BlockSpec((1, 2 * heads, length, length), lambda i, *_: (i, 0, 0, 0))
    inverse = pl.BlockSpec((1, 2 * heads, length), lambda i, *_: (i, 0, 0))
    rows = texts * length
    if back is None:
        return call(
            clock,
            functools.partial(attend_body, step=length // 4, heads=heads),
            [shape_of((rows, width))] * 2
            + [shape_of((texts, 2 * heads, length, length)), shape_of((texts, 2 * heads, length), F32)],
            tuple(qkv),
            grid=(texts,),
            in_specs=[wide] * 2,
            out_specs=[slim] * 2 + [probs, inverse],
            scalars=(lens,),
            name="attend",
            flops=cost,
        )
    return call(
        clock,
        functools.partial(attend_back_body, step=length // 4, heads=heads),
        [shape_of((rows, 3 * width))] * 2 + [shape_of((1, 3 * width), F32)] * 2,
        tuple(qkv) + tuple(back),
        grid=(texts,),
        in_specs=[wide] * 2 + [full] + [whole(w) for w in back[1:3]] + [probs, inverse],
        out_specs=[wide] * 2 + [pl.BlockSpec((1, 3 * width), lambda i, *_: (0, 0))] * 2,
        scalars=(lens,),
        scratch=[pltpu.VMEM((length, width), F32)],
        name="attend_back",
    )


COST_FAR, COST_OUT, COST_END = 14 * 10**9, 4 * 10**9, 7 * 10**9


def program(dp_size, tensor_size):
    bits = dp_size.bit_length() - 1

    def pp_tensor(values, flip):
        return lax.ppermute(values, "tensor", [(i, i ^ flip) for i in range(tensor_size)])

    def pp_dp(values, bit):
        return lax.ppermute(values, "dp", [(i, i ^ (1 << bit)) for i in range(dp_size)])

    def on_device(
        inputs,
        lengths,
        cotangent,
        ln1_gain,
        ln1_bias,
        w_qkv,
        b_qv,
        w_out,
        b_out,
        ln2_gain,
        ln2_bias,
        w_up,
        b_up,
        w_down,
        b_down,
    ):
        t = lax.axis_index("tensor")
        d = lax.axis_index("dp")
        texts_all, part = inputs.shape[:2]
        texts = texts_all // tensor_size
        length = part * tensor_size
        rows = texts * length
        rels = range(tensor_size)
        local = w_qkv.shape[2]
        units = b_up.shape[0]
        inner = D // dp_size
        bit_of = [(d >> b) & 1 for b in range(bits)]
        clock = Clock()
        chains = []

        def pick(values, index, axis):
            return lax.dynamic_index_in_dim(values, index, axis, keepdims=False)

        def text_blocks(values):
            return [
                lax.dynamic_slice(values, ((t ^ r) * texts, 0, 0), (texts, part, D)) for r in rels
            ]

        def exchange(blocks):
            far = {r: pp_tensor(blocks[r], r) for r in (3, 2, 1)}
            return [blocks[0]] + [far[r] for r in (1, 2, 3)]

        class Exchange:
            def __init__(self, own, near, far):
                self.own, self.near, self.far = own, near, pp_tensor(far, 2)

            def forward(self):
                self.far = clock.after(self.far)
                self.near = pp_tensor(clock.after(self.near), 1)
                self.last = pp_tensor(pick(self.far, 1 - t % 2, 0), 1)

            def blocks(self):
                return [self.own, clock.after(self.near), self.far, clock.after(self.last)]

        class Chain:
            def __init__(self, lefts, slots, near, steps, extra=None):
                self.steps = list(steps)
                self.dims = [len(slots)] + [2] * bits
                step = self.steps.pop(0)
                outer, index = self.place(step)
                if step == "y":
                    self.keep, self.sent = weight_grads(clock, lefts, slots, near, apart=True)
                elif inner % 16 == 0 and outer > len(slots):
                    split = (outer // len(slots), index)
                    self.sent, self.keep = weight_grads(clock, lefts, slots, near, split, extra=extra)
                else:
                    total = weight_grads(clock, lefts, slots, near, extra=extra)
                    self.sent, self.keep = self.halves(total, outer, index)
                self.fly(step)

            def place(self, step):
                axis = 0 if step == "y" else bits - step
                outer = 1
                for size in self.dims[:axis]:
                    outer *= size
                self.dims[axis] = 1
                return outer, 0 * t if step == "y" else bit_of[step]

            def halves(self, total, outer, index):
                view = total.reshape(outer, 2, -1, total.shape[-1])
                return pick(view, 1 - index, 1), pick(view, index, 1)

            def fly(self, step):
                self.flight = pp_tensor(self.sent, 2) if step == "y" else pp_dp(self.sent, step)

            def step(self):
                arrived = clock.after(self.flight)
                step = self.steps.pop(0)
                outer, index = self.place(step)
                if inner % 16 == 0:
                    self.sent, self.keep = add_split(clock, self.keep, arrived, outer, index)
                else:
                    total = (self.keep.astype(F32) + arrived.astype(F32)).astype(BF)
                    self.sent, self.keep = self.halves(total, outer, index)
                self.fly(step)

            def last(self):
                total = self.keep.astype(F32) + clock.after(self.flight).astype(F32)
                return total.reshape(-1, total.shape[-1])

        high = list(range(2, bits))

        always = (lengths[0] | 1) != 0

        def block(steps, *operands):
            operands = (clock.after(operands[0]),) + operands[1:]

            def run(*values):
                clock.last = None
                return steps(*values)

            saved = [(list(chain.steps), list(chain.dims)) for chain in chains]
            shapes = jax.eval_shape(lambda *v: run(*v), *operands)
            for chain, (left, dims) in zip(chains, saved):
                chain.steps, chain.dims = left, dims
            out = lax.cond(
                always, run, lambda *_: jax.tree.map(lambda v: jnp.zeros(v.shape, v.dtype), shapes), *operands
            )
            clock.last = None
            return clock.then(out)

        def from_near(lefts, slots):
            return [pp_tensor(v, 1) for v in weight_grads(clock, lefts, slots, pieces=True)]

        x_own = text_blocks(inputs)
        x_blocks = exchange(x_own)
        wq_own = side_by_side(clock, tie(w_qkv, *x_own[1:]))
        wq_near = [pp_tensor(v, 1) for v in wq_own]
        wo_near = pp_tensor(tie(w_out, x_blocks[1]), 1)
        small = jnp.concatenate([b_qv.reshape(-1), tie(b_up, x_blocks[1])])
        small = jnp.stack([small, pp_tensor(small, 1)])
        small = list(small) + list(pp_tensor(small, 2))
        bqkv = [
            jnp.concatenate([s[:local], jnp.zeros((local,), F32), s[local : 2 * local]]) for s in small
        ]
        bup = [s[2 * local :] for s in small]
        lens = lax.dynamic_slice_in_dim(lengths, t * texts, texts)


        x_blocks[0] = tie(x_blocks[0], wo_near, *wq_near)
        wq_far = [pp_tensor(tie(v, x_blocks[3]), 2) for v in wq_own]
        cut = w_up.shape[0] // 2
        up_first, up_second = jnp.concatenate([w_up[:cut], w_out], 0), w_up[cut:]
        first_far, second_far = [pp_tensor(tie(v, x_blocks[3]), 2) for v in (up_first, up_second)]
        cot_far = lax.dynamic_slice_in_dim(cotangent, (t // 2 ^ 1) * 2 * texts, 2 * texts)
        cot_own = text_blocks(cotangent)
        cot = Exchange(cot_own[0], cot_own[1], tie(cot_far, x_blocks[3]).reshape(2, texts, part, D))
        wd_far = pp_tensor(tie(w_down, x_blocks[3]), 2)
        x, h1 = join_norm(clock, x_blocks, t, ln1_gain, ln1_bias)
        wq = [wq_own, wq_near]
        qkv = [project(clock, h1, wq[r], bqkv[r]) for r in (0, 1)]
        attn_a = attend_call(clock, lens, qkv[:2], None, length)
        wq_far = [clock.after(v) for v in wq_far]

        def project_far(values):
            passed = [pp_tensor(v, 1) for v in wq_far]
            ups, downs = pp_tensor(w_up, 1), pp_tensor(w_down, 1)
            return passed, project(clock, values, wq_far, bqkv[2]), ups, downs

        passed, q_first, wu_near, wd_near = block(project_far, h1)
        wq += [wq_far, passed]
        qkv += [q_first, project(clock, h1, wq[3], bqkv[3])]
        attn_b = attend_call(clock, lens, qkv[2:], None, length, COST_FAR)
        first_far = clock.after(first_far)
        wo_far = first_far[cut:]
        wo = [w_out, wo_near, wo_far, pp_tensor(wo_far, 1)]
        ctx = [attn_a[0], attn_a[1], attn_b[0], attn_b[1]]
        resid, h2 = attention_out(clock, x, ctx, wo, (b_out, ln2_gain, ln2_bias))
        ups = [up(clock, h2, [w_up], bup[0])]
        wu_far = [first_far[:cut], clock.after(second_far)]
        wu = [[w_up], [wu_near], wu_far, [pp_tensor(v, 1) for v in wu_far]]
        ups.append(up(clock, h2, wu[1], bup[1], COST_OUT))
        cot.forward()
        ups.append(up(clock, h2, wu[3], bup[3]))
        g_low, bias_down = join_mask(clock, cot.blocks(), t, lens)

        near = from_near([g_low], [[(0, ups[1][0])], [(0, ups[2][0])]])
        ups.insert(2, up(clock, h2, wu[2], bup[2]))
        acts, slopes = [u[0] for u in ups], [u[1] for u in ups]
        down = Chain([g_low], [[(0, acts[0])], [(0, acts[2])]], near, ["y", 0, 1] + high)
        wd_far = clock.after(wd_far)
        wd = [[w_down], [wd_near], [wd_far], [pp_tensor(wd_far, 1)]]
        dups_a, sums_a, dh2 = up_back(clock, g_low, wu[:2], wd[:2], slopes[:2], None, None, None)
        dups_b, sums_b, rest = up_back(clock, g_low, wu[2:], wd[2:], slopes[2:], dh2[0], resid, ln2_gain)
        dres, dres_low, gain_two, shift_two, bias_attn = rest
        dups, bias_up = dups_a + dups_b, sums_a + sums_b
        up_near = from_near([h2], [[(0, dups[1])], [(0, dups[3])]])
        down.step()
        grads_up = Chain([h2], [[(0, dups[0])], [(0, dups[2])]], up_near, ["y", 0, 1] + high)
        back = attend_call(clock, lens, qkv[2:], [dres_low] + wo[2:] + list(attn_b[2:]), length)
        dqkv_far, qkv_sums_far = back[:2], back[2:]
        near = from_near([h1, dres_low], [[(0, dqkv_far[1]), (1, ctx[3])]])
        down.step()
        q_far = weight_grads(clock, [h1, dres_low], [[(0, dqkv_far[0]), (1, ctx[2])]], near)
        q_far = pp_tensor(q_far, 2)
        back = attend_call(clock, lens, qkv[:2], [dres_low] + wo[:2] + list(attn_a[2:]), length)
        dqkv, qkv_sums = list(back[:2]) + list(dqkv_far), list(back[2:]) + list(qkv_sums_far)
        grads_up.step()
        for bit in high:
            down.step()
        near = from_near([h1, dres_low], [[(0, dqkv[1]), (1, ctx[1])]])
        out = Exchange(*down_out(clock, resid, acts, wd, b_down, t, texts))
        grad_down = clock.then(down.last())
        grads_up.step()
        q_own = Chain([h1, dres_low], [[(0, dqkv[0]), (1, ctx[0])]], near, [1, 0] + high, clock.after(q_far))
        in_blocks, gain_one, shift_one = norm_one_back(clock, x, dres, dqkv, wq, ln1_gain, t, texts)
        gin = Exchange(*in_blocks)
        shared = [gain_one, shift_one, gain_two, shift_two, bias_attn, bias_down]
        out.forward()
        chains += [grads_up, q_own]
        for chain in chains:
            chain.flight = clock.then(clock.after(chain.flight))
        total = pack(clock, shared, bias_up, qkv_sums, t, COST_END)
        out_blocks = out.blocks()

        def moved(values, flip, tensor):
            flight = pp_tensor(values, flip) if tensor else pp_dp(values, flip)
            return clock.then(values + clock.after(flight))

        def load(state):
            for chain, (keep, flight) in zip(chains, state):
                chain.keep, chain.flight = keep, flight

        def begin(total, state):
            load(state)
            for bit in high[:1]:
                grads_up.step()
            q_own.step()
            total = moved(total, 1, True)
            for bit in (1, 0)[-bits:]:
                total = moved(total, bit, False)
            return total, [(chain.keep, clock.after(chain.flight)) for chain in chains]

        def finish(total, state, blocks):
            load(state)
            for bit in high[1:]:
                grads_up.step()
            grad_up = clock.then(grads_up.last())
            for bit in high:
                q_own.step()
                total = moved(total, bit, False)
            total = moved(total, 2, True)
            rows_out = join_rows(clock, blocks, t)
            first = len(shared)
            vectors = [total[i] for i in range(first)]
            vectors.append(lax.dynamic_slice_in_dim(total, first + t, 1)[0, :units])
            qv = lax.dynamic_slice_in_dim(total, first + tensor_size + t, 1)[0, : 2 * local]
            vectors.append(qv.reshape(2, local))
            both = q_own.last()
            weights = jnp.stack([both[:, c * local : c * local + local] for c in range(3)])
            return rows_out, vectors, grad_up, weights, both[:, 3 * local :].T

        state = [(chain.keep, chain.flight) for chain in chains]
        total, state = block(begin, total, state)
        gin.forward()
        layer_out, vector, grad_up, grad_qkv, grad_out = block(finish, total, state, out_blocks)
        grad_input = join_rows(clock, gin.blocks(), t)
        return (
            layer_out,
            grad_input,
            vector[0],
            vector[1],
            grad_qkv,
            vector[7],
            grad_out,
            vector[4],
            vector[2],
            vector[3],
            grad_up,
            vector[6],
            grad_down.T,
            vector[5],
        )

    return on_device


def solution(mesh):
    return jax.shard_map(
        program(mesh.shape["dp"], mesh.shape["tensor"]),
        mesh=mesh,
        in_specs=(
            P("dp", "tensor", None),
            P("dp"),
            P("dp", "tensor", None),
            P(),
            P(),
            P(None, None, "tensor"),
            P(None, "tensor"),
            P("tensor", None),
            P(),
            P(),
            P(),
            P(None, "tensor"),
            P("tensor"),
            P("tensor", None),
            P(),
        ),
        out_specs=(
            P("dp", "tensor", None),
            P("dp", "tensor", None),
            P(),
            P(),
            P(None, "dp", "tensor"),
            P(None, "tensor"),
            P("tensor", "dp"),
            P(),
            P(),
            P(),
            P("dp", "tensor"),
            P("tensor"),
            P("tensor", "dp"),
            P(),
        ),
        check_vma=False,
    )
```

```python
import functools

import jax
import jax.numpy as jnp
from jax import lax
from jax.experimental import pallas as pl
from jax.experimental.pallas import tpu as pltpu
from jax.sharding import PartitionSpec as P

D = 768
HD = 64
BF = jnp.bfloat16
F32 = jnp.float32
SCALE = HD**-0.5
LOG2E = 1.4426950408889634


def dot(left, right, left_dim, right_dim):
    return lax.dot_general(
        left, right, (((left_dim,), (right_dim,)), ((), ())), preferred_element_type=F32
    )


def norm_stats(values):
    center = values - jnp.mean(values, -1, keepdims=True)
    rstd = lax.rsqrt(jnp.mean(center * center, -1, keepdims=True) + 1e-05)
    return center * rstd, rstd


def norm_back(grad_norm, normal, rstd, gain):
    scaled = grad_norm * gain
    return rstd * (
        scaled
        - jnp.mean(scaled, -1, keepdims=True)
        - normal * jnp.mean(scaled * normal, -1, keepdims=True)
    )


class Clock:
    def __init__(self):
        self.last = None

    def after(self, values):
        return values if self.last is None else tie(values, self.last)

    def then(self, values):
        self.last = jax.tree.leaves(values)[0]
        return values


def tie(value, *waits):
    return lax.optimization_barrier((value,) + waits)[0]


def call(clock, body, out_shape, operands, *, grid=(), in_specs=None, out_specs=None, scalars=(), scratch=(),
         name=None, flops=0, plain=False):
    operands = (clock.after(operands[0]),) + tuple(operands[1:])
    if plain:
        operands = [pltpu.with_memory_space_constraint(v, pltpu.HBM) for v in operands]
    out = pl.pallas_call(
        body,
        out_shape=jax.tree.map(lambda v: pltpu.HBM(v.shape, v.dtype), out_shape) if name in ("up", "attend", "up_back") else out_shape,
        grid_spec=pltpu.PrefetchScalarGridSpec(
            num_scalar_prefetch=len(scalars),
            grid=grid,
            in_specs=in_specs,
            out_specs=out_specs,
            scratch_shapes=scratch,
        ),
        compiler_params=pltpu.CompilerParams(vmem_limit_bytes=48 << 20),
        cost_estimate=pl.CostEstimate(flops=flops, bytes_accessed=0, transcendentals=0),
        name=name,
    )(*scalars, *operands)
    return clock.then(out)


def shape_of(dims, dtype=BF):
    return jax.ShapeDtypeStruct(tuple(dims), dtype)


def whole(values):
    return pl.BlockSpec(values.shape, lambda *_: (0,) * len(values.shape))


def side_by_side(clock, w):
    half, width = w.shape[1] // 2, w.shape[2]

    def body(w_ref, *refs):
        for i in range(2):
            for c in range(3):
                refs[i][:, c * width : (c + 1) * width] = w_ref[c, i * half : (i + 1) * half, :]

    out = [shape_of((half, 3 * width))] * 2
    return call(
        clock, body, out, (w,), grid=(1,), in_specs=[whole(w)], out_specs=[whole(v) for v in out],
        name="side_by_side",
    )


def times(left, pieces):
    total, start = None, 0
    for ref in pieces:
        part = dot(left[:, start : start + ref.shape[0]], ref[...], 1, 0)
        start += ref.shape[0]
        total = part if total is None else total + part
    return total


def times_turned(left, pieces):
    parts = [dot(left, ref[...], 1, 1) for ref in pieces]
    return parts[0] if len(parts) == 1 else jnp.concatenate(parts, 1)


def split_refs(refs, counts):
    out = []
    for count in counts:
        out.append(refs[:count])
        refs = refs[count:]
    return out


def row_block(values, steps):
    return pl.BlockSpec((values.shape[0] // steps, values.shape[1]), lambda i, *_: (i, 0))


def project(clock, h, w, bias):
    def body(h_ref, bias_ref, *refs):
        refs[-1][...] = (times(h_ref[...], refs[:-1]) + bias_ref[...]).astype(BF)

    bias = bias.reshape(1, -1)
    out = shape_of((h.shape[0], bias.shape[1]))
    return call(
        clock, body, out, (h, bias, *w), grid=(4,), in_specs=[row_block(h, 4), whole(bias)] + [whole(v) for v in w],
        out_specs=row_block(out, 4), name="project",
    )


def attention_out(clock, x, ctx, w, vectors, cost=0):
    count = len(ctx)

    def body(x_ref, *refs):
        ctx_refs, w_refs, (bias_ref, gain_ref, shift_ref), (out_ref, h_ref) = split_refs(refs, (count, count, 3, 2))
        total = x_ref[...].astype(F32) + bias_ref[...]
        for r in range(count):
            total = total + dot(ctx_refs[r][...], w_refs[r][...], 1, 0)
        out_ref[...] = total
        normal, _ = norm_stats(total)
        h_ref[...] = (normal * gain_ref[...] + shift_ref[...]).astype(BF)

    vectors = [v.reshape(1, -1) for v in vectors]
    out = [shape_of(x.shape, F32), shape_of(x.shape)]
    return call(
        clock, body, out, (x, *ctx, *w, *vectors), grid=(4,),
        in_specs=[row_block(v, 4) for v in (x, *ctx)] + [whole(v) for v in (*w, *vectors)],
        out_specs=[row_block(v, 4) for v in out], name="attention_out", flops=cost, plain=True,
    )


def up(clock, h, w, bias, cost=0):
    def body(h_ref, bias_ref, *refs):
        upper = times(h_ref[...], refs[:-2]) + bias_ref[...]
        below = 0.5 * (1.0 + lax.erf(upper * (0.5**0.5)))
        density = jnp.exp(-0.5 * upper * upper) * 0.3989422804014327
        refs[-2][...] = (upper * below).astype(BF)
        refs[-1][...] = (below + upper * density).astype(BF)

    bias = bias.reshape(1, -1)
    out = [shape_of((h.shape[0], bias.shape[1]))] * 2
    return call(
        clock, body, out, (h, bias, *w), grid=(4,), in_specs=[row_block(h, 4), whole(bias)] + [whole(v) for v in w],
        out_specs=[row_block(v, 4) for v in out], name="up", flops=cost,
    )


def to_owner(refs, at, values, scratch, count):
    text, late = pl.program_id(0) // 2, pl.program_id(0) % 2
    part = values.shape[0] * 2 // count
    scratch[...] = values.astype(BF)
    for r in range(count):
        place = at[0] ^ r

        @pl.when(place // (count // 2) == late)
        def _():
            start = pl.multiple_of((place % (count // 2)) * part, part)
            rows = scratch[pl.ds(start, part), :]
            if r < 2:
                refs[r][pl.ds(text, 1)] = rows[None]
            else:
                refs[2][pl.ds(place % 2, 1), pl.ds(text, 1)] = rows[None, None]


def owner_shapes(texts, count, rows, width):
    block = (texts, rows // texts // count, width)
    return [shape_of(block), shape_of(block), shape_of((2, *block))]


def down_out(clock, resid, acts, w, bias, me, texts):
    count = len(acts)
    sizes = [len(pieces) for pieces in w]
    w = [v for pieces in w for v in pieces]
    steps = texts * 2

    def body(at, resid_ref, *refs):
        act_refs, w_refs, (bias_ref,), outs, (scratch,) = split_refs(refs, (count, len(w), 1, 3, 1))
        w_refs = split_refs(w_refs, sizes)
        total = resid_ref[...] + bias_ref[...]
        for r in range(count):
            total = total + times(act_refs[r], w_refs[r])
        to_owner(outs, at, total, scratch, count)

    bias = bias.reshape(1, -1)
    out = owner_shapes(texts, count, *resid.shape)
    return call(
        clock, body, out, (resid, *acts, *w, bias), grid=(steps,),
        in_specs=[row_block(v, steps) for v in (resid, *acts)] + [whole(v) for v in (*w, bias)],
        out_specs=[whole(v) for v in out], scalars=(me.reshape(1),),
        scratch=[pltpu.VMEM((resid.shape[0] // steps, resid.shape[1]), BF)], name="down_out",
    )


def norm_one_back(clock, x, dres, dqkv, w, gain, me, texts):
    count = len(dqkv)
    steps = texts * 2
    sizes = [len(pieces) for pieces in w]
    flat = [v for pieces in w for v in pieces]

    def body(at, x_ref, dres_ref, *refs):
        grads, w_refs, (gain_ref,), outs, (gain_sum, shift_sum, scratch) = split_refs(
            refs, (count, len(flat), 1, 3, 3)
        )
        w_refs = split_refs(w_refs, sizes)
        total = None
        for r in range(count):
            part = times_turned(grads[r][...], w_refs[r])
            total = part if total is None else total + part
        normal, rstd = norm_stats(x_ref[...].astype(F32))

        @pl.when(pl.program_id(0) == 0)
        def _():
            gain_sum[...] = jnp.zeros_like(gain_sum)
            shift_sum[...] = jnp.zeros_like(shift_sum)

        gain_sum[...] += jnp.sum(total * normal, 0, keepdims=True)
        shift_sum[...] += jnp.sum(total, 0, keepdims=True)
        to_owner(outs, at, dres_ref[...] + norm_back(total, normal, rstd, gain_ref[...]), scratch, count)

    gain = gain.reshape(1, -1)
    out = owner_shapes(texts, count, *x.shape) + [shape_of(gain.shape, F32)] * 2
    out = call(
        clock, body, out, (x, dres, *dqkv, *flat, gain), grid=(steps,),
        in_specs=[row_block(v, steps) for v in (x, dres, *dqkv)] + [whole(v) for v in (*flat, gain)],
        out_specs=[whole(v) for v in out], scalars=(me.reshape(1),),
        scratch=[pltpu.VMEM((x.shape[0] // steps, x.shape[1]), BF)], name="norm_one_back",
    )
    return out[:3], out[3], out[4]


def block_of(refs, at, r, i):
    return refs[r][i] if refs[r].ndim == 3 else refs[r][at[0] % 2, i]


def join_norm(clock, blocks, me, gain, shift):
    texts, part, width = blocks[0].shape
    count = len(blocks)

    def body(at, *refs):
        ins, (gain_ref, shift_ref, x_ref, h_ref) = refs[:count], refs[count:]
        for r in range(count):
            for i in range(texts):
                start = pl.multiple_of(i * count * part + (at[0] ^ r) * part, part)
                low = ins[r][i]
                normal, _ = norm_stats(low.astype(F32))
                x_ref[pl.ds(start, part), :] = low
                h_ref[pl.ds(start, part), :] = (normal * gain_ref[...] + shift_ref[...]).astype(BF)

    out = [shape_of((texts * count * part, width))] * 2
    operands = (*blocks, gain.reshape(1, -1), shift.reshape(1, -1))
    return call(
        clock, body, out, operands, grid=(1,), in_specs=[whole(v) for v in operands], out_specs=[whole(v) for v in out],
        scalars=(me.reshape(1),), name="join_norm",
    )


def join_mask(clock, blocks, me, lens):
    texts, part, width = blocks[0].shape
    count = len(blocks)

    def body(at, n, *refs):
        ins, (g_ref, sum_ref) = refs[:count], refs[count:]
        total = jnp.zeros((1, width), F32)
        for r in range(count):
            for i in range(texts):
                place = (at[0] ^ r) * part
                start = pl.multiple_of(i * count * part + place, part)
                live = lax.broadcasted_iota(jnp.int32, (part, width), 0) + place < n[i]
                values = jnp.where(live, block_of(ins, at, r, i).astype(F32), 0.0)
                total = total + jnp.sum(values, 0, keepdims=True)
                g_ref[pl.ds(start, part), :] = values.astype(BF)
        sum_ref[...] = total

    out = [shape_of((texts * count * part, width)), shape_of((1, width), F32)]
    return call(
        clock, body, out, blocks, grid=(1,), in_specs=[whole(v) for v in blocks], out_specs=[whole(v) for v in out],
        scalars=(me.reshape(1), lens), name="join_mask",
    )


def split_texts(clock, values, index, me, texts, stacked):
    count = index.shape[0] // texts
    block = (texts,) + values.shape[1:]

    def body(at, text_at, values_ref, *refs):
        for r in range(count):
            for i in range(texts):
                rows = values_ref[pl.ds(text_at[r * texts + i], 1)]
                if stacked and r >= 2:
                    refs[2][pl.ds((at[0] ^ r) % 2, 1), i : i + 1] = rows[None]
                else:
                    refs[r][i : i + 1] = rows

    out = [shape_of(block)] * 2 + ([shape_of((2, *block))] if stacked else [shape_of(block)] * (count - 2))
    return call(
        clock, body, out, (values,), grid=(1,), in_specs=[whole(values)], out_specs=[whole(v) for v in out],
        scalars=(me.reshape(1), index), name="split_texts",
    )


def join_rows(clock, blocks, me, index):
    texts = blocks[0].shape[0]
    count = len(blocks)

    def body(at, text_at, *refs):
        for r in range(count):
            for i in range(texts):
                refs[count][pl.ds(text_at[r * texts + i], 1)] = block_of(refs, at, r, i)[None]

    out = shape_of((texts * count,) + blocks[0].shape[1:])
    return call(
        clock, body, out, blocks, grid=(1,), in_specs=[whole(v) for v in blocks], out_specs=whole(out),
        scalars=(me.reshape(1), index), name="join_rows",
    )


def up_back(clock, g, ups, downs, slopes, base, resid, gain):
    rows, width = g.shape
    count = len(ups)
    units = slopes[0].shape[1]
    down_sizes = [len(pieces) for pieces in downs]
    downs = [v for pieces in downs for v in pieces]
    sizes = [len(pieces) for pieces in ups]
    flat = [v for pieces in ups for v in pieces]
    last = base is not None

    def body(g_ref, *refs):
        up_refs, down_refs, slope_refs, more, grad_refs, sum_refs, outs = split_refs(
            refs, (len(flat), len(downs), count, 3 if last else 0, count, count, 5 if last else 1)
        )
        up_refs = split_refs(up_refs, sizes)
        down_refs = split_refs(down_refs, down_sizes)
        grad = g_ref[...]
        total = more[0][...] if last else None

        @pl.when(pl.program_id(0) == 0)
        def _():
            for ref in list(sum_refs) + list(outs[2:]):
                ref[...] = jnp.zeros_like(ref)

        for s in range(count):
            upper = times_turned(grad, down_refs[s]) * slope_refs[s][...].astype(F32)
            sum_refs[s][...] += jnp.sum(upper, 0, keepdims=True)
            low = upper.astype(BF)
            grad_refs[s][...] = low
            part = times_turned(low, up_refs[s])
            total = part if total is None else total + part
        if last:
            normal, rstd = norm_stats(more[1][...])
            outs[2][...] += jnp.sum(total * normal, 0, keepdims=True)
            outs[3][...] += jnp.sum(total, 0, keepdims=True)
            total = grad.astype(F32) + norm_back(total, normal, rstd, more[2][...])
            outs[4][...] += jnp.sum(total, 0, keepdims=True)
            outs[1][...] = total.astype(BF)
        outs[0][...] = total

    sums, vector = shape_of((1, units), F32), shape_of((1, width), F32)
    unit = pl.BlockSpec((rows // 4, units), lambda i: (i, 0))
    operands = (g, *flat, *downs, *slopes)
    in_specs = [row_block(g, 4)] + [whole(v) for v in (*flat, *downs)] + [unit] * count
    outs = [shape_of((rows, width), F32)]
    out_specs = [row_block(g, 4)]
    if last:
        gain = gain.reshape(1, -1)
        operands += (base, resid, gain)
        in_specs += [row_block(g, 4)] * 2 + [whole(gain)]
        outs += [shape_of((rows, width))] + [vector] * 3
        out_specs += [row_block(g, 4)] + [whole(vector)] * 3
    out = call(
        clock, body,
        [shape_of((rows, units))] * count + [sums] * count + outs,
        operands,
        grid=(4,),
        in_specs=in_specs,
        out_specs=[unit] * count + [whole(sums)] * count + out_specs,
        name="up_back",
    )
    return list(out[:count]), list(out[count : 2 * count]), out[2 * count :]


def weight_grads(clock, lefts, slots, near=None, split=None, apart=False, pieces=False, extra=None):
    rows, width = lefts[0].shape
    columns = sum(right.shape[1] for _, right in slots[0])
    count = len(slots)
    half = width // 2
    rights = [right for slot in slots for _, right in slot]

    def body(*refs):
        if split is not None:
            at, refs = refs[0], refs[1:]
        left_refs, refs = refs[: len(lefts)], refs[len(lefts) :]
        right_refs, refs = list(refs[: len(rights)]), refs[len(rights) :]
        if near is not None:
            near_refs, refs = refs[: len(near)], refs[len(near) :]
        if extra is not None:
            extra_ref, refs = refs[0], refs[1:]
        for s, slot in enumerate(slots):
            start = 0
            for which, right in slot:
                product = dot(left_refs[which][...], right_refs.pop(0)[...], 0, 0)
                cols = slice(start, start + right.shape[1])
                start = cols.stop
                for i in range(2):
                    low, high = max(cols.start, i * columns // 2), min(cols.stop, (i + 1) * columns // 2)
                    if low < high:
                        here = slice(low - cols.start, high - cols.start)
                        there = slice(low - i * columns // 2, high - i * columns // 2)
                        value = product[:, here]
                        if near is not None:
                            value = value + near_refs[2 * s + i][:, there].astype(F32)
                        if extra is not None:
                            value = value + extra_ref[s, :, low:high].astype(F32)
                        if pieces:
                            refs[2 * s + i][:, there] = value.astype(BF)
                        elif apart:
                            refs[s][0, :, low:high] = value.astype(BF)
                        elif split is None:
                            refs[0][s, :, low:high] = value.astype(BF)
                        else:
                            refs[2][:, low:high] = value
            if split is not None:
                outer, inner = split[0] // 2, width // split[0] // 2
                for a in range(outer):
                    for ref, bit in ((refs[0], 1 - at[0]), (refs[1], at[0])):
                        place = pl.multiple_of((2 * a + bit) * inner, inner)
                        ref[s, a * inner : (a + 1) * inner, :] = refs[2][pl.ds(place, inner), :].astype(BF)

    left = pl.BlockSpec((rows, half), lambda i, *_: (0, i))
    tall = pl.BlockSpec((count, half, columns), lambda i, *_: (0, i, 0))
    narrow = pl.BlockSpec((half, columns // 2), lambda i, *_: (i, 0))
    short = pl.BlockSpec((count, half // 2, columns), lambda i, *_: (0, i, 0))
    operands = (*lefts, *rights) + (() if near is None else tuple(near)) + (() if extra is None else (extra,))
    if pieces:
        out_shape = [shape_of((width, columns // 2))] * (2 * count)
        out_specs = [narrow] * (2 * count)
    elif apart:
        out_shape = [shape_of((1, width, columns))] * count
        out_specs = [pl.BlockSpec((1, half, columns), lambda i, *_: (0, i, 0))] * count
    elif split is None:
        out_shape, out_specs = shape_of((count, width, columns)), tall
    else:
        out_shape, out_specs = [shape_of((count, half, columns))] * 2, [short] * 2
    return call(
        clock, body,
        out_shape,
        operands,
        grid=(2,),
        in_specs=[left] * len(lefts) + [whole(v) for v in rights] + ([] if near is None else [narrow] * len(near)) + ([] if extra is None else [tall]),
        out_specs=out_specs,
        scalars=() if split is None else (split[1].reshape(1),),
        scratch=[] if split is None else [pltpu.VMEM((half, columns), F32)],
        name="weight_grads",
    )


def add_split(clock, keep, arrived, outer, index):
    columns = keep.shape[-1]
    inner = keep.size // columns // outer // 2

    def body(at, keep_ref, arrived_ref, send_ref, out_ref):
        for ref, bit in ((send_ref, 1 - at[0]), (out_ref, at[0])):
            ref[0] = (keep_ref[0, bit].astype(F32) + arrived_ref[0, bit].astype(F32)).astype(BF)

    tall = pl.BlockSpec((1, 2, inner, columns), lambda i, *_: (i, 0, 0, 0))
    short = pl.BlockSpec((1, inner, columns), lambda i, *_: (i, 0, 0))
    return call(
        clock, body,
        [shape_of((outer, inner, columns))] * 2,
        (keep.reshape(outer, 2, inner, columns), arrived.reshape(outer, 2, inner, columns)),
        grid=(outer,),
        in_specs=[tall] * 2,
        out_specs=[short] * 2,
        scalars=(jnp.asarray(index, jnp.int32).reshape(1),),
        name="add_split",
    )


def pack(clock, shared, units, projected, me, cost=0):
    count = len(units)
    first = len(shared)

    def body(at, *refs):
        shared_refs, unit_refs, q_refs, (out_ref,) = split_refs(refs, (first, count, count, 1))
        out_ref[...] = jnp.zeros_like(out_ref)
        for i in range(first):
            out_ref[i : i + 1, :] = shared_refs[i][...]
        for r in range(count):
            width = q_refs[r].shape[1] // 3
            row = pl.ds(first + (at[0] ^ r), 1)
            out_ref[row, : unit_refs[r].shape[1]] = unit_refs[r][...]
            row = pl.ds(first + count + (at[0] ^ r), 1)
            out_ref[row, :width] = q_refs[r][:, :width]
            out_ref[row, width : 2 * width] = q_refs[r][:, 2 * width :]

    out = shape_of((first + 2 * count, max(D, units[0].shape[1])), F32)
    operands = (*shared, *units, *projected)
    return call(
        clock, body, out, operands, grid=(1,), in_specs=[whole(v) for v in operands], out_specs=whole(out),
        scalars=(me.reshape(1),), name="pack", flops=cost,
    )


def attend_body(lens, *refs, step, heads):
    ins, outs, (p_ref, inv_ref) = refs[:2], refs[2:4], refs[4:]
    n = lens[pl.program_id(0)]
    length = ins[0].shape[0]
    width = heads * HD

    def rows(live):
        edge = lax.broadcasted_iota(jnp.int32, (step, length), 0) < n - (live - step)
        for which in range(2):
            ref, ctx_ref = ins[which], outs[which]
            for head in range(heads):
                slot = which * heads + head
                cols = slice(head * HD, head * HD + HD)
                keys = ref[:live, width + head * HD : width + head * HD + HD]
                values = ref[:live, 2 * width + head * HD : 2 * width + head * HD + HD]
                scores = dot(keys, ref[:, cols], 1, 1)
                last = jnp.where(edge, scores[live - step :], -1e30)
                if live > step:
                    scores = jnp.concatenate([scores[: live - step], last], 0)
                else:
                    scores = last
                top = jnp.max(scores, 0, keepdims=True)
                power = jnp.exp2((scores - top) * (SCALE * LOG2E))
                inverse = 1.0 / jnp.sum(power, 0, keepdims=True)
                low = power.astype(BF)
                p_ref[0, slot, :live, :] = low
                inv_ref[0, slot : slot + 1, :] = inverse
                mixed = dot(low, values, 0, 0)
                ctx_ref[:, cols] = (mixed * inverse.reshape(length, 1)).astype(BF)

    for live in range(step, length + 1, step):
        pl.when((n > live - step) & (n <= live))(functools.partial(rows, live))


def attend_back_body(lens, *refs, step, heads):
    ins, (grad_ref,), w_refs, (p_ref, inv_ref) = refs[:2], refs[2:3], refs[3:5], refs[5:7]
    outs, sums, do_ref = refs[7:9], refs[9:11], refs[11]
    n = lens[pl.program_id(0)]
    length = ins[0].shape[0]
    width = heads * HD

    def rows(live):
        for which in range(2):
            ref, out_ref = ins[which], outs[which]
            do_ref[:live, :] = dot(grad_ref[:live, :], w_refs[which][...], 1, 1)
            for head in range(heads):
                slot = which * heads + head
                at = [slice(c * width + head * HD, c * width + head * HD + HD) for c in range(3)]
                inverse = inv_ref[0, slot : slot + 1, :live]
                grad = (do_ref[:live, at[0]] * inverse.reshape(live, 1)).astype(BF)
                low = p_ref[0, slot, :live, :live]
                grad_probs = dot(ref[:live, at[2]], grad, 1, 1)
                power = low.astype(F32)
                product = power * grad_probs
                inner = jnp.sum(product, 0, keepdims=True) * inverse
                grad_scores = (product - power * inner).astype(BF)
                out_ref[:live, at[2]] = dot(low, grad, 1, 0).astype(BF)
                out_ref[:live, at[1]] = (dot(grad_scores, ref[:live, at[0]], 1, 0) * SCALE).astype(BF)
                out_ref[:live, at[0]] = (dot(grad_scores, ref[:live, at[1]], 0, 0) * SCALE).astype(BF)
            if live < length:
                out_ref[live:, :] = jnp.zeros((length - live, 3 * width), BF)
            sums[which][...] += jnp.sum(out_ref[:live, :].astype(F32), 0, keepdims=True)

    @pl.when(pl.program_id(0) == 0)
    def _():
        for ref in sums:
            ref[...] = jnp.zeros_like(ref)

    for live in range(step, length + 1, step):
        pl.when((n > live - step) & (n <= live))(functools.partial(rows, live))


def attend_call(clock, lens, qkv, back, length, cost=0):
    texts = lens.shape[0]
    width = qkv[0].shape[1] // 3
    heads = width // HD
    wide = pl.BlockSpec((length, 3 * width), lambda i, *_: (i, 0))
    slim = pl.BlockSpec((length, width), lambda i, *_: (i, 0))
    full = pl.BlockSpec((length, D), lambda i, *_: (i, 0))
    probs = pl.BlockSpec((1, 2 * heads, length, length), lambda i, *_: (i, 0, 0, 0))
    inverse = pl.BlockSpec((1, 2 * heads, length), lambda i, *_: (i, 0, 0))
    rows = texts * length
    if back is None:
        return call(
            clock,
            functools.partial(attend_body, step=length // 4, heads=heads),
            [shape_of((rows, width))] * 2
            + [shape_of((texts, 2 * heads, length, length)), shape_of((texts, 2 * heads, length), F32)],
            tuple(qkv),
            grid=(texts,),
            in_specs=[wide] * 2,
            out_specs=[slim] * 2 + [probs, inverse],
            scalars=(lens,),
            name="attend",
            flops=cost,
        )
    return call(
        clock,
        functools.partial(attend_back_body, step=length // 4, heads=heads),
        [shape_of((rows, 3 * width))] * 2 + [shape_of((1, 3 * width), F32)] * 2,
        tuple(qkv) + tuple(back),
        grid=(texts,),
        in_specs=[wide] * 2 + [full] + [whole(w) for w in back[1:3]] + [probs, inverse],
        out_specs=[wide] * 2 + [pl.BlockSpec((1, 3 * width), lambda i, *_: (0, 0))] * 2,
        scalars=(lens,),
        scratch=[pltpu.VMEM((length, width), F32)],
        name="attend_back",
    )


COST_FAR, COST_OUT, COST_END = 14 * 10**9, 6 * 10**9, 7 * 10**9


def program(dp_size, tensor_size):
    bits = dp_size.bit_length() - 1

    def pp_tensor(values, flip):
        return lax.ppermute(values, "tensor", [(i, i ^ flip) for i in range(tensor_size)])

    def pp_dp(values, bit):
        return lax.ppermute(values, "dp", [(i, i ^ (1 << bit)) for i in range(dp_size)])

    def on_device(
        inputs,
        lengths,
        cotangent,
        ln1_gain,
        ln1_bias,
        w_qkv,
        b_qv,
        w_out,
        b_out,
        ln2_gain,
        ln2_bias,
        w_up,
        b_up,
        w_down,
        b_down,
    ):
        t = lax.axis_index("tensor")
        d = lax.axis_index("dp")
        texts_all, part = inputs.shape[:2]
        texts = texts_all // tensor_size
        length = part * tensor_size
        rows = texts * length
        rels = range(tensor_size)
        local = w_qkv.shape[2]
        units = b_up.shape[0]
        inner = D // dp_size
        bit_of = [(d >> b) & 1 for b in range(bits)]
        clock = Clock()
        chains = []

        def pick(values, index, axis):
            return lax.dynamic_index_in_dim(values, index, axis, keepdims=False)

        number = jnp.arange(texts_all)
        ahead = (lengths[None] > lengths[:, None]) | (
            (lengths[None] == lengths[:, None]) & (number[None] < number[:, None])
        )
        rank = jnp.sum(ahead, 1)
        dealt = []
        for r in rels:
            for i in range(texts):
                dealt.append(i * tensor_size + ((t ^ r) if i % 2 == 0 else tensor_size - 1 - (t ^ r)))
        text_at = jnp.sum(jnp.where(rank[None] == jnp.stack(dealt)[:, None], number[None], 0), 1).astype(jnp.int32)
        lens = jnp.sum(jnp.where(rank[None] == jnp.stack(dealt[:texts])[:, None], lengths[None], 0), 1).astype(jnp.int32)

        def exchange(blocks):
            far = {r: pp_tensor(blocks[r], r) for r in (3, 2, 1)}
            return [blocks[0]] + [far[r] for r in (1, 2, 3)]

        class Exchange:
            def __init__(self, own, near, far):
                self.own, self.near, self.far = own, near, pp_tensor(far, 2)

            def forward(self):
                self.far = clock.after(self.far)
                self.near = pp_tensor(clock.after(self.near), 1)
                self.last = pp_tensor(pick(self.far, 1 - t % 2, 0), 1)

            def blocks(self):
                return [self.own, clock.after(self.near), self.far, clock.after(self.last)]

        class Chain:
            def __init__(self, lefts, slots, near, steps, extra=None):
                self.steps = list(steps)
                self.dims = [len(slots)] + [2] * bits
                step = self.steps.pop(0)
                outer, index = self.place(step)
                if step == "y":
                    self.keep, self.sent = weight_grads(clock, lefts, slots, near, apart=True)
                elif inner % 16 == 0 and outer > len(slots):
                    split = (outer // len(slots), index)
                    self.sent, self.keep = weight_grads(clock, lefts, slots, near, split, extra=extra)
                else:
                    total = weight_grads(clock, lefts, slots, near, extra=extra)
                    self.sent, self.keep = self.halves(total, outer, index)
                self.fly(step)

            def place(self, step):
                axis = 0 if step == "y" else bits - step
                outer = 1
                for size in self.dims[:axis]:
                    outer *= size
                self.dims[axis] = 1
                return outer, 0 * t if step == "y" else bit_of[step]

            def halves(self, total, outer, index):
                view = total.reshape(outer, 2, -1, total.shape[-1])
                return pick(view, 1 - index, 1), pick(view, index, 1)

            def fly(self, step):
                self.flight = pp_tensor(self.sent, 2) if step == "y" else pp_dp(self.sent, step)

            def step(self):
                arrived = clock.after(self.flight)
                step = self.steps.pop(0)
                outer, index = self.place(step)
                if inner % 16 == 0:
                    self.sent, self.keep = add_split(clock, self.keep, arrived, outer, index)
                else:
                    total = (self.keep.astype(F32) + arrived.astype(F32)).astype(BF)
                    self.sent, self.keep = self.halves(total, outer, index)
                self.fly(step)

            def last(self):
                total = self.keep.astype(F32) + clock.after(self.flight).astype(F32)
                return total.reshape(-1, total.shape[-1])

        high = list(range(2, bits))

        always = (lengths[0] | 1) != 0

        def block(steps, *operands):
            operands = (clock.after(operands[0]),) + operands[1:]

            def run(*values):
                clock.last = None
                return steps(*values)

            saved = [(list(chain.steps), list(chain.dims)) for chain in chains]
            shapes = jax.eval_shape(lambda *v: run(*v), *operands)
            for chain, (left, dims) in zip(chains, saved):
                chain.steps, chain.dims = left, dims
            out = lax.cond(
                always, run, lambda *_: jax.tree.map(lambda v: jnp.zeros(v.shape, v.dtype), shapes), *operands
            )
            clock.last = None
            return clock.then(out)

        def from_near(lefts, slots):
            return [pp_tensor(v, 1) for v in weight_grads(clock, lefts, slots, pieces=True)]

        x_own = split_texts(clock, inputs, text_at, t, texts, False)
        x_blocks = exchange(x_own)
        wq_own = side_by_side(clock, tie(w_qkv, *x_own[1:]))
        wq_near = [pp_tensor(v, 1) for v in wq_own]
        wo_near = pp_tensor(tie(w_out, x_blocks[1]), 1)
        small = jnp.concatenate([b_qv.reshape(-1), tie(b_up, x_blocks[1])])
        small = jnp.stack([small, pp_tensor(small, 1)])
        small = list(small) + list(pp_tensor(small, 2))
        bqkv = [
            jnp.concatenate([s[:local], jnp.zeros((local,), F32), s[local : 2 * local]]) for s in small
        ]
        bup = [s[2 * local :] for s in small]


        x_blocks[0] = tie(x_blocks[0], wo_near, *wq_near)
        wq_far = [pp_tensor(tie(v, x_blocks[3]), 2) for v in wq_own]
        cut = w_up.shape[0] // 2
        up_first, up_second = jnp.concatenate([w_up[:cut], w_out], 0), w_up[cut:]
        first_far, second_far = [pp_tensor(tie(v, x_blocks[3]), 2) for v in (up_first, up_second)]
        cot = Exchange(*split_texts(clock, tie(cotangent, x_blocks[1]), text_at, t, texts, True))
        wd_far = pp_tensor(tie(w_down, x_blocks[3]), 2)
        x, h1 = join_norm(clock, x_blocks, t, ln1_gain, ln1_bias)
        wq = [wq_own, wq_near]
        qkv = [project(clock, h1, wq[r], bqkv[r]) for r in (0, 1)]
        attn_a = attend_call(clock, lens, qkv[:2], None, length)
        wq_far = [clock.after(v) for v in wq_far]

        def project_far(values):
            passed = [pp_tensor(v, 1) for v in wq_far]
            ups, downs = pp_tensor(w_up, 1), pp_tensor(w_down, 1)
            return passed, project(clock, values, wq_far, bqkv[2]), ups, downs

        passed, q_first, wu_near, wd_near = block(project_far, h1)
        wq += [wq_far, passed]
        qkv += [q_first, project(clock, h1, wq[3], bqkv[3])]
        attn_b = attend_call(clock, lens, qkv[2:], None, length, COST_FAR)
        first_far = clock.after(first_far)
        wo_far = first_far[cut:]
        wo = [w_out, wo_near, wo_far, pp_tensor(wo_far, 1)]
        ctx = [attn_a[0], attn_a[1], attn_b[0], attn_b[1]]
        resid, h2 = attention_out(clock, x, ctx, wo, (b_out, ln2_gain, ln2_bias))
        ups = [up(clock, h2, [w_up], bup[0])]
        wu_far = [first_far[:cut], clock.after(second_far)]
        wu = [[w_up], [wu_near], wu_far, [pp_tensor(v, 1) for v in wu_far]]
        ups.append(up(clock, h2, wu[1], bup[1], COST_OUT))
        cot.forward()
        ups.append(up(clock, h2, wu[3], bup[3]))
        g_low, bias_down = join_mask(clock, cot.blocks(), t, lens)

        near = from_near([g_low], [[(0, ups[1][0])], [(0, ups[2][0])]])
        ups.insert(2, up(clock, h2, wu[2], bup[2]))
        acts, slopes = [u[0] for u in ups], [u[1] for u in ups]
        down = Chain([g_low], [[(0, acts[0])], [(0, acts[2])]], near, ["y", 0, 1] + high)
        wd_far = clock.after(wd_far)
        wd = [[w_down], [wd_near], [wd_far], [pp_tensor(wd_far, 1)]]
        dups_a, sums_a, dh2 = up_back(clock, g_low, wu[:2], wd[:2], slopes[:2], None, None, None)
        dups_b, sums_b, rest = up_back(clock, g_low, wu[2:], wd[2:], slopes[2:], dh2[0], resid, ln2_gain)
        dres, dres_low, gain_two, shift_two, bias_attn = rest
        dups, bias_up = dups_a + dups_b, sums_a + sums_b
        up_near = from_near([h2], [[(0, dups[1])], [(0, dups[3])]])
        down.step()
        grads_up = Chain([h2], [[(0, dups[0])], [(0, dups[2])]], up_near, ["y", 0, 1] + high)
        back = attend_call(clock, lens, qkv[2:], [dres_low] + wo[2:] + list(attn_b[2:]), length)
        dqkv_far, qkv_sums_far = back[:2], back[2:]
        near = from_near([h1, dres_low], [[(0, dqkv_far[1]), (1, ctx[3])]])
        down.step()
        q_far = weight_grads(clock, [h1, dres_low], [[(0, dqkv_far[0]), (1, ctx[2])]], near)
        q_far = pp_tensor(q_far, 2)
        back = attend_call(clock, lens, qkv[:2], [dres_low] + wo[:2] + list(attn_a[2:]), length)
        dqkv, qkv_sums = list(back[:2]) + list(dqkv_far), list(back[2:]) + list(qkv_sums_far)
        grads_up.step()
        for bit in high:
            down.step()
        near = from_near([h1, dres_low], [[(0, dqkv[1]), (1, ctx[1])]])
        out = Exchange(*down_out(clock, resid, acts, wd, b_down, t, texts))
        grad_down = clock.then(down.last())
        grads_up.step()
        q_own = Chain([h1, dres_low], [[(0, dqkv[0]), (1, ctx[0])]], near, [1, 0] + high, clock.after(q_far))
        in_blocks, gain_one, shift_one = norm_one_back(clock, x, dres, dqkv, wq, ln1_gain, t, texts)
        gin = Exchange(*in_blocks)
        shared = [gain_one, shift_one, gain_two, shift_two, bias_attn, bias_down]
        out.forward()
        chains += [grads_up, q_own]
        for chain in chains:
            chain.flight = clock.then(clock.after(chain.flight))
        total = pack(clock, shared, bias_up, qkv_sums, t, COST_END)
        out_blocks = out.blocks()

        def moved(values, flip, tensor):
            flight = pp_tensor(values, flip) if tensor else pp_dp(values, flip)
            return clock.then(values + clock.after(flight))

        def load(state):
            for chain, (keep, flight) in zip(chains, state):
                chain.keep, chain.flight = keep, flight

        def begin(total, state):
            load(state)
            for bit in high[:1]:
                grads_up.step()
            q_own.step()
            total = moved(total, 1, True)
            for bit in (1, 0)[-bits:]:
                total = moved(total, bit, False)
            return total, [(chain.keep, clock.after(chain.flight)) for chain in chains]

        def finish(total, state, blocks):
            load(state)
            for bit in high[1:]:
                grads_up.step()
            grad_up = clock.then(grads_up.last())
            for bit in high:
                q_own.step()
                total = moved(total, bit, False)
            total = moved(total, 2, True)
            rows_out = join_rows(clock, blocks, t, text_at)
            first = len(shared)
            vectors = [total[i] for i in range(first)]
            vectors.append(lax.dynamic_slice_in_dim(total, first + t, 1)[0, :units])
            qv = lax.dynamic_slice_in_dim(total, first + tensor_size + t, 1)[0, : 2 * local]
            vectors.append(qv.reshape(2, local))
            both = q_own.last()
            weights = jnp.stack([both[:, c * local : c * local + local] for c in range(3)])
            return rows_out, vectors, grad_up, weights, both[:, 3 * local :].T

        state = [(chain.keep, chain.flight) for chain in chains]
        total, state = block(begin, total, state)
        gin.forward()
        layer_out, vector, grad_up, grad_qkv, grad_out = block(finish, total, state, out_blocks)
        grad_input = join_rows(clock, gin.blocks(), t, text_at)
        return (
            layer_out,
            grad_input,
            vector[0],
            vector[1],
            grad_qkv,
            vector[7],
            grad_out,
            vector[4],
            vector[2],
            vector[3],
            grad_up,
            vector[6],
            grad_down.T,
            vector[5],
        )

    return on_device


def solution(mesh):
    return jax.shard_map(
        program(mesh.shape["dp"], mesh.shape["tensor"]),
        mesh=mesh,
        in_specs=(
            P("dp", "tensor", None),
            P("dp"),
            P("dp", "tensor", None),
            P(),
            P(),
            P(None, None, "tensor"),
            P(None, "tensor"),
            P("tensor", None),
            P(),
            P(),
            P(),
            P(None, "tensor"),
            P("tensor"),
            P("tensor", None),
            P(),
        ),
        out_specs=(
            P("dp", "tensor", None),
            P("dp", "tensor", None),
            P(),
            P(),
            P(None, "dp", "tensor"),
            P(None, "tensor"),
            P("tensor", "dp"),
            P(),
            P(),
            P(),
            P("dp", "tensor"),
            P("tensor"),
            P("tensor", "dp"),
            P(),
        ),
        check_vma=False,
    )
```

```python
import functools

import jax
import jax.numpy as jnp
from jax import lax
from jax.experimental import pallas as pl
from jax.experimental.pallas import tpu as pltpu
from jax.sharding import PartitionSpec as P

D = 768
HD = 64
BF = jnp.bfloat16
F32 = jnp.float32
SCALE = HD**-0.5
LOG2E = 1.4426950408889634


def dot(left, right, left_dim, right_dim):
    return lax.dot_general(
        left, right, (((left_dim,), (right_dim,)), ((), ())), preferred_element_type=F32
    )


def norm_stats(values):
    center = values - jnp.mean(values, -1, keepdims=True)
    rstd = lax.rsqrt(jnp.mean(center * center, -1, keepdims=True) + 1e-05)
    return center * rstd, rstd


def norm_back(grad_norm, normal, rstd, gain):
    scaled = grad_norm * gain
    return rstd * (
        scaled
        - jnp.mean(scaled, -1, keepdims=True)
        - normal * jnp.mean(scaled * normal, -1, keepdims=True)
    )


class Clock:
    def __init__(self):
        self.last = None

    def after(self, values):
        return values if self.last is None else tie(values, self.last)

    def then(self, values):
        self.last = jax.tree.leaves(values)[0]
        return values


def tie(value, *waits):
    return lax.optimization_barrier((value,) + waits)[0]


def call(clock, body, out_shape, operands, *, grid=(), in_specs=None, out_specs=None, scalars=(), scratch=(),
         name=None, flops=0, plain=False):
    operands = (clock.after(operands[0]),) + tuple(operands[1:])
    if plain:
        operands = [pltpu.with_memory_space_constraint(v, pltpu.HBM) for v in operands]
    out = pl.pallas_call(
        body,
        out_shape=jax.tree.map(lambda v: pltpu.HBM(v.shape, v.dtype), out_shape) if name in ("up", "attend", "up_back") else out_shape,
        grid_spec=pltpu.PrefetchScalarGridSpec(
            num_scalar_prefetch=len(scalars),
            grid=grid,
            in_specs=in_specs,
            out_specs=out_specs,
            scratch_shapes=scratch,
        ),
        compiler_params=pltpu.CompilerParams(vmem_limit_bytes=48 << 20),
        cost_estimate=pl.CostEstimate(flops=flops, bytes_accessed=0, transcendentals=0),
        name=name,
    )(*scalars, *operands)
    return clock.then(out)


def shape_of(dims, dtype=BF):
    return jax.ShapeDtypeStruct(tuple(dims), dtype)


def whole(values):
    return pl.BlockSpec(values.shape, lambda *_: (0,) * len(values.shape))


def side_by_side(clock, w):
    half, width = w.shape[1] // 2, w.shape[2]

    def body(w_ref, *refs):
        for i in range(2):
            for c in range(3):
                refs[i][:, c * width : (c + 1) * width] = w_ref[c, i * half : (i + 1) * half, :]

    out = [shape_of((half, 3 * width))] * 2
    return call(
        clock, body, out, (w,), grid=(1,), in_specs=[whole(w)], out_specs=[whole(v) for v in out],
        name="side_by_side",
    )


def times(left, pieces):
    total, start = None, 0
    for ref in pieces:
        part = dot(left[:, start : start + ref.shape[0]], ref[...], 1, 0)
        start += ref.shape[0]
        total = part if total is None else total + part
    return total


def times_turned(left, pieces):
    parts = [dot(left, ref[...], 1, 1) for ref in pieces]
    return parts[0] if len(parts) == 1 else jnp.concatenate(parts, 1)


def split_refs(refs, counts):
    out = []
    for count in counts:
        out.append(refs[:count])
        refs = refs[count:]
    return out


def row_block(values, steps):
    return pl.BlockSpec((values.shape[0] // steps, values.shape[1]), lambda i, *_: (i, 0))


def project(clock, h, w, bias):
    def body(h_ref, bias_ref, *refs):
        refs[-1][...] = (times(h_ref[...], refs[:-1]) + bias_ref[...]).astype(BF)

    bias = bias.reshape(1, -1)
    out = shape_of((h.shape[0], bias.shape[1]))
    return call(
        clock, body, out, (h, bias, *w), grid=(4,), in_specs=[row_block(h, 4), whole(bias)] + [whole(v) for v in w],
        out_specs=row_block(out, 4), name="project",
    )


def attention_out(clock, x, ctx, w, vectors, cost=0):
    count = len(ctx)

    def body(x_ref, *refs):
        ctx_refs, w_refs, (bias_ref, gain_ref, shift_ref), (out_ref, h_ref) = split_refs(refs, (count, count, 3, 2))
        total = x_ref[...].astype(F32) + bias_ref[...]
        for r in range(count):
            total = total + dot(ctx_refs[r][...], w_refs[r][...], 1, 0)
        out_ref[...] = total
        normal, _ = norm_stats(total)
        h_ref[...] = (normal * gain_ref[...] + shift_ref[...]).astype(BF)

    vectors = [v.reshape(1, -1) for v in vectors]
    out = [shape_of(x.shape, F32), shape_of(x.shape)]
    return call(
        clock, body, out, (x, *ctx, *w, *vectors), grid=(4,),
        in_specs=[row_block(v, 4) for v in (x, *ctx)] + [whole(v) for v in (*w, *vectors)],
        out_specs=[row_block(v, 4) for v in out], name="attention_out", flops=cost, plain=True,
    )


def up(clock, h, w, bias, cost=0):
    def body(h_ref, bias_ref, *refs):
        upper = times(h_ref[...], refs[:-2]) + bias_ref[...]
        below = 0.5 * (1.0 + lax.erf(upper * (0.5**0.5)))
        density = jnp.exp(-0.5 * upper * upper) * 0.3989422804014327
        refs[-2][...] = (upper * below).astype(BF)
        refs[-1][...] = (below + upper * density).astype(BF)

    bias = bias.reshape(1, -1)
    out = [shape_of((h.shape[0], bias.shape[1]))] * 2
    return call(
        clock, body, out, (h, bias, *w), grid=(4,), in_specs=[row_block(h, 4), whole(bias)] + [whole(v) for v in w],
        out_specs=[row_block(v, 4) for v in out], name="up", flops=cost,
    )


def to_owner(refs, at, values, scratch, count):
    text, late = pl.program_id(0) // 2, pl.program_id(0) % 2
    part = values.shape[0] * 2 // count
    scratch[...] = values.astype(BF)
    for r in range(count):
        place = at[0] ^ r

        @pl.when(place // (count // 2) == late)
        def _():
            start = pl.multiple_of((place % (count // 2)) * part, part)
            rows = scratch[pl.ds(start, part), :]
            if r < 2:
                refs[r][pl.ds(text, 1)] = rows[None]
            else:
                refs[2][pl.ds(place % 2, 1), pl.ds(text, 1)] = rows[None, None]


def owner_shapes(texts, count, rows, width):
    block = (texts, rows // texts // count, width)
    return [shape_of(block), shape_of(block), shape_of((2, *block))]


def down_out(clock, resid, acts, w, bias, me, texts):
    count = len(acts)
    sizes = [len(pieces) for pieces in w]
    w = [v for pieces in w for v in pieces]
    steps = texts * 2

    def body(at, resid_ref, *refs):
        act_refs, w_refs, (bias_ref,), outs, (scratch,) = split_refs(refs, (count, len(w), 1, 3, 1))
        w_refs = split_refs(w_refs, sizes)
        total = resid_ref[...] + bias_ref[...]
        for r in range(count):
            total = total + times(act_refs[r], w_refs[r])
        to_owner(outs, at, total, scratch, count)

    bias = bias.reshape(1, -1)
    out = owner_shapes(texts, count, *resid.shape)
    return call(
        clock, body, out, (resid, *acts, *w, bias), grid=(steps,),
        in_specs=[row_block(v, steps) for v in (resid, *acts)] + [whole(v) for v in (*w, bias)],
        out_specs=[whole(v) for v in out], scalars=(me.reshape(1),),
        scratch=[pltpu.VMEM((resid.shape[0] // steps, resid.shape[1]), BF)], name="down_out",
    )


def norm_one_back(clock, x, dres, dqkv, w, gain, me, texts):
    count = len(dqkv)
    steps = texts * 2
    sizes = [len(pieces) for pieces in w]
    flat = [v for pieces in w for v in pieces]

    def body(at, x_ref, dres_ref, *refs):
        grads, w_refs, (gain_ref,), outs, (gain_sum, shift_sum, scratch) = split_refs(
            refs, (count, len(flat), 1, 3, 3)
        )
        w_refs = split_refs(w_refs, sizes)
        total = None
        for r in range(count):
            part = times_turned(grads[r][...], w_refs[r])
            total = part if total is None else total + part
        normal, rstd = norm_stats(x_ref[...].astype(F32))

        @pl.when(pl.program_id(0) == 0)
        def _():
            gain_sum[...] = jnp.zeros_like(gain_sum)
            shift_sum[...] = jnp.zeros_like(shift_sum)

        gain_sum[...] += jnp.sum(total * normal, 0, keepdims=True)
        shift_sum[...] += jnp.sum(total, 0, keepdims=True)
        to_owner(outs, at, dres_ref[...] + norm_back(total, normal, rstd, gain_ref[...]), scratch, count)

    gain = gain.reshape(1, -1)
    out = owner_shapes(texts, count, *x.shape) + [shape_of(gain.shape, F32)] * 2
    out = call(
        clock, body, out, (x, dres, *dqkv, *flat, gain), grid=(steps,),
        in_specs=[row_block(v, steps) for v in (x, dres, *dqkv)] + [whole(v) for v in (*flat, gain)],
        out_specs=[whole(v) for v in out], scalars=(me.reshape(1),),
        scratch=[pltpu.VMEM((x.shape[0] // steps, x.shape[1]), BF)], name="norm_one_back",
    )
    return out[:3], out[3], out[4]


def block_of(refs, at, r, i):
    return refs[r][i] if refs[r].ndim == 3 else refs[r][at[0] % 2, i]


def join_norm(clock, blocks, me, gain, shift):
    texts, part, width = blocks[0].shape
    count = len(blocks)

    def body(at, *refs):
        ins, (gain_ref, shift_ref, x_ref, h_ref) = refs[:count], refs[count:]
        for r in range(count):
            for i in range(texts):
                start = pl.multiple_of(i * count * part + (at[0] ^ r) * part, part)
                low = ins[r][i]
                normal, _ = norm_stats(low.astype(F32))
                x_ref[pl.ds(start, part), :] = low
                h_ref[pl.ds(start, part), :] = (normal * gain_ref[...] + shift_ref[...]).astype(BF)

    out = [shape_of((texts * count * part, width))] * 2
    operands = (*blocks, gain.reshape(1, -1), shift.reshape(1, -1))
    return call(
        clock, body, out, operands, grid=(1,), in_specs=[whole(v) for v in operands], out_specs=[whole(v) for v in out],
        scalars=(me.reshape(1),), name="join_norm",
    )


def join_mask(clock, blocks, me, lens):
    texts, part, width = blocks[0].shape
    count = len(blocks)

    def body(at, n, *refs):
        ins, (g_ref, sum_ref) = refs[:count], refs[count:]
        total = jnp.zeros((1, width), F32)
        for r in range(count):
            for i in range(texts):
                place = (at[0] ^ r) * part
                start = pl.multiple_of(i * count * part + place, part)
                live = lax.broadcasted_iota(jnp.int32, (part, width), 0) + place < n[i]
                values = jnp.where(live, block_of(ins, at, r, i).astype(F32), 0.0)
                total = total + jnp.sum(values, 0, keepdims=True)
                g_ref[pl.ds(start, part), :] = values.astype(BF)
        sum_ref[...] = total

    out = [shape_of((texts * count * part, width)), shape_of((1, width), F32)]
    return call(
        clock, body, out, blocks, grid=(1,), in_specs=[whole(v) for v in blocks], out_specs=[whole(v) for v in out],
        scalars=(me.reshape(1), lens), name="join_mask",
    )


def split_texts(clock, values, index, me, texts, stacked):
    count = index.shape[0] // texts
    block = (texts,) + values.shape[1:]

    def body(at, text_at, values_ref, *refs):
        for r in range(count):
            for i in range(texts):
                rows = values_ref[pl.ds(text_at[r * texts + i], 1)]
                if stacked and r >= 2:
                    refs[2][pl.ds((at[0] ^ r) % 2, 1), i : i + 1] = rows[None]
                else:
                    refs[r][i : i + 1] = rows

    out = [shape_of(block)] * 2 + ([shape_of((2, *block))] if stacked else [shape_of(block)] * (count - 2))
    return call(
        clock, body, out, (values,), grid=(1,), in_specs=[whole(values)], out_specs=[whole(v) for v in out],
        scalars=(me.reshape(1), index), name="split_texts",
    )


def join_rows(clock, blocks, me, index):
    texts = blocks[0].shape[0]
    count = len(blocks)

    def body(at, text_at, *refs):
        for r in range(count):
            for i in range(texts):
                refs[count][pl.ds(text_at[r * texts + i], 1)] = block_of(refs, at, r, i)[None]

    out = shape_of((texts * count,) + blocks[0].shape[1:])
    return call(
        clock, body, out, blocks, grid=(1,), in_specs=[whole(v) for v in blocks], out_specs=whole(out),
        scalars=(me.reshape(1), index), name="join_rows",
    )


def up_back(clock, g, ups, downs, slopes, base, resid, gain):
    rows, width = g.shape
    count = len(ups)
    units = slopes[0].shape[1]
    down_sizes = [len(pieces) for pieces in downs]
    downs = [v for pieces in downs for v in pieces]
    sizes = [len(pieces) for pieces in ups]
    flat = [v for pieces in ups for v in pieces]
    last = base is not None

    def body(g_ref, *refs):
        up_refs, down_refs, slope_refs, more, grad_refs, sum_refs, outs = split_refs(
            refs, (len(flat), len(downs), count, 3 if last else 0, count, count, 5 if last else 1)
        )
        up_refs = split_refs(up_refs, sizes)
        down_refs = split_refs(down_refs, down_sizes)
        grad = g_ref[...]
        total = more[0][...] if last else None

        @pl.when(pl.program_id(0) == 0)
        def _():
            for ref in list(sum_refs) + list(outs[2:]):
                ref[...] = jnp.zeros_like(ref)

        for s in range(count):
            upper = times_turned(grad, down_refs[s]) * slope_refs[s][...].astype(F32)
            sum_refs[s][...] += jnp.sum(upper, 0, keepdims=True)
            low = upper.astype(BF)
            grad_refs[s][...] = low
            part = times_turned(low, up_refs[s])
            total = part if total is None else total + part
        if last:
            normal, rstd = norm_stats(more[1][...])
            outs[2][...] += jnp.sum(total * normal, 0, keepdims=True)
            outs[3][...] += jnp.sum(total, 0, keepdims=True)
            total = grad.astype(F32) + norm_back(total, normal, rstd, more[2][...])
            outs[4][...] += jnp.sum(total, 0, keepdims=True)
            outs[1][...] = total.astype(BF)
        outs[0][...] = total

    sums, vector = shape_of((1, units), F32), shape_of((1, width), F32)
    unit = pl.BlockSpec((rows // 4, units), lambda i: (i, 0))
    operands = (g, *flat, *downs, *slopes)
    in_specs = [row_block(g, 4)] + [whole(v) for v in (*flat, *downs)] + [unit] * count
    outs = [shape_of((rows, width), F32)]
    out_specs = [row_block(g, 4)]
    if last:
        gain = gain.reshape(1, -1)
        operands += (base, resid, gain)
        in_specs += [row_block(g, 4)] * 2 + [whole(gain)]
        outs += [shape_of((rows, width))] + [vector] * 3
        out_specs += [row_block(g, 4)] + [whole(vector)] * 3
    out = call(
        clock, body,
        [shape_of((rows, units))] * count + [sums] * count + outs,
        operands,
        grid=(4,),
        in_specs=in_specs,
        out_specs=[unit] * count + [whole(sums)] * count + out_specs,
        name="up_back",
    )
    return list(out[:count]), list(out[count : 2 * count]), out[2 * count :]


def weight_grads(clock, lefts, slots, near=None, split=None, apart=False, pieces=False, extra=None):
    rows, width = lefts[0].shape
    columns = sum(right.shape[1] for _, right in slots[0])
    count = len(slots)
    half = width // 2
    rights = [right for slot in slots for _, right in slot]

    def body(*refs):
        if split is not None:
            at, refs = refs[0], refs[1:]
        left_refs, refs = refs[: len(lefts)], refs[len(lefts) :]
        right_refs, refs = list(refs[: len(rights)]), refs[len(rights) :]
        if near is not None:
            near_refs, refs = refs[: len(near)], refs[len(near) :]
        if extra is not None:
            extra_ref, refs = refs[0], refs[1:]
        for s, slot in enumerate(slots):
            start = 0
            for which, right in slot:
                product = dot(left_refs[which][...], right_refs.pop(0)[...], 0, 0)
                cols = slice(start, start + right.shape[1])
                start = cols.stop
                for i in range(2):
                    low, high = max(cols.start, i * columns // 2), min(cols.stop, (i + 1) * columns // 2)
                    if low < high:
                        here = slice(low - cols.start, high - cols.start)
                        there = slice(low - i * columns // 2, high - i * columns // 2)
                        value = product[:, here]
                        if near is not None:
                            value = value + near_refs[2 * s + i][:, there].astype(F32)
                        if extra is not None:
                            value = value + extra_ref[s, :, low:high].astype(F32)
                        if pieces:
                            refs[2 * s + i][:, there] = value.astype(BF)
                        elif apart:
                            refs[s][0, :, low:high] = value.astype(BF)
                        elif split is None:
                            refs[0][s, :, low:high] = value.astype(BF)
                        else:
                            refs[2][:, low:high] = value
            if split is not None:
                outer, inner = split[0] // 2, width // split[0] // 2
                for a in range(outer):
                    for ref, bit in ((refs[0], 1 - at[0]), (refs[1], at[0])):
                        place = pl.multiple_of((2 * a + bit) * inner, inner)
                        ref[s, a * inner : (a + 1) * inner, :] = refs[2][pl.ds(place, inner), :].astype(BF)

    left = pl.BlockSpec((rows, half), lambda i, *_: (0, i))
    tall = pl.BlockSpec((count, half, columns), lambda i, *_: (0, i, 0))
    narrow = pl.BlockSpec((half, columns // 2), lambda i, *_: (i, 0))
    short = pl.BlockSpec((count, half // 2, columns), lambda i, *_: (0, i, 0))
    operands = (*lefts, *rights) + (() if near is None else tuple(near)) + (() if extra is None else (extra,))
    if pieces:
        out_shape = [shape_of((width, columns // 2))] * (2 * count)
        out_specs = [narrow] * (2 * count)
    elif apart:
        out_shape = [shape_of((1, width, columns))] * count
        out_specs = [pl.BlockSpec((1, half, columns), lambda i, *_: (0, i, 0))] * count
    elif split is None:
        out_shape, out_specs = shape_of((count, width, columns)), tall
    else:
        out_shape, out_specs = [shape_of((count, half, columns))] * 2, [short] * 2
    return call(
        clock, body,
        out_shape,
        operands,
        grid=(2,),
        in_specs=[left] * len(lefts) + [whole(v) for v in rights] + ([] if near is None else [narrow] * len(near)) + ([] if extra is None else [tall]),
        out_specs=out_specs,
        scalars=() if split is None else (split[1].reshape(1),),
        scratch=[] if split is None else [pltpu.VMEM((half, columns), F32)],
        name="weight_grads",
    )


def add_split(clock, keep, arrived, outer, index):
    columns = keep.shape[-1]
    inner = keep.size // columns // outer // 2

    def body(at, keep_ref, arrived_ref, send_ref, out_ref):
        for ref, bit in ((send_ref, 1 - at[0]), (out_ref, at[0])):
            ref[0] = (keep_ref[0, bit].astype(F32) + arrived_ref[0, bit].astype(F32)).astype(BF)

    tall = pl.BlockSpec((1, 2, inner, columns), lambda i, *_: (i, 0, 0, 0))
    short = pl.BlockSpec((1, inner, columns), lambda i, *_: (i, 0, 0))
    return call(
        clock, body,
        [shape_of((outer, inner, columns))] * 2,
        (keep.reshape(outer, 2, inner, columns), arrived.reshape(outer, 2, inner, columns)),
        grid=(outer,),
        in_specs=[tall] * 2,
        out_specs=[short] * 2,
        scalars=(jnp.asarray(index, jnp.int32).reshape(1),),
        name="add_split",
    )


def pack(clock, shared, units, projected, me, cost=0):
    count = len(units)
    first = len(shared)

    def body(at, *refs):
        shared_refs, unit_refs, q_refs, (out_ref,) = split_refs(refs, (first, count, count, 1))
        out_ref[...] = jnp.zeros_like(out_ref)
        for i in range(first):
            out_ref[i : i + 1, :] = shared_refs[i][...]
        for r in range(count):
            width = q_refs[r].shape[1] // 3
            row = pl.ds(first + (at[0] ^ r), 1)
            out_ref[row, : unit_refs[r].shape[1]] = unit_refs[r][...]
            row = pl.ds(first + count + (at[0] ^ r), 1)
            out_ref[row, :width] = q_refs[r][:, :width]
            out_ref[row, width : 2 * width] = q_refs[r][:, 2 * width :]

    out = shape_of((first + 2 * count, max(D, units[0].shape[1])), F32)
    operands = (*shared, *units, *projected)
    return call(
        clock, body, out, operands, grid=(1,), in_specs=[whole(v) for v in operands], out_specs=whole(out),
        scalars=(me.reshape(1),), name="pack", flops=cost,
    )


def attend_body(lens, *refs, step, heads):
    ins, outs, (p_ref, inv_ref) = refs[:2], refs[2:4], refs[4:]
    n = lens[pl.program_id(0)]
    length = ins[0].shape[0]
    width = heads * HD

    def rows(live):
        edge = lax.broadcasted_iota(jnp.int32, (step, length), 0) < n - (live - step)
        for which in range(2):
            ref, ctx_ref = ins[which], outs[which]
            for head in range(heads):
                slot = which * heads + head
                cols = slice(head * HD, head * HD + HD)
                keys = ref[:live, width + head * HD : width + head * HD + HD]
                values = ref[:live, 2 * width + head * HD : 2 * width + head * HD + HD]
                scores = dot(keys, ref[:, cols], 1, 1)
                last = jnp.where(edge, scores[live - step :], -1e30)
                if live > step:
                    scores = jnp.concatenate([scores[: live - step], last], 0)
                else:
                    scores = last
                top = jnp.max(scores, 0, keepdims=True)
                power = jnp.exp2((scores - top) * (SCALE * LOG2E))
                inverse = 1.0 / jnp.sum(power, 0, keepdims=True)
                low = power.astype(BF)
                p_ref[0, slot, :live, :] = low
                inv_ref[0, slot : slot + 1, :] = inverse
                mixed = dot(low, values, 0, 0)
                ctx_ref[:, cols] = (mixed * inverse.reshape(length, 1)).astype(BF)

    for live in range(step, length + 1, step):
        pl.when((n > live - step) & (n <= live))(functools.partial(rows, live))


def attend_back_body(lens, *refs, step, heads):
    ins, (grad_ref,), w_refs, (p_ref, inv_ref) = refs[:2], refs[2:3], refs[3:5], refs[5:7]
    outs, sums, do_ref = refs[7:9], refs[9:11], refs[11]
    n = lens[pl.program_id(0)]
    length = ins[0].shape[0]
    width = heads * HD

    def rows(live):
        for which in range(2):
            ref, out_ref = ins[which], outs[which]
            do_ref[:live, :] = dot(grad_ref[:live, :], w_refs[which][...], 1, 1)
            for head in range(heads):
                slot = which * heads + head
                at = [slice(c * width + head * HD, c * width + head * HD + HD) for c in range(3)]
                inverse = inv_ref[0, slot : slot + 1, :live]
                grad = (do_ref[:live, at[0]] * inverse.reshape(live, 1)).astype(BF)
                low = p_ref[0, slot, :live, :live]
                grad_probs = dot(ref[:live, at[2]], grad, 1, 1)
                power = low.astype(F32)
                product = power * grad_probs
                inner = jnp.sum(product, 0, keepdims=True) * inverse
                grad_scores = (product - power * inner).astype(BF)
                out_ref[:live, at[2]] = dot(low, grad, 1, 0).astype(BF)
                out_ref[:live, at[1]] = (dot(grad_scores, ref[:live, at[0]], 1, 0) * SCALE).astype(BF)
                out_ref[:live, at[0]] = (dot(grad_scores, ref[:live, at[1]], 0, 0) * SCALE).astype(BF)
            if live < length:
                out_ref[live:, :] = jnp.zeros((length - live, 3 * width), BF)
            sums[which][...] += jnp.sum(out_ref[:live, :].astype(F32), 0, keepdims=True)

    @pl.when(pl.program_id(0) == 0)
    def _():
        for ref in sums:
            ref[...] = jnp.zeros_like(ref)

    for live in range(step, length + 1, step):
        pl.when((n > live - step) & (n <= live))(functools.partial(rows, live))


def attend_call(clock, lens, qkv, back, length, cost=0):
    texts = lens.shape[0]
    width = qkv[0].shape[1] // 3
    heads = width // HD
    wide = pl.BlockSpec((length, 3 * width), lambda i, *_: (i, 0))
    slim = pl.BlockSpec((length, width), lambda i, *_: (i, 0))
    full = pl.BlockSpec((length, D), lambda i, *_: (i, 0))
    probs = pl.BlockSpec((1, 2 * heads, length, length), lambda i, *_: (i, 0, 0, 0))
    inverse = pl.BlockSpec((1, 2 * heads, length), lambda i, *_: (i, 0, 0))
    rows = texts * length
    if back is None:
        return call(
            clock,
            functools.partial(attend_body, step=length // 4, heads=heads),
            [shape_of((rows, width))] * 2
            + [shape_of((texts, 2 * heads, length, length)), shape_of((texts, 2 * heads, length), F32)],
            tuple(qkv),
            grid=(texts,),
            in_specs=[wide] * 2,
            out_specs=[slim] * 2 + [probs, inverse],
            scalars=(lens,),
            name="attend",
            flops=cost,
        )
    return call(
        clock,
        functools.partial(attend_back_body, step=length // 4, heads=heads),
        [shape_of((rows, 3 * width))] * 2 + [shape_of((1, 3 * width), F32)] * 2,
        tuple(qkv) + tuple(back),
        grid=(texts,),
        in_specs=[wide] * 2 + [full] + [whole(w) for w in back[1:3]] + [probs, inverse],
        out_specs=[wide] * 2 + [pl.BlockSpec((1, 3 * width), lambda i, *_: (0, 0))] * 2,
        scalars=(lens,),
        scratch=[pltpu.VMEM((length, width), F32)],
        name="attend_back",
    )


COST_FAR, COST_OUT, COST_END = 14 * 10**9, 6 * 10**9, 7 * 10**9


def program(dp_size, tensor_size):
    bits = dp_size.bit_length() - 1

    def pp_tensor(values, flip):
        return lax.ppermute(values, "tensor", [(i, i ^ flip) for i in range(tensor_size)])

    def pp_dp(values, bit):
        return lax.ppermute(values, "dp", [(i, i ^ (1 << bit)) for i in range(dp_size)])

    def on_device(
        inputs,
        lengths,
        cotangent,
        ln1_gain,
        ln1_bias,
        w_qkv,
        b_qv,
        w_out,
        b_out,
        ln2_gain,
        ln2_bias,
        w_up,
        b_up,
        w_down,
        b_down,
    ):
        t = lax.axis_index("tensor")
        d = lax.axis_index("dp")
        texts_all, part = inputs.shape[:2]
        texts = texts_all // tensor_size
        length = part * tensor_size
        rows = texts * length
        rels = range(tensor_size)
        local = w_qkv.shape[2]
        units = b_up.shape[0]
        inner = D // dp_size
        bit_of = [(d >> b) & 1 for b in range(bits)]
        clock = Clock()
        chains = []

        def pick(values, index, axis):
            return lax.dynamic_index_in_dim(values, index, axis, keepdims=False)

        number = jnp.arange(texts_all)
        ahead = (lengths[None] > lengths[:, None]) | (
            (lengths[None] == lengths[:, None]) & (number[None] < number[:, None])
        )
        rank = jnp.sum(ahead, 1)
        dealt = []
        for r in rels:
            for i in range(texts):
                dealt.append(i * tensor_size + ((t ^ r) if i % 2 == 0 else tensor_size - 1 - (t ^ r)))
        text_at = jnp.sum(jnp.where(rank[None] == jnp.stack(dealt)[:, None], number[None], 0), 1).astype(jnp.int32)
        lens = jnp.sum(jnp.where(rank[None] == jnp.stack(dealt[:texts])[:, None], lengths[None], 0), 1).astype(jnp.int32)

        def exchange(blocks):
            far = {r: pp_tensor(blocks[r], r) for r in (3, 2, 1)}
            return [blocks[0]] + [far[r] for r in (1, 2, 3)]

        class Exchange:
            def __init__(self, own, near, far):
                self.own, self.near, self.far = own, near, pp_tensor(far, 2)

            def forward(self):
                self.far = clock.after(self.far)
                self.near = pp_tensor(clock.after(self.near), 1)
                self.last = pp_tensor(pick(self.far, 1 - t % 2, 0), 1)

            def blocks(self):
                return [self.own, clock.after(self.near), self.far, clock.after(self.last)]

        class Chain:
            def __init__(self, lefts, slots, near, steps, extra=None):
                self.steps = list(steps)
                self.dims = [len(slots)] + [2] * bits
                step = self.steps.pop(0)
                outer, index = self.place(step)
                if step == "y":
                    self.keep, self.sent = weight_grads(clock, lefts, slots, near, apart=True)
                elif inner % 16 == 0 and outer > len(slots):
                    split = (outer // len(slots), index)
                    self.sent, self.keep = weight_grads(clock, lefts, slots, near, split, extra=extra)
                else:
                    total = weight_grads(clock, lefts, slots, near, extra=extra)
                    self.sent, self.keep = self.halves(total, outer, index)
                self.fly(step)

            def place(self, step):
                axis = 0 if step == "y" else bits - step
                outer = 1
                for size in self.dims[:axis]:
                    outer *= size
                self.dims[axis] = 1
                return outer, 0 * t if step == "y" else bit_of[step]

            def halves(self, total, outer, index):
                view = total.reshape(outer, 2, -1, total.shape[-1])
                return pick(view, 1 - index, 1), pick(view, index, 1)

            def fly(self, step):
                self.flight = pp_tensor(self.sent, 2) if step == "y" else pp_dp(self.sent, step)

            def step(self):
                arrived = clock.after(self.flight)
                step = self.steps.pop(0)
                outer, index = self.place(step)
                if inner % 16 == 0:
                    self.sent, self.keep = add_split(clock, self.keep, arrived, outer, index)
                else:
                    total = (self.keep.astype(F32) + arrived.astype(F32)).astype(BF)
                    self.sent, self.keep = self.halves(total, outer, index)
                self.fly(step)

            def last(self):
                total = self.keep.astype(F32) + clock.after(self.flight).astype(F32)
                return total.reshape(-1, total.shape[-1])

        high = list(range(2, bits))

        always = (lengths[0] | 1) != 0

        def block(steps, *operands):
            operands = (clock.after(operands[0]),) + operands[1:]

            def run(*values):
                clock.last = None
                return steps(*values)

            saved = [(list(chain.steps), list(chain.dims)) for chain in chains]
            shapes = jax.eval_shape(lambda *v: run(*v), *operands)
            for chain, (left, dims) in zip(chains, saved):
                chain.steps, chain.dims = left, dims
            out = lax.cond(
                always, run, lambda *_: jax.tree.map(lambda v: jnp.zeros(v.shape, v.dtype), shapes), *operands
            )
            clock.last = None
            return clock.then(out)

        def from_near(lefts, slots):
            return [pp_tensor(v, 1) for v in weight_grads(clock, lefts, slots, pieces=True)]

        x_own = split_texts(clock, inputs, text_at, t, texts, False)
        x_blocks = exchange(x_own)
        wq_own = side_by_side(clock, tie(w_qkv, *x_own[1:]))
        wq_near = [pp_tensor(v, 1) for v in wq_own]
        wo_near = pp_tensor(tie(w_out, x_blocks[1]), 1)
        small = jnp.concatenate([b_qv.reshape(-1), tie(b_up, x_blocks[1])])
        small = jnp.stack([small, pp_tensor(small, 1)])
        small = list(small) + list(pp_tensor(small, 2))
        bqkv = [
            jnp.concatenate([s[:local], jnp.zeros((local,), F32), s[local : 2 * local]]) for s in small
        ]
        bup = [s[2 * local :] for s in small]


        x_blocks[0] = tie(x_blocks[0], wo_near, *wq_near)
        wq_far = [pp_tensor(tie(v, x_blocks[3]), 2) for v in wq_own]
        cut = w_up.shape[0] // 2
        up_first, up_second = jnp.concatenate([w_up[:cut], w_out], 0), w_up[cut:]
        first_far, second_far = [pp_tensor(tie(v, x_blocks[3]), 2) for v in (up_first, up_second)]
        cot = Exchange(*split_texts(clock, tie(cotangent, x_blocks[1]), text_at, t, texts, True))
        wd_far = pp_tensor(tie(w_down, x_blocks[3]), 2)
        x, h1 = join_norm(clock, x_blocks, t, ln1_gain, ln1_bias)
        wq = [wq_own, wq_near]
        qkv = [project(clock, h1, wq[r], bqkv[r]) for r in (0, 1)]
        attn_a = attend_call(clock, lens, qkv[:2], None, length)
        wq_far = [clock.after(v) for v in wq_far]

        def project_far(values):
            passed = [pp_tensor(v, 1) for v in wq_far]
            ups, downs = pp_tensor(w_up, 1), pp_tensor(w_down, 1)
            return passed, project(clock, values, wq_far, bqkv[2]), ups, downs

        passed, q_first, wu_near, wd_near = block(project_far, h1)
        wq += [wq_far, passed]
        qkv += [q_first, project(clock, h1, wq[3], bqkv[3])]
        attn_b = attend_call(clock, lens, qkv[2:], None, length, COST_FAR)
        first_far = clock.after(first_far)
        wo_far = first_far[cut:]
        wo = [w_out, wo_near, wo_far, pp_tensor(wo_far, 1)]
        ctx = [attn_a[0], attn_a[1], attn_b[0], attn_b[1]]
        resid, h2 = attention_out(clock, x, ctx, wo, (b_out, ln2_gain, ln2_bias))
        ups = [up(clock, h2, [w_up], bup[0])]
        wu_far = [first_far[:cut], clock.after(second_far)]
        wu = [[w_up], [wu_near], wu_far, [pp_tensor(v, 1) for v in wu_far]]
        ups.append(up(clock, h2, wu[1], bup[1], COST_OUT))
        cot.forward()
        ups.append(up(clock, h2, wu[3], bup[3]))
        g_low, bias_down = join_mask(clock, cot.blocks(), t, lens)

        near = from_near([g_low], [[(0, ups[1][0])], [(0, ups[2][0])]])
        ups.insert(2, up(clock, h2, wu[2], bup[2]))
        acts, slopes = [u[0] for u in ups], [u[1] for u in ups]
        down = Chain([g_low], [[(0, acts[0])], [(0, acts[2])]], near, ["y", 0, 1] + high)
        wd_far = clock.after(wd_far)
        wd = [[w_down], [wd_near], [wd_far], [pp_tensor(wd_far, 1)]]
        dups_a, sums_a, dh2 = up_back(clock, g_low, wu[:2], wd[:2], slopes[:2], None, None, None)
        dups_b, sums_b, rest = up_back(clock, g_low, wu[2:], wd[2:], slopes[2:], dh2[0], resid, ln2_gain)
        dres, dres_low, gain_two, shift_two, bias_attn = rest
        dups, bias_up = dups_a + dups_b, sums_a + sums_b
        up_near = from_near([h2], [[(0, dups[1])], [(0, dups[3])]])
        down.step()
        grads_up = Chain([h2], [[(0, dups[0])], [(0, dups[2])]], up_near, ["y", 0, 1] + high)
        back = attend_call(clock, lens, qkv[2:], [dres_low] + wo[2:] + list(attn_b[2:]), length)
        dqkv_far, qkv_sums_far = back[:2], back[2:]
        near = from_near([h1, dres_low], [[(0, dqkv_far[1]), (1, ctx[3])]])
        down.step()
        q_far = weight_grads(clock, [h1, dres_low], [[(0, dqkv_far[0]), (1, ctx[2])]], near)
        q_far = pp_tensor(q_far, 2)
        back = attend_call(clock, lens, qkv[:2], [dres_low] + wo[:2] + list(attn_a[2:]), length)
        dqkv, qkv_sums = list(back[:2]) + list(dqkv_far), list(back[2:]) + list(qkv_sums_far)
        grads_up.step()
        for bit in high:
            down.step()
        near = from_near([h1, dres_low], [[(0, dqkv[1]), (1, ctx[1])]])
        out = Exchange(*down_out(clock, resid, acts, wd, b_down, t, texts))
        grad_down = clock.then(down.last())
        grads_up.step()
        q_own = Chain([h1, dres_low], [[(0, dqkv[0]), (1, ctx[0])]], near, [0, 1] + high, clock.after(q_far))
        in_blocks, gain_one, shift_one = norm_one_back(clock, x, dres, dqkv, wq, ln1_gain, t, texts)
        gin = Exchange(*in_blocks)
        shared = [gain_one, shift_one, gain_two, shift_two, bias_attn, bias_down]
        out.forward()
        chains += [grads_up, q_own]
        for chain in chains:
            chain.flight = clock.then(clock.after(chain.flight))
        total = pack(clock, shared, bias_up, qkv_sums, t, COST_END)
        out_blocks = out.blocks()

        def moved(values, flip, tensor):
            flight = pp_tensor(values, flip) if tensor else pp_dp(values, flip)
            return clock.then(values + clock.after(flight))

        def load(state):
            for chain, (keep, flight) in zip(chains, state):
                chain.keep, chain.flight = keep, flight

        def begin(total, state):
            load(state)
            for bit in high[:1]:
                grads_up.step()
            q_own.step()
            total = moved(total, 1, True)
            for bit in (0, 1)[:bits]:
                total = moved(total, bit, False)
            return total, [(chain.keep, clock.after(chain.flight)) for chain in chains]

        def finish(total, state, blocks):
            load(state)
            for bit in high[1:]:
                grads_up.step()
            grad_up = clock.then(grads_up.last())
            for bit in high:
                q_own.step()
                total = moved(total, bit, False)
            total = moved(total, 2, True)
            rows_out = join_rows(clock, blocks, t, text_at)
            first = len(shared)
            vectors = [total[i] for i in range(first)]
            vectors.append(lax.dynamic_slice_in_dim(total, first + t, 1)[0, :units])
            qv = lax.dynamic_slice_in_dim(total, first + tensor_size + t, 1)[0, : 2 * local]
            vectors.append(qv.reshape(2, local))
            both = q_own.last()
            weights = jnp.stack([both[:, c * local : c * local + local] for c in range(3)])
            return rows_out, vectors, grad_up, weights, both[:, 3 * local :].T

        state = [(chain.keep, chain.flight) for chain in chains]
        total, state = block(begin, total, state)
        gin.forward()
        layer_out, vector, grad_up, grad_qkv, grad_out = block(finish, total, state, out_blocks)
        grad_input = join_rows(clock, gin.blocks(), t, text_at)
        return (
            layer_out,
            grad_input,
            vector[0],
            vector[1],
            grad_qkv,
            vector[7],
            grad_out,
            vector[4],
            vector[2],
            vector[3],
            grad_up,
            vector[6],
            grad_down.T,
            vector[5],
        )

    return on_device


def solution(mesh):
    return jax.shard_map(
        program(mesh.shape["dp"], mesh.shape["tensor"]),
        mesh=mesh,
        in_specs=(
            P("dp", "tensor", None),
            P("dp"),
            P("dp", "tensor", None),
            P(),
            P(),
            P(None, None, "tensor"),
            P(None, "tensor"),
            P("tensor", None),
            P(),
            P(),
            P(),
            P(None, "tensor"),
            P("tensor"),
            P("tensor", None),
            P(),
        ),
        out_specs=(
            P("dp", "tensor", None),
            P("dp", "tensor", None),
            P(),
            P(),
            P(None, "dp", "tensor"),
            P(None, "tensor"),
            P("tensor", "dp"),
            P(),
            P(),
            P(),
            P("dp", "tensor"),
            P("tensor"),
            P("tensor", "dp"),
            P(),
        ),
        check_vma=False,
    )
```

```python
import functools

import jax
import jax.numpy as jnp
from jax import lax
from jax.experimental import pallas as pl
from jax.experimental.pallas import tpu as pltpu
from jax.sharding import PartitionSpec as P

D = 768
HD = 64
BF = jnp.bfloat16
F32 = jnp.float32
SCALE = HD**-0.5
LOG2E = 1.4426950408889634


def dot(left, right, left_dim, right_dim):
    return lax.dot_general(
        left, right, (((left_dim,), (right_dim,)), ((), ())), preferred_element_type=F32
    )


def norm_stats(values):
    center = values - jnp.mean(values, -1, keepdims=True)
    rstd = lax.rsqrt(jnp.mean(center * center, -1, keepdims=True) + 1e-05)
    return center * rstd, rstd


def norm_back(grad_norm, normal, rstd, gain):
    scaled = grad_norm * gain
    return rstd * (
        scaled
        - jnp.mean(scaled, -1, keepdims=True)
        - normal * jnp.mean(scaled * normal, -1, keepdims=True)
    )


class Clock:
    def __init__(self):
        self.last = None

    def after(self, values):
        return values if self.last is None else tie(values, self.last)

    def then(self, values):
        self.last = jax.tree.leaves(values)[0]
        return values


def tie(value, *waits):
    return lax.optimization_barrier((value,) + waits)[0]


def call(clock, body, out_shape, operands, *, grid=(), in_specs=None, out_specs=None, scalars=(), scratch=(),
         name=None, flops=0, plain=False):
    operands = (clock.after(operands[0]),) + tuple(operands[1:])
    if plain:
        operands = [pltpu.with_memory_space_constraint(v, pltpu.HBM) for v in operands]
    out = pl.pallas_call(
        body,
        out_shape=jax.tree.map(lambda v: pltpu.HBM(v.shape, v.dtype), out_shape) if name in ("up", "attend", "up_back") else out_shape,
        grid_spec=pltpu.PrefetchScalarGridSpec(
            num_scalar_prefetch=len(scalars),
            grid=grid,
            in_specs=in_specs,
            out_specs=out_specs,
            scratch_shapes=scratch,
        ),
        compiler_params=pltpu.CompilerParams(vmem_limit_bytes=48 << 20),
        cost_estimate=pl.CostEstimate(flops=flops, bytes_accessed=0, transcendentals=0),
        name=name,
    )(*scalars, *operands)
    return clock.then(out)


def shape_of(dims, dtype=BF):
    return jax.ShapeDtypeStruct(tuple(dims), dtype)


def whole(values):
    return pl.BlockSpec(values.shape, lambda *_: (0,) * len(values.shape))


def side_by_side(clock, w):
    half, width = w.shape[1] // 2, w.shape[2]

    def body(w_ref, *refs):
        for i in range(2):
            for c in range(3):
                refs[i][:, c * width : (c + 1) * width] = w_ref[c, i * half : (i + 1) * half, :]

    out = [shape_of((half, 3 * width))] * 2
    return call(
        clock, body, out, (w,), grid=(1,), in_specs=[whole(w)], out_specs=[whole(v) for v in out],
        name="side_by_side",
    )


def times(left, pieces):
    total, start = None, 0
    for ref in pieces:
        part = dot(left[:, start : start + ref.shape[0]], ref[...], 1, 0)
        start += ref.shape[0]
        total = part if total is None else total + part
    return total


def times_turned(left, pieces):
    parts = [dot(left, ref[...], 1, 1) for ref in pieces]
    return parts[0] if len(parts) == 1 else jnp.concatenate(parts, 1)


def split_refs(refs, counts):
    out = []
    for count in counts:
        out.append(refs[:count])
        refs = refs[count:]
    return out


def row_block(values, steps):
    return pl.BlockSpec((values.shape[0] // steps, values.shape[1]), lambda i, *_: (i, 0))


def project(clock, h, w, bias):
    def body(h_ref, bias_ref, *refs):
        refs[-1][...] = (times(h_ref[...], refs[:-1]) + bias_ref[...]).astype(BF)

    bias = bias.reshape(1, -1)
    out = shape_of((h.shape[0], bias.shape[1]))
    return call(
        clock, body, out, (h, bias, *w), grid=(4,), in_specs=[row_block(h, 4), whole(bias)] + [whole(v) for v in w],
        out_specs=row_block(out, 4), name="project",
    )


def attention_out(clock, x, ctx, w, vectors, cost=0):
    count = len(ctx)

    def body(x_ref, *refs):
        ctx_refs, w_refs, (bias_ref, gain_ref, shift_ref), (out_ref, h_ref) = split_refs(refs, (count, count, 3, 2))
        total = x_ref[...].astype(F32) + bias_ref[...]
        for r in range(count):
            total = total + dot(ctx_refs[r][...], w_refs[r][...], 1, 0)
        out_ref[...] = total
        normal, _ = norm_stats(total)
        h_ref[...] = (normal * gain_ref[...] + shift_ref[...]).astype(BF)

    vectors = [v.reshape(1, -1) for v in vectors]
    out = [shape_of(x.shape, F32), shape_of(x.shape)]
    return call(
        clock, body, out, (x, *ctx, *w, *vectors), grid=(4,),
        in_specs=[row_block(v, 4) for v in (x, *ctx)] + [whole(v) for v in (*w, *vectors)],
        out_specs=[row_block(v, 4) for v in out], name="attention_out", flops=cost, plain=True,
    )


def up(clock, h, w, bias, cost=0):
    def body(h_ref, bias_ref, *refs):
        upper = times(h_ref[...], refs[:-2]) + bias_ref[...]
        below = 0.5 * (1.0 + lax.erf(upper * (0.5**0.5)))
        density = jnp.exp(-0.5 * upper * upper) * 0.3989422804014327
        refs[-2][...] = (upper * below).astype(BF)
        refs[-1][...] = (below + upper * density).astype(BF)

    bias = bias.reshape(1, -1)
    out = [shape_of((h.shape[0], bias.shape[1]))] * 2
    return call(
        clock, body, out, (h, bias, *w), grid=(4,), in_specs=[row_block(h, 4), whole(bias)] + [whole(v) for v in w],
        out_specs=[row_block(v, 4) for v in out], name="up", flops=cost,
    )


def to_owner(refs, at, values, scratch, count):
    text, late = pl.program_id(0) // 2, pl.program_id(0) % 2
    part = values.shape[0] * 2 // count
    scratch[...] = values.astype(BF)
    for r in range(count):
        place = at[0] ^ r

        @pl.when(place // (count // 2) == late)
        def _():
            start = pl.multiple_of((place % (count // 2)) * part, part)
            rows = scratch[pl.ds(start, part), :]
            if r < 2:
                refs[r][pl.ds(text, 1)] = rows[None]
            else:
                refs[2][pl.ds(place % 2, 1), pl.ds(text, 1)] = rows[None, None]


def owner_shapes(texts, count, rows, width):
    block = (texts, rows // texts // count, width)
    return [shape_of(block), shape_of(block), shape_of((2, *block))]


def down_out(clock, resid, acts, w, bias, me, texts):
    count = len(acts)
    sizes = [len(pieces) for pieces in w]
    w = [v for pieces in w for v in pieces]
    steps = texts * 2

    def body(at, resid_ref, *refs):
        act_refs, w_refs, (bias_ref,), outs, (scratch,) = split_refs(refs, (count, len(w), 1, 3, 1))
        w_refs = split_refs(w_refs, sizes)
        total = resid_ref[...] + bias_ref[...]
        for r in range(count):
            total = total + times(act_refs[r], w_refs[r])
        to_owner(outs, at, total, scratch, count)

    bias = bias.reshape(1, -1)
    out = owner_shapes(texts, count, *resid.shape)
    return call(
        clock, body, out, (resid, *acts, *w, bias), grid=(steps,),
        in_specs=[row_block(v, steps) for v in (resid, *acts)] + [whole(v) for v in (*w, bias)],
        out_specs=[whole(v) for v in out], scalars=(me.reshape(1),),
        scratch=[pltpu.VMEM((resid.shape[0] // steps, resid.shape[1]), BF)], name="down_out",
    )


def norm_one_back(clock, x, dres, dqkv, w, gain, me, texts):
    count = len(dqkv)
    steps = texts * 2
    sizes = [len(pieces) for pieces in w]
    flat = [v for pieces in w for v in pieces]

    def body(at, x_ref, dres_ref, *refs):
        grads, w_refs, (gain_ref,), outs, (gain_sum, shift_sum, scratch) = split_refs(
            refs, (count, len(flat), 1, 3, 3)
        )
        w_refs = split_refs(w_refs, sizes)
        total = None
        for r in range(count):
            part = times_turned(grads[r][...], w_refs[r])
            total = part if total is None else total + part
        normal, rstd = norm_stats(x_ref[...].astype(F32))

        @pl.when(pl.program_id(0) == 0)
        def _():
            gain_sum[...] = jnp.zeros_like(gain_sum)
            shift_sum[...] = jnp.zeros_like(shift_sum)

        gain_sum[...] += jnp.sum(total * normal, 0, keepdims=True)
        shift_sum[...] += jnp.sum(total, 0, keepdims=True)
        to_owner(outs, at, dres_ref[...] + norm_back(total, normal, rstd, gain_ref[...]), scratch, count)

    gain = gain.reshape(1, -1)
    out = owner_shapes(texts, count, *x.shape) + [shape_of(gain.shape, F32)] * 2
    out = call(
        clock, body, out, (x, dres, *dqkv, *flat, gain), grid=(steps,),
        in_specs=[row_block(v, steps) for v in (x, dres, *dqkv)] + [whole(v) for v in (*flat, gain)],
        out_specs=[whole(v) for v in out], scalars=(me.reshape(1),),
        scratch=[pltpu.VMEM((x.shape[0] // steps, x.shape[1]), BF)], name="norm_one_back",
    )
    return out[:3], out[3], out[4]


def block_of(refs, at, r, i):
    return refs[r][i] if refs[r].ndim == 3 else refs[r][at[0] % 2, i]


def join_norm(clock, blocks, me, gain, shift):
    texts, part, width = blocks[0].shape
    count = len(blocks)

    def body(at, *refs):
        ins, (gain_ref, shift_ref, x_ref, h_ref) = refs[:count], refs[count:]
        for r in range(count):
            for i in range(texts):
                start = pl.multiple_of(i * count * part + (at[0] ^ r) * part, part)
                low = ins[r][i]
                normal, _ = norm_stats(low.astype(F32))
                x_ref[pl.ds(start, part), :] = low
                h_ref[pl.ds(start, part), :] = (normal * gain_ref[...] + shift_ref[...]).astype(BF)

    out = [shape_of((texts * count * part, width))] * 2
    operands = (*blocks, gain.reshape(1, -1), shift.reshape(1, -1))
    return call(
        clock, body, out, operands, grid=(1,), in_specs=[whole(v) for v in operands], out_specs=[whole(v) for v in out],
        scalars=(me.reshape(1),), name="join_norm",
    )


def join_mask(clock, blocks, me, lens):
    texts, part, width = blocks[0].shape
    count = len(blocks)

    def body(at, n, *refs):
        ins, (g_ref, sum_ref) = refs[:count], refs[count:]
        total = jnp.zeros((1, width), F32)
        for r in range(count):
            for i in range(texts):
                place = (at[0] ^ r) * part
                start = pl.multiple_of(i * count * part + place, part)
                live = lax.broadcasted_iota(jnp.int32, (part, width), 0) + place < n[i]
                values = jnp.where(live, block_of(ins, at, r, i).astype(F32), 0.0)
                total = total + jnp.sum(values, 0, keepdims=True)
                g_ref[pl.ds(start, part), :] = values.astype(BF)
        sum_ref[...] = total

    out = [shape_of((texts * count * part, width)), shape_of((1, width), F32)]
    return call(
        clock, body, out, blocks, grid=(1,), in_specs=[whole(v) for v in blocks], out_specs=[whole(v) for v in out],
        scalars=(me.reshape(1), lens), name="join_mask",
    )


def split_texts(clock, values, index, me, texts, stacked):
    count = index.shape[0] // texts
    block = (texts,) + values.shape[1:]

    def body(at, text_at, values_ref, *refs):
        for r in range(count):
            for i in range(texts):
                rows = values_ref[pl.ds(text_at[r * texts + i], 1)]
                if stacked and r >= 2:
                    refs[2][pl.ds((at[0] ^ r) % 2, 1), i : i + 1] = rows[None]
                else:
                    refs[r][i : i + 1] = rows

    out = [shape_of(block)] * 2 + ([shape_of((2, *block))] if stacked else [shape_of(block)] * (count - 2))
    return call(
        clock, body, out, (values,), grid=(1,), in_specs=[whole(values)], out_specs=[whole(v) for v in out],
        scalars=(me.reshape(1), index), name="split_texts",
    )


def join_rows(clock, blocks, me, index):
    texts = blocks[0].shape[0]
    count = len(blocks)

    def body(at, text_at, *refs):
        for r in range(count):
            for i in range(texts):
                refs[count][pl.ds(text_at[r * texts + i], 1)] = block_of(refs, at, r, i)[None]

    out = shape_of((texts * count,) + blocks[0].shape[1:])
    return call(
        clock, body, out, blocks, grid=(1,), in_specs=[whole(v) for v in blocks], out_specs=whole(out),
        scalars=(me.reshape(1), index), name="join_rows",
    )


def up_back(clock, g, ups, downs, slopes, base, resid, gain):
    rows, width = g.shape
    count = len(ups)
    units = slopes[0].shape[1]
    down_sizes = [len(pieces) for pieces in downs]
    downs = [v for pieces in downs for v in pieces]
    sizes = [len(pieces) for pieces in ups]
    flat = [v for pieces in ups for v in pieces]
    last = base is not None

    def body(g_ref, *refs):
        up_refs, down_refs, slope_refs, more, grad_refs, sum_refs, outs = split_refs(
            refs, (len(flat), len(downs), count, 3 if last else 0, count, count, 5 if last else 1)
        )
        up_refs = split_refs(up_refs, sizes)
        down_refs = split_refs(down_refs, down_sizes)
        grad = g_ref[...]
        total = more[0][...] if last else None

        @pl.when(pl.program_id(0) == 0)
        def _():
            for ref in list(sum_refs) + list(outs[2:]):
                ref[...] = jnp.zeros_like(ref)

        for s in range(count):
            upper = times_turned(grad, down_refs[s]) * slope_refs[s][...].astype(F32)
            sum_refs[s][...] += jnp.sum(upper, 0, keepdims=True)
            low = upper.astype(BF)
            grad_refs[s][...] = low
            part = times_turned(low, up_refs[s])
            total = part if total is None else total + part
        if last:
            normal, rstd = norm_stats(more[1][...])
            outs[2][...] += jnp.sum(total * normal, 0, keepdims=True)
            outs[3][...] += jnp.sum(total, 0, keepdims=True)
            total = grad.astype(F32) + norm_back(total, normal, rstd, more[2][...])
            outs[4][...] += jnp.sum(total, 0, keepdims=True)
            outs[1][...] = total.astype(BF)
        outs[0][...] = total

    sums, vector = shape_of((1, units), F32), shape_of((1, width), F32)
    unit = pl.BlockSpec((rows // 4, units), lambda i: (i, 0))
    operands = (g, *flat, *downs, *slopes)
    in_specs = [row_block(g, 4)] + [whole(v) for v in (*flat, *downs)] + [unit] * count
    outs = [shape_of((rows, width), F32)]
    out_specs = [row_block(g, 4)]
    if last:
        gain = gain.reshape(1, -1)
        operands += (base, resid, gain)
        in_specs += [row_block(g, 4)] * 2 + [whole(gain)]
        outs += [shape_of((rows, width))] + [vector] * 3
        out_specs += [row_block(g, 4)] + [whole(vector)] * 3
    out = call(
        clock, body,
        [shape_of((rows, units))] * count + [sums] * count + outs,
        operands,
        grid=(4,),
        in_specs=in_specs,
        out_specs=[unit] * count + [whole(sums)] * count + out_specs,
        name="up_back",
    )
    return list(out[:count]), list(out[count : 2 * count]), out[2 * count :]


def weight_grads(clock, lefts, slots, near=None, split=None, apart=False, pieces=False, extra=None):
    rows, width = lefts[0].shape
    columns = sum(right.shape[1] for _, right in slots[0])
    count = len(slots)
    half = width // 2
    rights = [right for slot in slots for _, right in slot]

    def body(*refs):
        if split is not None:
            at, refs = refs[0], refs[1:]
        left_refs, refs = refs[: len(lefts)], refs[len(lefts) :]
        right_refs, refs = list(refs[: len(rights)]), refs[len(rights) :]
        if near is not None:
            near_refs, refs = refs[: len(near)], refs[len(near) :]
        if extra is not None:
            extra_ref, refs = refs[0], refs[1:]
        for s, slot in enumerate(slots):
            start = 0
            for which, right in slot:
                product = dot(left_refs[which][...], right_refs.pop(0)[...], 0, 0)
                cols = slice(start, start + right.shape[1])
                start = cols.stop
                for i in range(2):
                    low, high = max(cols.start, i * columns // 2), min(cols.stop, (i + 1) * columns // 2)
                    if low < high:
                        here = slice(low - cols.start, high - cols.start)
                        there = slice(low - i * columns // 2, high - i * columns // 2)
                        value = product[:, here]
                        if near is not None:
                            value = value + near_refs[2 * s + i][:, there].astype(F32)
                        if extra is not None:
                            value = value + extra_ref[s, :, low:high].astype(F32)
                        if pieces:
                            refs[2 * s + i][:, there] = value.astype(BF)
                        elif apart:
                            refs[s][0, :, low:high] = value.astype(BF)
                        elif split is None:
                            refs[0][s, :, low:high] = value.astype(BF)
                        else:
                            refs[2][:, low:high] = value
            if split is not None:
                outer, inner = split[0] // 2, width // split[0] // 2
                for a in range(outer):
                    for ref, bit in ((refs[0], 1 - at[0]), (refs[1], at[0])):
                        place = pl.multiple_of((2 * a + bit) * inner, inner)
                        ref[s, a * inner : (a + 1) * inner, :] = refs[2][pl.ds(place, inner), :].astype(BF)

    left = pl.BlockSpec((rows, half), lambda i, *_: (0, i))
    tall = pl.BlockSpec((count, half, columns), lambda i, *_: (0, i, 0))
    narrow = pl.BlockSpec((half, columns // 2), lambda i, *_: (i, 0))
    short = pl.BlockSpec((count, half // 2, columns), lambda i, *_: (0, i, 0))
    operands = (*lefts, *rights) + (() if near is None else tuple(near)) + (() if extra is None else (extra,))
    if pieces:
        out_shape = [shape_of((width, columns // 2))] * (2 * count)
        out_specs = [narrow] * (2 * count)
    elif apart:
        out_shape = [shape_of((1, width, columns))] * count
        out_specs = [pl.BlockSpec((1, half, columns), lambda i, *_: (0, i, 0))] * count
    elif split is None:
        out_shape, out_specs = shape_of((count, width, columns)), tall
    else:
        out_shape, out_specs = [shape_of((count, half, columns))] * 2, [short] * 2
    return call(
        clock, body,
        out_shape,
        operands,
        grid=(2,),
        in_specs=[left] * len(lefts) + [whole(v) for v in rights] + ([] if near is None else [narrow] * len(near)) + ([] if extra is None else [tall]),
        out_specs=out_specs,
        scalars=() if split is None else (split[1].reshape(1),),
        scratch=[] if split is None else [pltpu.VMEM((half, columns), F32)],
        name="weight_grads",
    )


def add_split(clock, keep, arrived, outer, index):
    columns = keep.shape[-1]
    inner = keep.size // columns // outer // 2

    def body(at, keep_ref, arrived_ref, send_ref, out_ref):
        for ref, bit in ((send_ref, 1 - at[0]), (out_ref, at[0])):
            ref[0] = (keep_ref[0, bit].astype(F32) + arrived_ref[0, bit].astype(F32)).astype(BF)

    tall = pl.BlockSpec((1, 2, inner, columns), lambda i, *_: (i, 0, 0, 0))
    short = pl.BlockSpec((1, inner, columns), lambda i, *_: (i, 0, 0))
    return call(
        clock, body,
        [shape_of((outer, inner, columns))] * 2,
        (keep.reshape(outer, 2, inner, columns), arrived.reshape(outer, 2, inner, columns)),
        grid=(outer,),
        in_specs=[tall] * 2,
        out_specs=[short] * 2,
        scalars=(jnp.asarray(index, jnp.int32).reshape(1),),
        name="add_split",
    )


def pack(clock, shared, units, projected, me, cost=0):
    count = len(units)
    first = len(shared)

    def body(at, *refs):
        shared_refs, unit_refs, q_refs, (out_ref,) = split_refs(refs, (first, count, count, 1))
        out_ref[...] = jnp.zeros_like(out_ref)
        for i in range(first):
            out_ref[i : i + 1, :] = shared_refs[i][...]
        for r in range(count):
            width = q_refs[r].shape[1] // 3
            row = pl.ds(first + (at[0] ^ r), 1)
            out_ref[row, : unit_refs[r].shape[1]] = unit_refs[r][...]
            row = pl.ds(first + count + (at[0] ^ r), 1)
            out_ref[row, :width] = q_refs[r][:, :width]
            out_ref[row, width : 2 * width] = q_refs[r][:, 2 * width :]

    out = shape_of((first + 2 * count, max(D, units[0].shape[1])), F32)
    operands = (*shared, *units, *projected)
    return call(
        clock, body, out, operands, grid=(1,), in_specs=[whole(v) for v in operands], out_specs=whole(out),
        scalars=(me.reshape(1),), name="pack", flops=cost,
    )


def attend_body(lens, *refs, step, heads):
    ins, outs, (p_ref, inv_ref) = refs[:2], refs[2:4], refs[4:]
    n = lens[pl.program_id(0)]
    length = ins[0].shape[0]
    width = heads * HD

    def rows(live):
        edge = lax.broadcasted_iota(jnp.int32, (step, length), 0) < n - (live - step)
        for which in range(2):
            ref, ctx_ref = ins[which], outs[which]
            for head in range(heads):
                slot = which * heads + head
                cols = slice(head * HD, head * HD + HD)
                keys = ref[:live, width + head * HD : width + head * HD + HD]
                values = ref[:live, 2 * width + head * HD : 2 * width + head * HD + HD]
                scores = dot(keys, ref[:, cols], 1, 1)
                last = jnp.where(edge, scores[live - step :], -1e30)
                if live > step:
                    scores = jnp.concatenate([scores[: live - step], last], 0)
                else:
                    scores = last
                top = jnp.max(scores, 0, keepdims=True)
                power = jnp.exp2((scores - top) * (SCALE * LOG2E))
                inverse = 1.0 / jnp.sum(power, 0, keepdims=True)
                low = power.astype(BF)
                p_ref[0, slot, :live, :] = low
                inv_ref[0, slot : slot + 1, :] = inverse
                mixed = dot(low, values, 0, 0)
                ctx_ref[:, cols] = (mixed * inverse.reshape(length, 1)).astype(BF)

    for live in range(step, length + 1, step):
        pl.when((n > live - step) & (n <= live))(functools.partial(rows, live))


def attend_back_body(lens, *refs, step, heads):
    ins, (grad_ref,), w_refs, (p_ref, inv_ref) = refs[:2], refs[2:3], refs[3:5], refs[5:7]
    outs, sums, do_ref = refs[7:9], refs[9:11], refs[11]
    n = lens[pl.program_id(0)]
    length = ins[0].shape[0]
    width = heads * HD

    def rows(live):
        for which in range(2):
            ref, out_ref = ins[which], outs[which]
            do_ref[:live, :] = dot(grad_ref[:live, :], w_refs[which][...], 1, 1)
            for head in range(heads):
                slot = which * heads + head
                at = [slice(c * width + head * HD, c * width + head * HD + HD) for c in range(3)]
                inverse = inv_ref[0, slot : slot + 1, :live]
                grad = (do_ref[:live, at[0]] * inverse.reshape(live, 1)).astype(BF)
                low = p_ref[0, slot, :live, :live]
                grad_probs = dot(ref[:live, at[2]], grad, 1, 1)
                power = low.astype(F32)
                product = power * grad_probs
                inner = jnp.sum(product, 0, keepdims=True) * inverse
                grad_scores = (product - power * inner).astype(BF)
                out_ref[:live, at[2]] = dot(low, grad, 1, 0).astype(BF)
                out_ref[:live, at[1]] = (dot(grad_scores, ref[:live, at[0]], 1, 0) * SCALE).astype(BF)
                out_ref[:live, at[0]] = (dot(grad_scores, ref[:live, at[1]], 0, 0) * SCALE).astype(BF)
            if live < length:
                out_ref[live:, :] = jnp.zeros((length - live, 3 * width), BF)
            sums[which][...] += jnp.sum(out_ref[:live, :].astype(F32), 0, keepdims=True)

    @pl.when(pl.program_id(0) == 0)
    def _():
        for ref in sums:
            ref[...] = jnp.zeros_like(ref)

    for live in range(step, length + 1, step):
        pl.when((n > live - step) & (n <= live))(functools.partial(rows, live))


def attend_call(clock, lens, qkv, back, length, cost=0):
    texts = lens.shape[0]
    width = qkv[0].shape[1] // 3
    heads = width // HD
    wide = pl.BlockSpec((length, 3 * width), lambda i, *_: (i, 0))
    slim = pl.BlockSpec((length, width), lambda i, *_: (i, 0))
    full = pl.BlockSpec((length, D), lambda i, *_: (i, 0))
    probs = pl.BlockSpec((1, 2 * heads, length, length), lambda i, *_: (i, 0, 0, 0))
    inverse = pl.BlockSpec((1, 2 * heads, length), lambda i, *_: (i, 0, 0))
    rows = texts * length
    if back is None:
        return call(
            clock,
            functools.partial(attend_body, step=length // 4, heads=heads),
            [shape_of((rows, width))] * 2
            + [shape_of((texts, 2 * heads, length, length)), shape_of((texts, 2 * heads, length), F32)],
            tuple(qkv),
            grid=(texts,),
            in_specs=[wide] * 2,
            out_specs=[slim] * 2 + [probs, inverse],
            scalars=(lens,),
            name="attend",
            flops=cost,
        )
    return call(
        clock,
        functools.partial(attend_back_body, step=length // 4, heads=heads),
        [shape_of((rows, 3 * width))] * 2 + [shape_of((1, 3 * width), F32)] * 2,
        tuple(qkv) + tuple(back),
        grid=(texts,),
        in_specs=[wide] * 2 + [full] + [whole(w) for w in back[1:3]] + [probs, inverse],
        out_specs=[wide] * 2 + [pl.BlockSpec((1, 3 * width), lambda i, *_: (0, 0))] * 2,
        scalars=(lens,),
        scratch=[pltpu.VMEM((length, width), F32)],
        name="attend_back",
    )


COST_FAR, COST_OUT, COST_END = 14 * 10**9, 6 * 10**9, 7 * 10**9


def program(dp_size, tensor_size):
    bits = dp_size.bit_length() - 1

    def pp_tensor(values, flip):
        return lax.ppermute(values, "tensor", [(i, i ^ flip) for i in range(tensor_size)])

    def pp_dp(values, bit):
        return lax.ppermute(values, "dp", [(i, i ^ (1 << bit)) for i in range(dp_size)])

    def on_device(
        inputs,
        lengths,
        cotangent,
        ln1_gain,
        ln1_bias,
        w_qkv,
        b_qv,
        w_out,
        b_out,
        ln2_gain,
        ln2_bias,
        w_up,
        b_up,
        w_down,
        b_down,
    ):
        t = lax.axis_index("tensor")
        d = lax.axis_index("dp")
        texts_all, part = inputs.shape[:2]
        texts = texts_all // tensor_size
        length = part * tensor_size
        rows = texts * length
        rels = range(tensor_size)
        local = w_qkv.shape[2]
        units = b_up.shape[0]
        inner = D // dp_size
        bit_of = [(d >> b) & 1 for b in range(bits)]
        clock = Clock()
        chains = []

        def pick(values, index, axis):
            return lax.dynamic_index_in_dim(values, index, axis, keepdims=False)

        number = jnp.arange(texts_all)
        ahead = (lengths[None] > lengths[:, None]) | (
            (lengths[None] == lengths[:, None]) & (number[None] < number[:, None])
        )
        rank = jnp.sum(ahead, 1)
        dealt = []
        for r in rels:
            for i in range(texts):
                dealt.append(i * tensor_size + ((t ^ r) if i % 2 == 0 else tensor_size - 1 - (t ^ r)))
        text_at = jnp.sum(jnp.where(rank[None] == jnp.stack(dealt)[:, None], number[None], 0), 1).astype(jnp.int32)
        lens = jnp.sum(jnp.where(rank[None] == jnp.stack(dealt[:texts])[:, None], lengths[None], 0), 1).astype(jnp.int32)

        def exchange(blocks):
            far = {r: pp_tensor(blocks[r], r) for r in (3, 2, 1)}
            return [blocks[0]] + [far[r] for r in (1, 2, 3)]

        class Exchange:
            def __init__(self, own, near, far):
                self.own, self.near, self.far = own, near, pp_tensor(far, 2)

            def forward(self):
                self.far = clock.after(self.far)
                self.near = pp_tensor(clock.after(self.near), 1)
                self.last = pp_tensor(pick(self.far, 1 - t % 2, 0), 1)

            def blocks(self):
                return [self.own, clock.after(self.near), self.far, clock.after(self.last)]

        class Chain:
            def __init__(self, lefts, slots, near, steps, extra=None):
                self.steps = list(steps)
                self.dims = [len(slots)] + [2] * bits
                step = self.steps.pop(0)
                outer, index = self.place(step)
                if step == "y":
                    self.keep, self.sent = weight_grads(clock, lefts, slots, near, apart=True)
                elif inner % 16 == 0 and outer > len(slots):
                    split = (outer // len(slots), index)
                    self.sent, self.keep = weight_grads(clock, lefts, slots, near, split, extra=extra)
                else:
                    total = weight_grads(clock, lefts, slots, near, extra=extra)
                    self.sent, self.keep = self.halves(total, outer, index)
                self.fly(step)

            def place(self, step):
                axis = 0 if step == "y" else bits - step
                outer = 1
                for size in self.dims[:axis]:
                    outer *= size
                self.dims[axis] = 1
                return outer, 0 * t if step == "y" else bit_of[step]

            def halves(self, total, outer, index):
                view = total.reshape(outer, 2, -1, total.shape[-1])
                return pick(view, 1 - index, 1), pick(view, index, 1)

            def fly(self, step):
                self.flight = pp_tensor(self.sent, 2) if step == "y" else pp_dp(self.sent, step)

            def step(self):
                arrived = clock.after(self.flight)
                step = self.steps.pop(0)
                outer, index = self.place(step)
                if inner % 16 == 0:
                    self.sent, self.keep = add_split(clock, self.keep, arrived, outer, index)
                else:
                    total = (self.keep.astype(F32) + arrived.astype(F32)).astype(BF)
                    self.sent, self.keep = self.halves(total, outer, index)
                self.fly(step)

            def last(self):
                total = self.keep.astype(F32) + clock.after(self.flight).astype(F32)
                return total.reshape(-1, total.shape[-1])

        high = list(range(2, bits))

        always = (lengths[0] | 1) != 0

        def block(steps, *operands):
            operands = (clock.after(operands[0]),) + operands[1:]

            def run(*values):
                clock.last = None
                return steps(*values)

            saved = [(list(chain.steps), list(chain.dims)) for chain in chains]
            shapes = jax.eval_shape(lambda *v: run(*v), *operands)
            for chain, (left, dims) in zip(chains, saved):
                chain.steps, chain.dims = left, dims
            out = lax.cond(
                always, run, lambda *_: jax.tree.map(lambda v: jnp.zeros(v.shape, v.dtype), shapes), *operands
            )
            clock.last = None
            return clock.then(out)

        def from_near(lefts, slots):
            return [pp_tensor(v, 1) for v in weight_grads(clock, lefts, slots, pieces=True)]

        x_own = split_texts(clock, inputs, text_at, t, texts, False)
        x_blocks = exchange(x_own)
        wq_own = side_by_side(clock, tie(w_qkv, *x_own[1:]))
        wq_near = [pp_tensor(v, 1) for v in wq_own]
        wo_near = pp_tensor(tie(w_out, x_blocks[1]), 1)
        small = jnp.concatenate([b_qv.reshape(-1), tie(b_up, x_blocks[1])])
        small = jnp.stack([small, pp_tensor(small, 1)])
        small = list(small) + list(pp_tensor(small, 2))
        bqkv = [
            jnp.concatenate([s[:local], jnp.zeros((local,), F32), s[local : 2 * local]]) for s in small
        ]
        bup = [s[2 * local :] for s in small]


        x_blocks[0] = tie(x_blocks[0], wo_near, *wq_near)
        wq_far = [pp_tensor(tie(v, x_blocks[3]), 2) for v in wq_own]
        cut = w_up.shape[0] // 2
        up_first, up_second = jnp.concatenate([w_up[:cut], w_out], 0), w_up[cut:]
        first_far, second_far = [pp_tensor(tie(v, x_blocks[3]), 2) for v in (up_first, up_second)]
        cot = Exchange(*split_texts(clock, tie(cotangent, x_blocks[1]), text_at, t, texts, True))
        wd_far = pp_tensor(tie(w_down, x_blocks[3]), 2)
        x, h1 = join_norm(clock, x_blocks, t, ln1_gain, ln1_bias)
        wq = [wq_own, wq_near]
        qkv = [project(clock, h1, wq[r], bqkv[r]) for r in (0, 1)]
        attn_a = attend_call(clock, lens, qkv[:2], None, length)
        wq_far = [clock.after(v) for v in wq_far]

        def project_far(values):
            passed = [pp_tensor(v, 1) for v in wq_far]
            ups, downs = pp_tensor(w_up, 1), pp_tensor(w_down, 1)
            return passed, project(clock, values, wq_far, bqkv[2]), ups, downs

        passed, q_first, wu_near, wd_near = block(project_far, h1)
        wq += [wq_far, passed]
        qkv += [q_first, project(clock, h1, wq[3], bqkv[3])]
        attn_b = attend_call(clock, lens, qkv[2:], None, length, COST_FAR)
        first_far = clock.after(first_far)
        wo_far = first_far[cut:]
        wo = [w_out, wo_near, wo_far, pp_tensor(wo_far, 1)]
        ctx = [attn_a[0], attn_a[1], attn_b[0], attn_b[1]]
        resid, h2 = attention_out(clock, x, ctx, wo, (b_out, ln2_gain, ln2_bias))
        ups = [up(clock, h2, [w_up], bup[0])]
        wu_far = [first_far[:cut], clock.after(second_far)]
        wu = [[w_up], [wu_near], wu_far, [pp_tensor(v, 1) for v in wu_far]]
        ups.append(up(clock, h2, wu[1], bup[1], COST_OUT))
        cot.forward()
        ups.append(up(clock, h2, wu[3], bup[3]))
        g_low, bias_down = join_mask(clock, cot.blocks(), t, lens)

        near = from_near([g_low], [[(0, ups[1][0])], [(0, ups[2][0])]])
        ups.insert(2, up(clock, h2, wu[2], bup[2]))
        acts, slopes = [u[0] for u in ups], [u[1] for u in ups]
        down = Chain([g_low], [[(0, acts[0])], [(0, acts[2])]], near, ["y", 0, 1] + high)
        wd_far = clock.after(wd_far)
        wd = [[w_down], [wd_near], [wd_far], [pp_tensor(wd_far, 1)]]
        dups_a, sums_a, dh2 = up_back(clock, g_low, wu[:2], wd[:2], slopes[:2], None, None, None)
        dups_b, sums_b, rest = up_back(clock, g_low, wu[2:], wd[2:], slopes[2:], dh2[0], resid, ln2_gain)
        dres, dres_low, gain_two, shift_two, bias_attn = rest
        dups, bias_up = dups_a + dups_b, sums_a + sums_b
        up_near = from_near([h2], [[(0, dups[1])], [(0, dups[3])]])
        down.step()
        grads_up = Chain([h2], [[(0, dups[0])], [(0, dups[2])]], up_near, ["y", 0, 1] + high)
        back = attend_call(clock, lens, qkv[2:], [dres_low] + wo[2:] + list(attn_b[2:]), length)
        dqkv_far, qkv_sums_far = back[:2], back[2:]
        near = from_near([h1, dres_low], [[(0, dqkv_far[1]), (1, ctx[3])]])
        down.step()
        q_far = weight_grads(clock, [h1, dres_low], [[(0, dqkv_far[0]), (1, ctx[2])]], near)
        q_far = pp_tensor(q_far, 2)
        back = attend_call(clock, lens, qkv[:2], [dres_low] + wo[:2] + list(attn_a[2:]), length)
        dqkv, qkv_sums = list(back[:2]) + list(dqkv_far), list(back[2:]) + list(qkv_sums_far)
        grads_up.step()
        for bit in high:
            down.step()
        near = from_near([h1, dres_low], [[(0, dqkv[1]), (1, ctx[1])]])
        out = Exchange(*down_out(clock, resid, acts, wd, b_down, t, texts))
        grad_down = clock.then(down.last())
        grads_up.step()
        q_own = Chain([h1, dres_low], [[(0, dqkv[0]), (1, ctx[0])]], near, [0, 1] + high, clock.after(q_far))
        in_blocks, gain_one, shift_one = norm_one_back(clock, x, dres, dqkv, wq, ln1_gain, t, texts)
        gin = Exchange(*in_blocks)
        shared = [gain_one, shift_one, gain_two, shift_two, bias_attn, bias_down]
        out.forward()
        chains += [grads_up, q_own]
        for chain in chains:
            chain.flight = clock.then(clock.after(chain.flight))
        total = pack(clock, shared, bias_up, qkv_sums, t, COST_END)
        out_blocks = out.blocks()

        def moved(values, flip, tensor):
            flight = pp_tensor(values, flip) if tensor else pp_dp(values, flip)
            return clock.then(values + clock.after(flight))

        def load(state):
            for chain, (keep, flight) in zip(chains, state):
                chain.keep, chain.flight = keep, flight

        def begin(total, state):
            load(state)
            for bit in high[:1]:
                grads_up.step()
            q_own.step()
            total = moved(total, 1, True)
            for bit in (0, 1)[:bits]:
                total = moved(total, bit, False)
            return total, [(chain.keep, clock.after(chain.flight)) for chain in chains]

        def finish(total, state, blocks):
            load(state)
            for bit in high[1:]:
                grads_up.step()
            for bit in high:
                q_own.step()
                total = moved(total, bit, False)
            total = moved(total, 2, True)
            grad_up = clock.then(grads_up.last())
            rows_out = join_rows(clock, blocks, t, text_at)
            first = len(shared)
            vectors = [total[i] for i in range(first)]
            vectors.append(lax.dynamic_slice_in_dim(total, first + t, 1)[0, :units])
            qv = lax.dynamic_slice_in_dim(total, first + tensor_size + t, 1)[0, : 2 * local]
            vectors.append(qv.reshape(2, local))
            both = q_own.last()
            weights = jnp.stack([both[:, c * local : c * local + local] for c in range(3)])
            return rows_out, vectors, grad_up, weights, both[:, 3 * local :].T

        state = [(chain.keep, chain.flight) for chain in chains]
        total, state = block(begin, total, state)
        gin.forward()
        layer_out, vector, grad_up, grad_qkv, grad_out = block(finish, total, state, out_blocks)
        grad_input = join_rows(clock, gin.blocks(), t, text_at)
        return (
            layer_out,
            grad_input,
            vector[0],
            vector[1],
            grad_qkv,
            vector[7],
            grad_out,
            vector[4],
            vector[2],
            vector[3],
            grad_up,
            vector[6],
            grad_down.T,
            vector[5],
        )

    return on_device


def solution(mesh):
    return jax.shard_map(
        program(mesh.shape["dp"], mesh.shape["tensor"]),
        mesh=mesh,
        in_specs=(
            P("dp", "tensor", None),
            P("dp"),
            P("dp", "tensor", None),
            P(),
            P(),
            P(None, None, "tensor"),
            P(None, "tensor"),
            P("tensor", None),
            P(),
            P(),
            P(),
            P(None, "tensor"),
            P("tensor"),
            P("tensor", None),
            P(),
        ),
        out_specs=(
            P("dp", "tensor", None),
            P("dp", "tensor", None),
            P(),
            P(),
            P(None, "dp", "tensor"),
            P(None, "tensor"),
            P("tensor", "dp"),
            P(),
            P(),
            P(),
            P("dp", "tensor"),
            P("tensor"),
            P("tensor", "dp"),
            P(),
        ),
        check_vma=False,
    )
```
